32 devices in a mesh: drift: 8 (over y, x, core), wire: 4 (over z).
Axes of the slice: x: 2, y: 2, z: 4, core: 2. Of those that a mesh axis runs over, the one named last changes fastest.
Arguments:
- features: bfloat16 [8, 4, 576, 128], P('drift', 'wire'), may hold values from -6 to 6
- first_weight: bfloat16 [27, 128, 128], replicated, may hold values from -0.109375 to 0.109375
- second_weight: bfloat16 [27, 128, 128], replicated, may hold values from -0.109375 to 0.109375
- cotangent: bfloat16 [8, 4, 576, 128], P('drift', 'wire'), may hold values from -6 to 6
- counts: int32 [8, 4], P('drift', 'wire'), may hold values from 1 to 9, as said below
- kernel_map: int32 [8, 4, 27, 9], P('drift', 'wire'), may hold values from 0 to 25, as said below
- send_lists: int32 [8, 4, 16], P('drift', 'wire'), may hold values from 0 to 9, as said below
Outputs:
- output: bfloat16 [8, 4, 576, 128], P('drift', 'wire')
- grad_features: bfloat16 [8, 4, 576, 128], P('drift', 'wire')
- grad_first: float32 [27, 128, 128], replicated
- grad_second: float32 [27, 128, 128], replicated
The draws below stay inside these ranges and needn't reach their ends.
Inputs may be any that keep to these rules, and one draw needn't show every extreme that they name: Slots below counts[i, j] hold the region's active blocks in order of position; some region has all 9 positions active and some region exactly one. kernel_map[i, j, k, s] is the block_table row of the active block at block offset k of slot s: a slot below 9 for a block of the same region, 10 + a segment position for a block of a neighbouring region (listed there in that region's send list), and 9 where that block is inactive, outside the volume, or s is an empty slot. `send_lists`: each segment lists, in order of position, the positions of the region's face, edge or corner next to that neighbour: the slot of an active block there, else 9.
All inputs are finite; a program needn't handle non-finite values.
Results may differ from the reference program's by a relative error of at most 0.0031.
Values may be sent and summed in bfloat16 or wider, within the bound.
No kernel may reach another device: no remote copies, remote signals or barrier semaphores. Data moves between devices by JAX's collectives and lax.ppermute only.
A program may use at most 128 MiB of HBM per device.

```python
import math
import jax
import jax.numpy as jnp
import numpy as np
from jax import lax

C = 128
BX = 3
BW = 3
BZ = 1
DRIFT_PARTS = 8
WIRE_PARTS = 4
NB = 9
VOXELS = 18432


DIRECTIONS = ((-1, 0), (1, 0), (0, -1), (0, 1), (-1, -1), (-1, 1), (1, -1), (1, 1))


def segment_length_drawn(drift_step, wire_step):
    return (BX if drift_step == 0 else 1) * (BW if wire_step == 0 else 1) * BZ


def segment_start_drawn(drift_step, wire_step):
    first_row = 0
    for direction in DIRECTIONS:
        if direction == (drift_step, wire_step):
            return first_row
        first_row = first_row + segment_length_drawn(direction[0], direction[1])
    return first_row


def face_positions(drift_step, wire_step):
    if drift_step == 1:
        drift_cells = [BX - 1]
    elif drift_step == -1:
        drift_cells = [0]
    else:
        drift_cells = list(range(BX))
    if wire_step == 1:
        wire_cells = [BW - 1]
    elif wire_step == -1:
        wire_cells = [0]
    else:
        wire_cells = list(range(BW))
    listed = []
    for drift_cell in drift_cells:
        for wire_cell in wire_cells:
            for depth_cell in range(BZ):
                listed.append((drift_cell * BW + wire_cell) * BZ + depth_cell)
    return listed


def offset_tables():
    region_size = BX * BW * BZ
    near_pos = np.zeros((27, region_size), np.int32)
    shift_ids = np.zeros((27, region_size), np.int32)
    halo_ids = np.zeros((27, region_size), np.int32)
    is_local = np.zeros((27, region_size), bool)
    depth_ok = np.zeros((27, region_size), bool)
    for offset in range(27):
        step_x = offset // 9 - 1
        step_y = offset // 3 % 3 - 1
        step_z = offset % 3 - 1
        for position in range(region_size):
            drift_cell = position // (BW * BZ)
            wire_cell = position // BZ % BW
            depth_cell = position % BZ
            target_drift = drift_cell + step_x
            drift_move = -1 if target_drift < 0 else 1 if target_drift >= BX else 0
            target_drift = target_drift - drift_move * BX
            target_wire = wire_cell + step_y
            wire_move = -1 if target_wire < 0 else 1 if target_wire >= BW else 0
            target_wire = target_wire - wire_move * BW
            target_depth = depth_cell + step_z
            inside_depth = 0 <= target_depth < BZ
            depth_value = target_depth if inside_depth else 0
            near_pos[offset, position] = (target_drift * BW + target_wire) * BZ + depth_value
            shift_ids[offset, position] = (drift_move + 1) * 3 + (wire_move + 1)
            is_local[offset, position] = drift_move == 0 and wire_move == 0
            depth_ok[offset, position] = inside_depth
            if drift_move != 0 or wire_move != 0:
                column_index = target_drift if drift_move == 0 else 0
                wire_count = BW if wire_move == 0 else 1
                row_index = target_wire if wire_move == 0 else 0
                halo_ids[offset, position] = segment_start_drawn(drift_move, wire_move) + (column_index * wire_count + row_index) * BZ + depth_value
    return (near_pos, shift_ids, halo_ids, is_local, depth_ok)


def geometry(key):
    base = jax.random.fold_in(key, 31)
    key_level, key_drift, key_wire, key_roll, key_seed = jax.random.split(base, 5)
    drift_parts = DRIFT_PARTS
    wire_parts = WIRE_PARTS
    region_size = BX * BW * BZ
    levels = jax.random.randint(key_level, (drift_parts, wire_parts), 2, 10)
    full_drift = jax.random.randint(key_drift, (), 1, drift_parts)
    full_wire = jax.random.randint(key_wire, (), 1, wire_parts)
    drift_ids = jnp.arange(drift_parts, dtype=jnp.int32)[:, None]
    wire_ids = jnp.arange(wire_parts, dtype=jnp.int32)[None, :]
    is_full = (drift_ids == full_drift) & (wire_ids == full_wire)
    is_single = (drift_ids == 0) & (wire_ids == wire_parts - 1)
    is_corner = (drift_ids == full_drift - 1) & (wire_ids == full_wire - 1)
    is_anchor = (drift_ids == 0) & (wire_ids == 0)
    levels = jnp.where(is_full, 16, jnp.where(is_single, 0, levels))
    rolls = jax.random.randint(key_roll, (drift_parts, wire_parts, region_size), 0, 16)
    seeds = jax.random.randint(key_seed, (drift_parts, wire_parts), 0, region_size)
    seeds = jnp.where(is_corner | is_anchor, region_size - 1, seeds)
    positions = jnp.arange(region_size, dtype=jnp.int32)
    off_position = (BX - 1) * BW * BZ
    active = (rolls < levels[:, :, None]) | (positions[None, None, :] == seeds[:, :, None])
    active = active & jnp.logical_not(is_anchor[:, :, None] & (positions[None, None, :] == off_position))
    active_ints = active.astype(jnp.int32)
    counts = jnp.sum(active_ints, axis=2).astype(jnp.int32)
    slot_of_pos = jnp.where(active, jnp.cumsum(active_ints, axis=2) - 1, NB).astype(jnp.int32)
    near_pos, shift_ids, halo_ids, is_local, depth_ok = offset_tables()
    padded = jnp.pad(active, ((1, 1), (1, 1), (0, 0)))
    stacks = []
    for drift_move in (-1, 0, 1):
        for wire_move in (-1, 0, 1):
            stacks.append(padded[1 + drift_move:1 + drift_move + drift_parts, 1 + wire_move:1 + wire_move + wire_parts])
    near_active = jnp.stack(stacks, axis=2)
    local_slot = slot_of_pos[:, :, jnp.asarray(near_pos)]
    remote_ok = near_active[:, :, jnp.asarray(shift_ids), jnp.asarray(near_pos)]
    map_pos = jnp.where(jnp.asarray(is_local), local_slot, jnp.where(remote_ok, NB + 1 + jnp.asarray(halo_ids), NB))
    map_pos = jnp.where(jnp.asarray(depth_ok), map_pos, NB).astype(jnp.int32)
    slot_ids = jnp.arange(NB, dtype=jnp.int32)
    matches = slot_of_pos[:, :, None, :] == slot_ids[None, None, :, None]
    pos_of_slot = jnp.sum(jnp.where(matches, positions[None, None, None, :], 0), axis=3).astype(jnp.int32)
    index_rows = jnp.broadcast_to(pos_of_slot[:, :, None, :], (drift_parts, wire_parts, 27, NB))
    gathered = jnp.take_along_axis(map_pos, index_rows, axis=3)
    live_slots = slot_ids[None, None, :] < counts[:, :, None]
    kernel_map = jnp.where(live_slots[:, :, None, :], gathered, NB).astype(jnp.int32)
    send_pos = []
    for drift_step, wire_step in DIRECTIONS:
        send_pos = send_pos + face_positions(drift_step, wire_step)
    send_lists = slot_of_pos[:, :, jnp.asarray(np.array(send_pos, np.int32))].astype(jnp.int32)
    return (counts, kernel_map, send_lists)


def draw_counts(key, part):
    return geometry(key)[0]


def draw_kernel_map(key, part):
    return geometry(key)[1]


def draw_send_lists(key, part):
    return geometry(key)[2]


def steps_of(stream_key, shape, cuts, low, high):
    factor_of = 1.0
    for dim, blocks in cuts:
        draws = jax.random.uniform(jax.random.fold_in(jax.random.fold_in(stream_key, 6), dim), (blocks,), jnp.float32, low / len(cuts), high / len(cuts))
        factor_of = factor_of * jnp.repeat(jnp.exp(draws), shape[dim] // blocks).reshape((-1,) + (1,) * (len(shape) - 1 - dim))
    return factor_of


def normal_values(rng, extent, width, limit, shards=(), kind=jnp.bfloat16):
    values = jax.random.normal(rng, extent, jnp.float32) * width
    if len(shards) > 0:
        values = steps_of(rng, extent, shards, -0.22, 0.18) * values
    return jnp.clip(values, min=-limit, max=limit).astype(kind)


def setup_inputs(seed: int = 0) -> dict:
    keys = jax.random.split(jax.random.key(seed), 8)
    features = normal_values(keys[0], (DRIFT_PARTS, WIRE_PARTS, NB * 64, C), 1.0, 6.0, ((0, 8), (1, 4)))
    first_weight = normal_values(keys[1], (27, C, C), (27 * C) ** -0.5, 0.109375)
    second_weight = normal_values(keys[2], (27, C, C), (27 * C) ** -0.5, 0.109375)
    cotangent = normal_values(keys[3], (DRIFT_PARTS, WIRE_PARTS, NB * 64, C), 1.0, 6.0, ((0, 8), (1, 4)))
    counts = draw_counts(jax.random.fold_in(keys[7], 71), 0)
    kernel_map = draw_kernel_map(jax.random.fold_in(keys[7], 71), 0)
    send_lists = draw_send_lists(jax.random.fold_in(keys[7], 71), 0)
    return dict(features=features, first_weight=first_weight, second_weight=second_weight, cotangent=cotangent, counts=counts, kernel_map=kernel_map, send_lists=send_lists)


DIRECTIONS = ((-1, 0), (1, 0), (0, -1), (0, 1), (-1, -1), (-1, 1), (1, -1), (1, 1))

def segment_length(drift_step, wire_step):
    return (BX if drift_step == 0 else 1) * (BW if wire_step == 0 else 1) * BZ

def segment_start(drift_step, wire_step):
    first_row = 0
    for direction in DIRECTIONS:
        if direction == (drift_step, wire_step):
            return first_row
        first_row = first_row + segment_length(direction[0], direction[1])
    return first_row

def voxel_span(step_value):
    if step_value < 0:
        return slice(3, 4)
    if step_value == 0:
        return slice(0, 4)
    return slice(0, 1)

def neighbourhood(block_table, kernel_rows):
    planes = []
    for step_x in (-1, 0, 1):
        columns = []
        for step_y in (-1, 0, 1):
            pieces = []
            for step_z in (-1, 0, 1):
                offset = 9 * (step_x + 1) + 3 * (step_y + 1) + (step_z + 1)
                sliced = block_table[:, voxel_span(step_x), voxel_span(step_y), voxel_span(step_z), :]
                pieces.append(jnp.take(sliced, kernel_rows[offset], axis=0))
            columns.append(jnp.concatenate(pieces, axis=3))
        planes.append(jnp.concatenate(columns, axis=2))
    return jnp.concatenate(planes, axis=1)

def gather_columns(window, shift_x):
    block_count = window.shape[0]
    channels = window.shape[-1]
    pieces = []
    for shift_y in range(3):
        for shift_z in range(3):
            sliced = window[:, shift_x:shift_x + 4, shift_y:shift_y + 4, shift_z:shift_z + 4, :]
            pieces.append(sliced.reshape(block_count * 64, channels))
    return jnp.concatenate(pieces, axis=1)

def convolve(window, weight):
    channels = window.shape[-1]
    summed = jnp.zeros((window.shape[0] * 64, weight.shape[2]), jnp.float32)
    for shift_x in range(3):
        stacked = gather_columns(window, shift_x)
        matrix = weight[9 * shift_x:9 * shift_x + 9].reshape(9 * channels, weight.shape[2])
        summed = summed + jnp.dot(stacked, matrix, preferred_element_type=jnp.float32)
    return summed

def weight_terms(window, grad_rows):
    groups = []
    for shift_x in range(3):
        stacked = gather_columns(window, shift_x)
        product = jnp.dot(stacked.T, grad_rows, preferred_element_type=jnp.float32)
        groups.append(product.reshape(9, window.shape[-1], grad_rows.shape[1]))
    return jnp.concatenate(groups, axis=0)

def flipped(weight):
    return jnp.transpose(weight[::-1], (0, 2, 1))

def silu_slope(pre_value):
    sigmoid_value = jax.nn.sigmoid(pre_value)
    return sigmoid_value * (1.0 + pre_value * (1.0 - sigmoid_value))

def region_table(blocks, send_lists, drift_index, wire_index):
    pieces = [blocks[drift_index, wire_index]]
    for drift_step, wire_step in DIRECTIONS:
        near_drift = drift_index + drift_step
        near_wire = wire_index + wire_step
        inside = (near_drift >= 0) & (near_drift < DRIFT_PARTS) & (near_wire >= 0) & (near_wire < WIRE_PARTS)
        clipped_drift = jnp.clip(near_drift, 0, DRIFT_PARTS - 1)
        clipped_wire = jnp.clip(near_wire, 0, WIRE_PARTS - 1)
        first_row = segment_start(-drift_step, -wire_step)
        length = segment_length(-drift_step, -wire_step)
        entries = send_lists[clipped_drift, clipped_wire, first_row:first_row + length]
        picked = jnp.take(blocks[clipped_drift, clipped_wire], entries, axis=0)
        pieces.append(jnp.where(inside, picked, jnp.zeros_like(picked)))
    return jnp.concatenate(pieces, axis=0)

def as_blocks(source):
    shaped = source.reshape(DRIFT_PARTS, WIRE_PARTS, NB, 4, 4, 4, C)
    zero_block = jnp.zeros((DRIFT_PARTS, WIRE_PARTS, 1, 4, 4, 4, C), source.dtype)
    return jnp.concatenate([shaped, zero_block], axis=2)

def reference(features, first_weight, second_weight, cotangent, counts, kernel_map, send_lists):
    slot_ids = jnp.arange(NB * 64, dtype=jnp.int32) // 64
    live_rows = (slot_ids[None, None, :] < counts[:, :, None])[..., None]
    masked_input = jnp.where(live_rows, features, jnp.zeros_like(features))
    regions = jnp.arange(DRIFT_PARTS * WIRE_PARTS, dtype=jnp.int32)

    def windows(blocks, region):
        drift_index = region // WIRE_PARTS
        wire_index = region % WIRE_PARTS
        block_table = region_table(blocks, send_lists, drift_index, wire_index)
        return neighbourhood(block_table, kernel_map[drift_index, wire_index])

    def apply_conv(source, weight):
        blocks = as_blocks(source)
        result = lax.map(lambda region: convolve(windows(blocks, region), weight), regions)
        return result.reshape(DRIFT_PARTS, WIRE_PARTS, NB * 64, C)

    def weight_sum(source, grad_field):
        blocks = as_blocks(source)
        flat_grads = grad_field.reshape(DRIFT_PARTS * WIRE_PARTS, NB * 64, C)

        def accumulate(running, region):
            return (running + weight_terms(windows(blocks, region), flat_grads[region]), None)
        summed, unused = lax.scan(accumulate, jnp.zeros((27, C, C), jnp.float32), regions)
        return summed / math.sqrt(float(VOXELS))
    first_pre = apply_conv(masked_input, first_weight)
    hidden = jnp.where(live_rows, jax.nn.silu(first_pre), 0.0).astype(jnp.bfloat16)
    second_pre = apply_conv(hidden, second_weight)
    output = jnp.where(live_rows, masked_input.astype(jnp.float32) + second_pre, 0.0).astype(jnp.bfloat16)
    grad_in = jnp.where(live_rows, cotangent, jnp.zeros_like(cotangent))
    back_hidden = apply_conv(grad_in, flipped(second_weight))
    back_pre = jnp.where(live_rows, back_hidden * silu_slope(first_pre), 0.0).astype(jnp.bfloat16)
    back_input = apply_conv(back_pre, flipped(first_weight))
    grad_features = jnp.where(live_rows, grad_in.astype(jnp.float32) + back_input, 0.0).astype(jnp.bfloat16)
    grad_second = weight_sum(hidden, grad_in)
    grad_first = weight_sum(masked_input, back_pre)
    return (output, grad_features, grad_first, grad_second)
```

```python
import functools
import math

import jax
import jax.numpy as jnp
from jax import lax
from jax.experimental import pallas as pl
from jax.experimental.pallas import tpu as pltpu
from jax.sharding import PartitionSpec as P

BX = 3
BW = 3
NX = 4 * BX
NY = 4 * BW
J = 16
PLANE = NX * J
WIDE = (NX + 2) * J
ROWS = 4 * PLANE
FACE = 4 * NX
SLAB = 4 * J
VMEM = pl.BlockSpec(memory_space=pltpu.VMEM)
SMEM = pl.BlockSpec(memory_space=pltpu.SMEM)
LISTED = {0: 0, 1: 1, 2: 2, 3: 7, 5: 10, 6: 3, 7: 4, 8: 5}


def call(kernel, out_shape, n_smem, n_vmem, scratch=(), flops=0, bytes_accessed=0):
    return pl.pallas_call(
        kernel,
        out_shape=out_shape,
        in_specs=[SMEM] * n_smem + [VMEM] * n_vmem,
        out_specs=jax.tree.map(lambda _: VMEM, out_shape),
        scratch_shapes=list(scratch),
        compiler_params=pltpu.CompilerParams(vmem_limit_bytes=40 * 1024 * 1024),
        cost_estimate=pl.CostEstimate(flops=flops, bytes_accessed=bytes_accessed, transcendentals=0),
    )


def bf16(*shape):
    return jax.ShapeDtypeStruct(shape, jnp.bfloat16)


def f32(*shape):
    return jax.ShapeDtypeStruct(shape, jnp.float32)


def iota(shape, dim):
    return lax.broadcasted_iota(jnp.int32, shape, dim)


def position_slots(geo):
    slots = {p: geo[i] for p, i in LISTED.items()}
    present = {p: (s < 9).astype(jnp.int32) for p, s in slots.items()}
    before = present[0] + present[1] + present[2] + present[3]
    others = before + present[5] + present[6] + present[7] + present[8]
    slots[4] = jnp.where(geo[16] > others, before, 9)
    return slots


def slot_rows(slots, z, x, y, valid):
    position = (x >> 2) * BW + (y >> 2)
    slot = jnp.full(position.shape, 9, jnp.int32)
    for p, s in slots.items():
        slot = jnp.where(position == p, s, slot)
    row = slot * 64 + (x & 3) * 16 + (y & 3) * 4 + z
    return jnp.where(valid & (slot < 9), row, -1)


def one_hot(rows, width):
    lane = iota(rows.shape, 1)
    parts = [jnp.where(rows == lane + 128 * c, 1.0, 0.0).astype(jnp.bfloat16) for c in range(width // 128)]
    return jnp.concatenate(parts, axis=1)


def dot(a, b):
    return jnp.dot(a, b, preferred_element_type=jnp.float32)


def grid_indices():
    shape = (4, NX, J, 128)
    z, x, j = (iota(shape, d).reshape(ROWS, 128) for d in range(3))
    return z, x, j


def faces_kernel(geo, f, g, low, high, both):
    both[...] = jnp.zeros_like(both)
    both[0 : f.shape[0], 0:128] = f[...]
    both[0 : f.shape[0], 128:256] = g[...]
    slots = position_slots(geo)
    shape = (4, NX // 4, 4, 128)
    r = iota((FACE, 128), 0)
    z = (r >= NX).astype(jnp.int32) + (r >= 2 * NX) + (r >= 3 * NX)
    x = r - NX * z
    for y, out in ((0, low), (NY - 1, high)):
        rows = slot_rows(slots, z, x, jnp.full_like(x, y), x >= 0)
        out[...] = dot(one_hot(rows, 640), both[...]).astype(jnp.bfloat16)


def place_kernel(geo, f, g, out, live, both):
    both[...] = jnp.zeros_like(both)
    both[0 : f.shape[0], 0:128] = f[...]
    both[0 : f.shape[0], 128:256] = g[...]
    z, x, j = grid_indices()
    rows = slot_rows(position_slots(geo), z, x, j - 1, (j >= 1) & (j <= NY))
    live[...] = (rows >= 0).astype(jnp.bfloat16)
    out[...] = dot(one_hot(rows, 640), both[...]).astype(jnp.bfloat16)


def insert_kernel(placed, from_low, from_high, out, slab_low, slab_high, faces):
    faces[...] = jnp.zeros_like(faces)
    faces[0:FACE, :] = from_low[...]
    faces[FACE : 2 * FACE, :] = from_high[...]
    z, x, j = grid_indices()
    rows = z * NX + x
    rows = jnp.where(j == 0, rows, jnp.where(j == NY + 1, rows + FACE, -1))
    full = (placed[...].astype(jnp.float32) + dot(one_hot(rows, 128), faces[...])).astype(jnp.bfloat16)
    out[...] = full
    for z in range(4):
        slab_low[z * J : (z + 1) * J, :] = full[z * PLANE : z * PLANE + J, :]
        slab_high[z * J : (z + 1) * J, :] = full[(z + 1) * PLANE - J : (z + 1) * PLANE, :]


def build_window(window, base, plane_of):
    for zi in range(4):
        plane = plane_of(zi)
        wide = plane.astype(jnp.float32)
        before = pltpu.roll(wide, 1, 0).astype(jnp.bfloat16)
        after = pltpu.roll(wide, WIDE - 1, 0).astype(jnp.bfloat16)
        for oy, shifted in enumerate((before, plane, after)):
            for z in range(max(0, zi - 1), min(3, zi + 1) + 1):
                lane = 128 * (3 * oy + zi - z + 1)
                window[base + z, :, lane : lane + 128] = shifted
    empty = jnp.zeros((WIDE, 128), jnp.bfloat16)
    for oy in range(3):
        window[base, :, 384 * oy : 384 * oy + 128] = empty
        window[base + 3, :, 384 * oy + 256 : 384 * oy + 384] = empty


def wide_plane(full, low, high, z, lanes):
    return jnp.concatenate(
        [
            low[z * J : (z + 1) * J, lanes],
            full[z * PLANE : (z + 1) * PLANE, lanes],
            high[z * J : (z + 1) * J, lanes],
        ],
        axis=0,
    )


def conv(window, weight):
    total = None
    for ox in range(3):
        rows = window[:, ox * J : ox * J + PLANE, :].reshape(ROWS, 1152)
        term = dot(rows, weight[1152 * ox : 1152 * (ox + 1), :])
        total = term if total is None else total + term
    return total


def first_kernel(place, full, low, high, live, w1, w2f, hb, face_low, face_high, keep, send, window):
    core = place[0]
    f_lanes, g_lanes = slice(0, 128), slice(128, 256)
    alive = live[...].astype(jnp.float32)
    build_window(window, 0, lambda z: wide_plane(full, low, high, z, f_lanes))
    first_pre = conv(window, w1)
    gate = jax.nn.sigmoid(first_pre)
    hidden = (alive * (first_pre * gate)).astype(jnp.bfloat16)
    slope = alive * (gate * (1.0 + first_pre * (1.0 - gate)))
    build_window(window, 0, lambda z: wide_plane(full, low, high, z, g_lanes))
    back = (conv(window, w2f) * slope).astype(jnp.bfloat16)
    both = jnp.concatenate([hidden, back], axis=1)
    hb[...] = both
    r = iota((FACE, 128), 0)
    z = (r >= NX).astype(jnp.int32) + (r >= 2 * NX) + (r >= 3 * NX)
    rows = z * PLANE + (r - NX * z) * J
    face_low[...] = dot(one_hot(rows + 1, ROWS), both).astype(jnp.bfloat16)
    face_high[...] = dot(one_hot(rows + NY, ROWS), both).astype(jnp.bfloat16)

    def write(to, values, lanes):
        to[0:ROWS, :] = values
        for z in range(4):
            start = ROWS + z * WIDE
            to[start : start + WIDE, :] = wide_plane(full, low, high, z, lanes)

    @pl.when(core == 0)
    def _():
        write(keep, hidden, g_lanes)
        write(send, back, f_lanes)

    @pl.when(core != 0)
    def _():
        write(keep, back, f_lanes)
        write(send, hidden, g_lanes)


def terms_kernel(chunk, place, mine, theirs, *refs):
    *sends, own, window, total = refs
    for base, part in ((0, mine), (4, theirs)):
        build_window(
            window, base, lambda z: part[ROWS + z * WIDE : ROWS + (z + 1) * WIDE, :]
        )
    left = jnp.concatenate([mine[0:ROWS, :], theirs[0:ROWS, :]], axis=0)
    left = left.astype(jnp.float32).T.astype(jnp.bfloat16)
    if total.shape[0] > 3456:
        total[3456:, :] = jnp.zeros((total.shape[0] - 3456, 128), jnp.float32)
    for ox in range(3):
        rows = window[:, ox * J : ox * J + PLANE, :].reshape(2 * ROWS, 1152)
        product = dot(left, rows)
        for k in range(9):
            start = 128 * (9 * ox + k)
            total[start : start + 128, :] = product[:, 128 * k : 128 * (k + 1)]
    me = place[1]
    own[...] = total[pl.ds(pl.multiple_of(me * chunk, 8), chunk), :]
    for step, out in enumerate(sends):
        start = pl.multiple_of((me ^ (step + 1)) * chunk, 8)
        out[...] = total[pl.ds(start, chunk), :].astype(jnp.bfloat16)


def split_kernel(unit, count, place, own, *refs):
    received, (*sends, rest, total) = refs[:count], refs[count:]
    summed = own[...]
    for part in received:
        summed = summed + part[...].astype(jnp.float32)
    total[...] = summed
    me = place[2]
    rest[...] = total[pl.ds(pl.multiple_of(me * unit, 8), unit), :]
    for step, out in enumerate(sends):
        start = pl.multiple_of((me ^ (step + 1)) * unit, 8)
        out[...] = total[pl.ds(start, unit), :].astype(jnp.bfloat16)


def joined_kernel(unit, place, *refs):
    *parts, out, total = refs
    me = place[2]
    for step, part in enumerate(parts):
        start = pl.multiple_of((me ^ step) * unit, 8)
        total[pl.ds(start, unit), :] = part[...].astype(jnp.float32)
    out[...] = total[...].astype(jnp.bfloat16)


def final_kernel(chunk, count, place, *refs):
    mine, theirs = refs[:count], refs[count : 2 * count]
    first, second, total = refs[2 * count :]
    core, me = place[0], place[1]
    for step in range(count):
        start = pl.multiple_of((me ^ step) * chunk, 8)
        total[core, pl.ds(start, chunk), :] = mine[step][...].astype(jnp.float32)
        total[1 - core, pl.ds(start, chunk), :] = theirs[step][...].astype(jnp.float32)
    for k in range(27):
        second[26 - k] = total[0, 128 * k : 128 * (k + 1), :]
        first[k] = total[1, 128 * k : 128 * (k + 1), :].T


def second_kernel(geo, hb, low, high, base, live, w2, w1f, output, grad, window):
    alive = live[...].astype(jnp.float32)
    results = []
    for lanes, weight in ((slice(0, 128), w2), (slice(128, 256), w1f)):
        build_window(window, 0, lambda z: wide_plane(hb, low, high, z, lanes))
        value = conv(window, weight)
        results.append((alive * (base[:, lanes].astype(jnp.float32) + value)).astype(jnp.bfloat16))
    both = jnp.concatenate(results, axis=1)
    slots = position_slots(geo)
    pieces = []
    row = iota((576, 128), 0)
    for c in range(ROWS // 128):
        col = iota((8, 128), 1) + 128 * c
        z = (col >= PLANE).astype(jnp.int32) + (col >= 2 * PLANE) + (col >= 3 * PLANE)
        rest = col - PLANE * z
        x, j = rest >> 4, rest & 15
        source = slot_rows(slots, z, x, j - 1, (j >= 1) & (j <= NY))
        source = jnp.broadcast_to(source[0:1, :], (576, 128))
        pieces.append(jnp.where(row == source, 1.0, 0.0).astype(jnp.bfloat16))
    by_slot = dot(jnp.concatenate(pieces, axis=1), both).astype(jnp.bfloat16)
    output[...] = by_slot[:, 0:128]
    grad[...] = by_slot[:, 128:256]


def shift(value, axis, steps):
    count = lax.axis_size(axis)
    return lax.ppermute(value, axis, [(i, i + steps) for i in range(count) if 0 <= i + steps < count])


def on_device(features, first_weight, second_weight, cotangent, counts, kernel_map, send_lists):
    drift, wire = lax.axis_size("drift"), lax.axis_size("wire")
    chips = drift // 2
    rows = 27 * 128
    unit = -(-rows // (chips * wire * 8)) * 8
    chunk = unit * wire
    f, g = features[0, 0], cotangent[0, 0]
    slots = f.shape[0]
    geo = jnp.concatenate([send_lists.reshape(16), counts.reshape(1)])
    d, w = lax.axis_index("drift"), lax.axis_index("wire")
    place = jnp.stack([d % 2, d // 2, w]).astype(jnp.int32)
    w1, w2 = first_weight.reshape(rows, 128), second_weight.reshape(rows, 128)
    w1f = jnp.transpose(first_weight[::-1], (0, 2, 1)).reshape(rows, 128)
    w2f = jnp.transpose(second_weight[::-1], (0, 2, 1)).reshape(rows, 128)
    both = pltpu.VMEM((640, 256), jnp.bfloat16)
    window = pltpu.VMEM((4, WIDE, 1152), jnp.bfloat16)

    def halo(placed, face_low, face_high):
        from_high = shift(face_low, "wire", -1)
        from_low = shift(face_high, "wire", 1)
        full, slab_low, slab_high = call(
            insert_kernel,
            (bf16(ROWS, 256), bf16(SLAB, 256), bf16(SLAB, 256)),
            0,
            3,
            [pltpu.VMEM((128, 256), jnp.bfloat16)],
        )(placed, from_low, from_high)
        high = shift(slab_low, "drift", -1)
        low = shift(slab_high, "drift", 1)
        return full, low, high

    face_low, face_high = call(faces_kernel, (bf16(FACE, 256), bf16(FACE, 256)), 1, 2, [both])(geo, f, g)
    placed, live = call(place_kernel, (bf16(ROWS, 256), bf16(ROWS, 128)), 1, 2, [both])(geo, f, g)
    full, low, high = halo(placed, face_low, face_high)
    message = bf16(ROWS + 4 * WIDE, 128)
    hb, hb_low, hb_high, keep, send = call(
        first_kernel,
        (bf16(ROWS, 256), bf16(FACE, 256), bf16(FACE, 256), message, message),
        1,
        6,
        [window],
    )(place, full, low, high, live, w1, w2f)

    def swap_core(value):
        return lax.ppermute(value, "drift", [(i, i ^ 1) for i in range(drift)])

    def to_chip(value, step):
        return lax.ppermute(value, "drift", [(i, i ^ (2 * step)) for i in range(drift)])

    def to_wire(value, step):
        return lax.ppermute(value, "wire", [(i, i ^ step) for i in range(wire)])

    got = swap_core(send)
    *sends, own = call(
        functools.partial(terms_kernel, chunk),
        tuple([bf16(chunk, 128)] * (chips - 1) + [f32(chunk, 128)]),
        1,
        2,
        [pltpu.VMEM((8, WIDE, 1152), jnp.bfloat16), pltpu.VMEM((chunk * chips, 128), jnp.float32)],
    )(place, keep, got)
    parts = [to_chip(s, k + 1) for k, s in enumerate(sends)]
    *sends, own = call(
        functools.partial(split_kernel, unit, chips - 1),
        tuple([bf16(unit, 128)] * (wire - 1) + [f32(unit, 128)]),
        1,
        chips,
        [pltpu.VMEM((chunk, 128), jnp.float32)],
    )(place, own, *parts)
    summed = own
    for k, s in enumerate(sends):
        summed = summed + to_wire(s, k + 1).astype(jnp.float32)
    summed = (summed / math.sqrt(float(drift * wire * slots))).astype(jnp.bfloat16)
    pieces = [summed] + [to_wire(summed, k) for k in range(1, wire)]
    mine = call(
        functools.partial(joined_kernel, unit), bf16(chunk, 128), 1, wire, [pltpu.VMEM((chunk, 128), jnp.float32)]
    )(place, *pieces)
    mine = [mine] + [to_chip(mine, k) for k in range(1, chips)]
    theirs = [swap_core(m) for m in mine]
    grad_first, grad_second = call(
        functools.partial(final_kernel, chunk, chips),
        (f32(27, 128, 128), f32(27, 128, 128)),
        1,
        2 * chips,
        [pltpu.VMEM((2, chunk * chips, 128), jnp.float32)],
    )(place, *mine, *theirs)

    hb_full, hb_low, hb_high = halo(hb, hb_low, hb_high)
    output, grad_features = call(
        second_kernel, (bf16(slots, 128), bf16(slots, 128)), 1, 7, [window]
    )(geo, hb_full, hb_low, hb_high, full, live, w2, w1f)
    return output[None, None], grad_features[None, None], grad_first, grad_second


def solution(mesh):
    placed = (
        P("drift", "wire", None, None),
        P(),
        P(),
        P("drift", "wire", None, None),
        P("drift", "wire"),
        P("drift", "wire", None, None),
        P("drift", "wire", None),
    )
    return jax.shard_map(
        on_device,
        mesh=mesh,
        in_specs=placed,
        out_specs=(P("drift", "wire", None, None), P("drift", "wire", None, None), P(), P()),
        check_vma=False,
    )
```

```python
import functools
import math

import jax
import jax.numpy as jnp
from jax import lax
from jax.experimental import pallas as pl
from jax.experimental.pallas import tpu as pltpu
from jax.sharding import PartitionSpec as P

BX = 3
BW = 3
NX = 4 * BX
NY = 4 * BW
J = 16
PLANE = NX * J
WIDE = (NX + 2) * J
ROWS = 4 * PLANE
FACE = 4 * NX
SLAB = 4 * J
CHANNELS = 128
TAPS = 27
VMEM = pl.BlockSpec(memory_space=pltpu.VMEM)
HBM = pl.BlockSpec(memory_space=pltpu.HBM)
SMEM = pl.BlockSpec(memory_space=pltpu.SMEM)
LISTED = {0: 0, 1: 1, 2: 2, 3: 7, 5: 10, 6: 3, 7: 4, 8: 5}


def call(kernel, out_shape, in_specs, scratch=(), microseconds=0, out_spec=VMEM, aliases={}, vmem=40):
    return pl.pallas_call(
        kernel,
        out_shape=out_shape,
        in_specs=in_specs,
        out_specs=jax.tree.map(lambda _: out_spec, out_shape),
        scratch_shapes=list(scratch),
        input_output_aliases=aliases,
        compiler_params=pltpu.CompilerParams(vmem_limit_bytes=vmem * 1024 * 1024),
        cost_estimate=pl.CostEstimate(
            flops=0, bytes_accessed=int(microseconds * 3.0e6), transcendentals=0
        ),
    )


def bf16(*shape):
    return jax.ShapeDtypeStruct(shape, jnp.bfloat16)


def f32(*shape):
    return jax.ShapeDtypeStruct(shape, jnp.float32)


def iota(shape, dim):
    return lax.broadcasted_iota(jnp.int32, shape, dim)


def position_slots(lists, counts):
    slots = {p: lists[0, 0, i] for p, i in LISTED.items()}
    present = {p: (s < 9).astype(jnp.int32) for p, s in slots.items()}
    before = present[0] + present[1] + present[2] + present[3]
    others = before + present[5] + present[6] + present[7] + present[8]
    slots[4] = jnp.where(counts[0, 0] > others, before, 9)
    return slots


def slot_rows(slots, z, x, y, valid):
    position = (x >> 2) * BW + (y >> 2)
    slot = jnp.full(position.shape, 9, jnp.int32)
    for p, s in slots.items():
        slot = jnp.where(position == p, s, slot)
    row = slot * 64 + (x & 3) * 16 + (y & 3) * 4 + z
    return jnp.where(valid & (slot < 9), row, -1)


def one_hot(rows, width):
    lane = iota(rows.shape, 1)
    parts = [jnp.where(rows == lane + 128 * c, 1.0, 0.0).astype(jnp.bfloat16) for c in range(width // 128)]
    return jnp.concatenate(parts, axis=1)


def dot(a, b):
    return jnp.dot(a, b, preferred_element_type=jnp.float32)


def grid_indices():
    shape = (4, NX, J, 128)
    z, x, j = (iota(shape, d).reshape(ROWS, 128) for d in range(3))
    return z, x, j


def load_pair(lists, f, g, held_lists, both, sems):
    count = f.shape[0]
    copies = [
        pltpu.make_async_copy(lists, held_lists, sems.at[2]),
        pltpu.make_async_copy(f, both.at[pl.ds(0, count), pl.ds(0, 128)], sems.at[0]),
        pltpu.make_async_copy(g, both.at[pl.ds(0, count), pl.ds(128, 128)], sems.at[1]),
    ]
    for copy in copies:
        copy.start()
    both[count:, :] = jnp.zeros((both.shape[0] - count, 256), jnp.bfloat16)
    copies[0].wait()
    return copies[1:]


def face_indices():
    r = iota((FACE, 128), 0)
    z = (r >= NX).astype(jnp.int32) + (r >= 2 * NX) + (r >= 3 * NX)
    return z, r - NX * z


def write_by_parity(axis, low, high, first, second):
    even = lax.axis_index(axis) % 2 == 0
    first[...] = jnp.where(even, high, low)
    second[...] = jnp.where(even, low, high)


def read_by_parity(axis, first, second):
    me, count = lax.axis_index(axis), lax.axis_size(axis)
    even = me % 2 == 0
    a, b = first[...], second[...]
    nothing = jnp.zeros_like(a)
    low = jnp.where(me > 0, jnp.where(even, b, a), nothing)
    high = jnp.where(me < count - 1, jnp.where(even, a, b), nothing)
    return low, high


def faces_kernel(counts, lists, f, g, first, second, held_lists, both, sems):
    copies = load_pair(lists, f, g, held_lists, both, sems)
    slots = position_slots(held_lists, counts)
    z, x = face_indices()
    picks = [
        one_hot(slot_rows(slots, z, x, jnp.full_like(x, y), x >= 0), both.shape[0]) for y in (0, NY - 1)
    ]
    for copy in copies:
        copy.wait()
    low, high = (dot(pick, both[...]).astype(jnp.bfloat16) for pick in picks)
    write_by_parity("wire", low, high, first, second)


def place_kernel(counts, lists, f, g, out, live, held_lists, both, sems):
    copies = load_pair(lists, f, g, held_lists, both, sems)
    z, x, j = grid_indices()
    rows = slot_rows(position_slots(held_lists, counts), z, x, j - 1, (j >= 1) & (j <= NY))
    live[...] = (rows >= 0).astype(jnp.bfloat16)
    pick = one_hot(rows, both.shape[0])
    for copy in copies:
        copy.wait()
    out[...] = dot(pick, both[...]).astype(jnp.bfloat16)


def insert_faces(placed, got_first, got_second, out, slab_first, slab_second, faces):
    low, high = read_by_parity("wire", got_first, got_second)
    faces[0:FACE, :] = low
    faces[FACE : 2 * FACE, :] = high
    faces[2 * FACE :, :] = jnp.zeros((faces.shape[0] - 2 * FACE, 256), jnp.bfloat16)
    z, x, j = grid_indices()
    rows = z * NX + x
    rows = jnp.where(j == 0, rows, jnp.where(j == NY + 1, rows + FACE, -1))
    full = (placed[...].astype(jnp.float32) + dot(one_hot(rows, 128), faces[...])).astype(jnp.bfloat16)
    out[...] = full
    low = jnp.concatenate([full[z * PLANE : z * PLANE + J, :] for z in range(4)], axis=0)
    high = jnp.concatenate([full[(z + 1) * PLANE - J : (z + 1) * PLANE, :] for z in range(4)], axis=0)
    write_by_parity("drift", low, high, slab_first, slab_second)


def build_window(window, base, plane_of):
    for zi in range(4):
        plane = plane_of(zi)
        wide = plane.astype(jnp.float32)
        before = pltpu.roll(wide, 1, 0).astype(jnp.bfloat16)
        after = pltpu.roll(wide, WIDE - 1, 0).astype(jnp.bfloat16)
        for oy, shifted in enumerate((before, plane, after)):
            for z in range(max(0, zi - 1), min(3, zi + 1) + 1):
                lane = 128 * (3 * oy + zi - z + 1)
                window[base + z, :, lane : lane + 128] = shifted
    empty = jnp.zeros((WIDE, 128), jnp.bfloat16)
    for oy in range(3):
        window[base, :, 384 * oy : 384 * oy + 128] = empty
        window[base + 3, :, 384 * oy + 256 : 384 * oy + 384] = empty


def wide_plane(full, low, high, z, lanes):
    return jnp.concatenate(
        [
            low[z * J : (z + 1) * J, lanes],
            full[z * PLANE : (z + 1) * PLANE, lanes],
            high[z * J : (z + 1) * J, lanes],
        ],
        axis=0,
    )


def conv(window, weight):
    total = None
    for ox in range(3):
        rows = window[:, ox * J : ox * J + PLANE, :].reshape(ROWS, 1152)
        term = dot(rows, weight[9 * ox : 9 * (ox + 1)].reshape(1152, 128))
        total = term if total is None else total + term
    return total


def flip_blocks(weight, flipped):
    for k in range(TAPS):
        flipped[:, 128 * k : 128 * (k + 1)] = weight[TAPS - 1 - k]


def conv_flipped(window, flipped):
    total = None
    for ox in range(3):
        rows = window[:, ox * J : ox * J + PLANE, :].reshape(ROWS, 1152)
        term = lax.dot_general(
            rows,
            flipped[:, 1152 * ox : 1152 * (ox + 1)],
            (((1,), (1,)), ((), ())),
            preferred_element_type=jnp.float32,
        )
        total = term if total is None else total + term
    return total


def first_kernel(full, got_first, got_second, live, w1, w2, hb, keep, send, window, flipped):
    f_lanes, g_lanes = slice(0, 128), slice(128, 256)
    low, high = read_by_parity("drift", got_first, got_second)
    alive = live[...].astype(jnp.float32)
    flip_blocks(w2, flipped)
    build_window(window, 0, lambda z: wide_plane(full, low, high, z, f_lanes))
    first_pre = conv(window, w1)
    gate = jax.nn.sigmoid(first_pre)
    hidden = (alive * (first_pre * gate)).astype(jnp.bfloat16)
    slope = alive * (gate * (1.0 + first_pre * (1.0 - gate)))
    build_window(window, 0, lambda z: wide_plane(full, low, high, z, g_lanes))
    back = (conv_flipped(window, flipped) * slope).astype(jnp.bfloat16)
    hb[...] = jnp.concatenate([hidden, back], axis=1)
    core = lax.axis_index("drift") % 2

    def write(to, values, lanes):
        to[0:ROWS, :] = values
        for z in range(4):
            start = ROWS + z * WIDE
            to[start : start + WIDE, :] = wide_plane(full, low, high, z, lanes)

    @pl.when(core == 0)
    def _():
        write(keep, hidden, g_lanes)
        write(send, back, f_lanes)

    @pl.when(core != 0)
    def _():
        write(keep, back, f_lanes)
        write(send, hidden, g_lanes)


def terms_kernel(chunk, mine, theirs, hb, *refs):
    *sends, own, first, second, window, total = refs
    for base, part in ((0, mine), (4, theirs)):
        build_window(window, base, lambda z: part[ROWS + z * WIDE : ROWS + (z + 1) * WIDE, :])
    left = jnp.concatenate([mine[0:ROWS, :], theirs[0:ROWS, :]], axis=0)
    left = left.astype(jnp.float32).T.astype(jnp.bfloat16)
    rows = TAPS * CHANNELS
    if total.shape[0] > rows:
        total[rows:, :] = jnp.zeros((total.shape[0] - rows, 128), jnp.float32)
    for ox in range(3):
        shifted = window[:, ox * J : ox * J + PLANE, :].reshape(2 * ROWS, 1152)
        product = dot(left, shifted)
        for k in range(9):
            start = 128 * (9 * ox + k)
            total[start : start + 128, :] = product[:, 128 * k : 128 * (k + 1)]
    me = lax.axis_index("drift") // 2
    own[...] = total[pl.ds(pl.multiple_of(me * chunk, 16), chunk), :]
    for step, out in enumerate(sends):
        start = pl.multiple_of((me ^ (step + 1)) * chunk, 16)
        out[...] = total[pl.ds(start, chunk), :].astype(jnp.bfloat16)
    z, x = face_indices()
    start = z * PLANE + x * J
    low, high = (dot(one_hot(start + j, ROWS), hb[...]).astype(jnp.bfloat16) for j in (1, NY))
    write_by_parity("wire", low, high, first, second)


def split_kernel(unit, count, after_first, after_second, own, *refs):
    received, (*sends, rest, total) = refs[:count], refs[count:]
    summed = own[...]
    for part in received:
        summed = summed + part[...].astype(jnp.float32)
    total[...] = summed
    me = lax.axis_index("wire")
    rest[...] = total[pl.ds(pl.multiple_of(me * unit, 16), unit), :]
    for step, out in enumerate(sends):
        start = pl.multiple_of((me ^ (step + 1)) * unit, 16)
        out[...] = total[pl.ds(start, unit), :].astype(jnp.bfloat16)


def sum_kernel(scale, after, own, *refs):
    *received, out = refs
    summed = own[...]
    for part in received:
        summed = summed + part[...].astype(jnp.float32)
    out[...] = (summed * scale).astype(jnp.bfloat16)


def joined_kernel(unit, after, *refs):
    *parts, out = refs
    me = lax.axis_index("wire")
    for step, part in enumerate(parts):
        start = pl.multiple_of((me ^ step) * unit, 16)
        out[pl.ds(start, unit), :] = part[...]


def final_kernel(step, *refs):
    mine, theirs = refs[:2]
    first, second, staged, sems = refs[-4:]
    me = lax.axis_index("drift") // 2
    even = lax.axis_index("drift") % 2 == 0
    blocks = staged.shape[1]

    def copies(i):
        tap = (me ^ step) * blocks + i
        safe = jnp.minimum(tap, TAPS - 1)
        return tap < TAPS, (
            pltpu.make_async_copy(staged.at[0, i], second.at[TAPS - 1 - safe], sems.at[0, i]),
            pltpu.make_async_copy(staged.at[1, i], first.at[safe], sems.at[1, i]),
        )

    a, b = mine[...], theirs[...]
    for_second = jnp.where(even, a, b).astype(jnp.float32)
    for_first = jnp.where(even, b, a).astype(jnp.float32)
    for i in range(blocks):
        staged[0, i] = for_second[128 * i : 128 * (i + 1), :]
        staged[1, i] = for_first[128 * i : 128 * (i + 1), :].T
        used, pair = copies(i)

        @pl.when(used)
        def _():
            for copy in pair:
                copy.start()

    for i in range(blocks):
        used, pair = copies(i)

        @pl.when(used)
        def _():
            for copy in pair:
                copy.wait()


def second_kernel(field, flip, lists, counts, hb, got_first, got_second, base, live, weight, output, done, window, *flipped):
    low, high = read_by_parity("drift", got_first, got_second)
    lanes = slice(128 * field, 128 * (field + 1))
    build_window(window, 0, lambda z: wide_plane(hb, low, high, z, lanes))
    if flip:
        flip_blocks(weight, *flipped)
        value = conv_flipped(window, *flipped)
    else:
        value = conv(window, weight)
    result = (live[...].astype(jnp.float32) * (base[:, lanes].astype(jnp.float32) + value)).astype(jnp.bfloat16)
    slots = position_slots(lists, counts)
    count = output.shape[0]
    pieces = []
    row = iota((count, 128), 0)
    for c in range(ROWS // 128):
        col = iota((8, 128), 1) + 128 * c
        z = (col >= PLANE).astype(jnp.int32) + (col >= 2 * PLANE) + (col >= 3 * PLANE)
        rest = col - PLANE * z
        x, j = rest >> 4, rest & 15
        source = slot_rows(slots, z, x, j - 1, (j >= 1) & (j <= NY))
        source = jnp.broadcast_to(source[0:1, :], (count, 128))
        pieces.append(jnp.where(row == source, 1.0, 0.0).astype(jnp.bfloat16))
    output[...] = dot(jnp.concatenate(pieces, axis=1), result).astype(jnp.bfloat16)
    done[...] = jnp.zeros_like(done)


def pairs(value_first, value_second, axis, wrap):
    count = lax.axis_size(axis)
    first = [(i, i ^ 1) for i in range(count) if i ^ 1 < count]
    second = [(i, i + 1) for i in range(1, count - 1, 2)] + [(i + 1, i) for i in range(1, count - 1, 2)]
    if wrap and count % 2 == 0:
        second = second + [(0, count - 1), (count - 1, 0)]
    got_second = lax.ppermute(value_second, axis, second)
    got_first = lax.ppermute(value_first, axis, first)
    return got_first, got_second


def on_device(features, first_weight, second_weight, cotangent, counts, kernel_map, send_lists):
    drift, wire = lax.axis_size("drift"), lax.axis_size("wire")
    chips = drift // 2
    blocks = -(-TAPS // chips)
    chunk = blocks * CHANNELS
    unit = chunk // wire
    rows = TAPS * CHANNELS
    f, g = features[0, 0], cotangent[0, 0]
    slots = f.shape[0]
    padded = -(-slots // 128) * 128
    pair_scratch = [
        pltpu.SMEM((1, 1, 16), jnp.int32),
        pltpu.VMEM((padded, 256), jnp.bfloat16),
        pltpu.SemaphoreType.DMA((3,)),
    ]
    conv_scratch = [pltpu.VMEM((4, WIDE, 1152), jnp.bfloat16), pltpu.VMEM((128, rows), jnp.bfloat16)]
    faces_scratch = pltpu.VMEM((128, 256), jnp.bfloat16)
    face, slab, grid = bf16(FACE, 256), bf16(SLAB, 256), bf16(ROWS, 256)

    def swap_core(value):
        return lax.ppermute(value, "drift", [(i, i ^ 1) for i in range(drift)])

    def to_chip(value, step):
        return lax.ppermute(value, "drift", [(i, i ^ (2 * step)) for i in range(drift)])

    def to_wire(value, step):
        return lax.ppermute(value, "wire", [(i, i ^ step) for i in range(wire)])

    faces = call(faces_kernel, (face, face), [SMEM] + [HBM] * 3, pair_scratch, 20, vmem=60)(
        counts, send_lists, f, g
    )
    placed, live = call(place_kernel, (grid, bf16(ROWS, 128)), [SMEM] + [HBM] * 3, pair_scratch, 20)(
        counts, send_lists, f, g
    )
    faces = pairs(*faces, "wire", False)
    full, *slabs = call(insert_faces, (grid, slab, slab), [VMEM] * 3, [faces_scratch], 20)(placed, *faces)
    slabs = pairs(*slabs, "drift", True)
    message = bf16(ROWS + 4 * WIDE, 128)
    hb, keep, send = call(first_kernel, (grid, message, message), [VMEM] * 6, conv_scratch)(
        full, *slabs, live, first_weight, second_weight
    )
    got = swap_core(send)
    *sends, own, face_first, face_second = call(
        functools.partial(terms_kernel, chunk),
        tuple([bf16(chunk, 128)] * (chips - 1) + [f32(chunk, 128), face, face]),
        [VMEM] * 3,
        [pltpu.VMEM((8, WIDE, 1152), jnp.bfloat16), pltpu.VMEM((chunk * chips, 128), jnp.float32)],
    )(keep, got, hb)
    parts = [to_chip(s, k + 1) for k, s in enumerate(sends)]
    faces = pairs(face_first, face_second, "wire", False)
    hb_full, *hb_slabs = call(insert_faces, (grid, slab, slab), [VMEM] * 3, [faces_scratch])(hb, *faces)
    hb_slabs = pairs(*hb_slabs, "drift", True)
    *sends, own = call(
        functools.partial(split_kernel, unit, chips - 1),
        tuple([bf16(unit, 128)] * (wire - 1) + [f32(unit, 128)]),
        [HBM] * 2 + [VMEM] * chips,
        [pltpu.VMEM((chunk, 128), jnp.float32)],
    )(*hb_slabs, own, *parts)

    def second(field, weight, flip):
        return call(
            functools.partial(second_kernel, field, flip),
            (bf16(slots, 128), f32(8, 128)),
            [SMEM] * 2 + [VMEM] * 6,
            conv_scratch if flip else conv_scratch[:1],
            3,
        )(send_lists, counts, hb_full, *hb_slabs, full, live, weight)

    grad_features, done = second(1, first_weight, True)
    received = [to_wire(s, k + 1) for k, s in enumerate(sends)]
    scale = 1.0 / math.sqrt(float(drift * wire * slots))
    summed = call(functools.partial(sum_kernel, scale), bf16(unit, 128), [VMEM] * (1 + wire))(
        done, own, *received
    )
    pieces = [summed] + [to_wire(summed, k) for k in range(1, wire)]
    output, done = second(0, second_weight, False)
    mine = call(functools.partial(joined_kernel, unit), bf16(chunk, 128), [VMEM] * (1 + wire))(done, *pieces)
    mine = [mine] + [to_chip(mine, k) for k in range(1, chips)]
    grads = ()
    for step in range(chips):
        grads = call(
            functools.partial(final_kernel, step),
            (f32(TAPS, 128, 128), f32(TAPS, 128, 128)),
            [VMEM] * 2 + [HBM] * len(grads),
            [pltpu.VMEM((2, blocks, 128, 128), jnp.float32), pltpu.SemaphoreType.DMA((2, blocks))],
            10,
            HBM,
            {2: 0, 3: 1} if grads else {},
        )(mine[step], swap_core(mine[step]), *grads)
    grad_first, grad_second = grads
    return output[None, None], grad_features[None, None], grad_first, grad_second


def solution(mesh):
    placed = (
        P("drift", "wire", None, None),
        P(),
        P(),
        P("drift", "wire", None, None),
        P("drift", "wire"),
        P("drift", "wire", None, None),
        P("drift", "wire", None),
    )
    return jax.shard_map(
        on_device,
        mesh=mesh,
        in_specs=placed,
        out_specs=(P("drift", "wire", None, None), P("drift", "wire", None, None), P(), P()),
        check_vma=False,
    )
```

```python
import functools
import math

import jax
import jax.numpy as jnp
from jax import lax
from jax.experimental import pallas as pl
from jax.experimental.pallas import tpu as pltpu
from jax.sharding import PartitionSpec as P

BX = 3
BW = 3
NX = 4 * BX
NY = 4 * BW
J = 16
PLANE = NX * J
WIDE = (NX + 2) * J
ROWS = 4 * PLANE
FACE = 4 * NX
SLAB = 4 * J
CHANNELS = 128
TAPS = 27
VMEM = pl.BlockSpec(memory_space=pltpu.VMEM)
HBM = pl.BlockSpec(memory_space=pltpu.HBM)
SMEM = pl.BlockSpec(memory_space=pltpu.SMEM)
LISTED = {0: 0, 1: 1, 2: 2, 3: 7, 5: 10, 6: 3, 7: 4, 8: 5}


def call(kernel, out_shape, in_specs, scratch=(), flops=0, out_spec=VMEM, aliases={}, vmem=40):
    return pl.pallas_call(
        kernel,
        out_shape=out_shape,
        in_specs=in_specs,
        out_specs=jax.tree.map(lambda _: out_spec, out_shape),
        scratch_shapes=list(scratch),
        input_output_aliases=aliases,
        compiler_params=pltpu.CompilerParams(vmem_limit_bytes=vmem * 1024 * 1024),
        cost_estimate=pl.CostEstimate(
            flops=flops, bytes_accessed=0, transcendentals=0
        ),
    )


def bf16(*shape):
    return jax.ShapeDtypeStruct(shape, jnp.bfloat16)


def f32(*shape):
    return jax.ShapeDtypeStruct(shape, jnp.float32)


def iota(shape, dim):
    return lax.broadcasted_iota(jnp.int32, shape, dim)


def position_slots(lists, counts):
    slots = {p: lists[0, 0, i] for p, i in LISTED.items()}
    present = {p: (s < 9).astype(jnp.int32) for p, s in slots.items()}
    before = present[0] + present[1] + present[2] + present[3]
    others = before + present[5] + present[6] + present[7] + present[8]
    slots[4] = jnp.where(counts[0, 0] > others, before, 9)
    return slots


def slot_rows(slots, z, x, y, valid):
    position = (x >> 2) * BW + (y >> 2)
    slot = jnp.full(position.shape, 9, jnp.int32)
    for p, s in slots.items():
        slot = jnp.where(position == p, s, slot)
    row = slot * 64 + (x & 3) * 16 + (y & 3) * 4 + z
    return jnp.where(valid & (slot < 9), row, -1)


def one_hot(rows, width):
    lane = iota(rows.shape, 1)
    parts = [jnp.where(rows == lane + 128 * c, 1.0, 0.0).astype(jnp.bfloat16) for c in range(width // 128)]
    return jnp.concatenate(parts, axis=1)


def dot(a, b):
    return jnp.dot(a, b, preferred_element_type=jnp.float32)


def grid_indices():
    shape = (4, NX, J, 128)
    z, x, j = (iota(shape, d).reshape(ROWS, 128) for d in range(3))
    return z, x, j


def face_indices():
    r = iota((FACE, 128), 0)
    z = (r >= NX).astype(jnp.int32) + (r >= 2 * NX) + (r >= 3 * NX)
    return z, r - NX * z


def write_by_parity(axis, low, high, first, second):
    even = lax.axis_index(axis) % 2 == 0
    first[...] = jnp.where(even, high, low)
    second[...] = jnp.where(even, low, high)


def read_by_parity(axis, first, second):
    me, count = lax.axis_index(axis), lax.axis_size(axis)
    even = me % 2 == 0
    a, b = first[...], second[...]
    nothing = jnp.zeros_like(a)
    low = jnp.where(me > 0, jnp.where(even, b, a), nothing)
    high = jnp.where(me < count - 1, jnp.where(even, a, b), nothing)
    return low, high


def place_kernel(counts, lists, pair, first, second, out, live, both):
    count = pair.shape[0]
    both[0:count, :] = pair[...]
    both[count:, :] = jnp.zeros((both.shape[0] - count, 256), jnp.bfloat16)
    slots = position_slots(lists, counts)
    z, x = face_indices()
    low, high = (
        dot(
            one_hot(slot_rows(slots, z, x, jnp.full_like(x, y), x >= 0), both.shape[0]), both[...]
        ).astype(jnp.bfloat16)
        for y in (0, NY - 1)
    )
    write_by_parity("wire", low, high, first, second)
    z, x, j = grid_indices()
    rows = slot_rows(slots, z, x, j - 1, (j >= 1) & (j <= NY))
    live[...] = (rows >= 0).astype(jnp.bfloat16)
    out[...] = dot(one_hot(rows, both.shape[0]), both[...]).astype(jnp.bfloat16)


def insert_faces(placed, got_first, got_second, out, slab_first, slab_second, faces):
    low, high = read_by_parity("wire", got_first, got_second)
    faces[0:FACE, :] = low
    faces[FACE : 2 * FACE, :] = high
    faces[2 * FACE :, :] = jnp.zeros((faces.shape[0] - 2 * FACE, 256), jnp.bfloat16)
    z, x, j = grid_indices()
    rows = z * NX + x
    rows = jnp.where(j == 0, rows, jnp.where(j == NY + 1, rows + FACE, -1))
    full = (placed[...].astype(jnp.float32) + dot(one_hot(rows, 128), faces[...])).astype(jnp.bfloat16)
    out[...] = full
    low = jnp.concatenate([full[z * PLANE : z * PLANE + J, :] for z in range(4)], axis=0)
    high = jnp.concatenate([full[(z + 1) * PLANE - J : (z + 1) * PLANE, :] for z in range(4)], axis=0)
    write_by_parity("drift", low, high, slab_first, slab_second)


def build_window(window, base, plane_of):
    for zi in range(4):
        plane = plane_of(zi)
        wide = plane.astype(jnp.float32)
        before = pltpu.roll(wide, 1, 0).astype(jnp.bfloat16)
        after = pltpu.roll(wide, plane.shape[0] - 1, 0).astype(jnp.bfloat16)
        for oy, shifted in enumerate((before, plane, after)):
            for z in range(max(0, zi - 1), min(3, zi + 1) + 1):
                lane = 128 * (3 * oy + zi - z + 1)
                window[base + z, :, lane : lane + 128] = shifted
    empty = jnp.zeros((plane.shape[0], 128), jnp.bfloat16)
    for oy in range(3):
        window[base, :, 384 * oy : 384 * oy + 128] = empty
        window[base + 3, :, 384 * oy + 256 : 384 * oy + 384] = empty


def wide_plane(full, low, high, z, lanes):
    return jnp.concatenate(
        [
            low[z * J : (z + 1) * J, lanes],
            full[z * PLANE : (z + 1) * PLANE, lanes],
            high[z * J : (z + 1) * J, lanes],
        ],
        axis=0,
    )


def conv(window, weights, base):
    total = None
    for ox in range(3):
        rows = window[:, ox * J : ox * J + PLANE, :].reshape(ROWS, 1152)
        term = dot(rows, weights[base + 9 * ox : base + 9 * (ox + 1)].reshape(1152, 128))
        total = term if total is None else total + term
    return total


def flip_blocks(weights, base, flipped):
    for k in range(TAPS):
        flipped[:, 128 * k : 128 * (k + 1)] = weights[base + TAPS - 1 - k]


def conv_flipped(window, flipped):
    total = None
    for ox in range(3):
        rows = window[:, ox * J : ox * J + PLANE, :].reshape(ROWS, 1152)
        term = lax.dot_general(
            rows,
            flipped[:, 1152 * ox : 1152 * (ox + 1)],
            (((1,), (1,)), ((), ())),
            preferred_element_type=jnp.float32,
        )
        total = term if total is None else total + term
    return total


def inner_kernel(full, weights, pre, window):
    edge = jnp.zeros((SLAB, 128), jnp.bfloat16)
    build_window(window, 0, lambda z: wide_plane(full, edge, edge, z, slice(0, 128)))
    pre[...] = conv(window, weights, 0)


def add_edges(pre, low, high, weights, edge_window):
    for ox, x, slab in ((0, 0, low), (2, NX - 1, high)):
        build_window(edge_window, 0, lambda z: slab[z * J : (z + 1) * J, :])
        taps = weights[9 * ox : 9 * (ox + 1)].reshape(1152, 128)
        term = dot(edge_window[...].reshape(SLAB, 1152), taps)
        for z in range(4):
            start = z * PLANE + x * J
            pre[start : start + J, :] += term[z * J : (z + 1) * J, :]


def first_kernel(full, got_first, got_second, live, weights, inner, hb, keep, send, window, flipped, edge_window, pre):
    f_lanes, g_lanes = slice(0, 128), slice(128, 256)
    low, high = read_by_parity("drift", got_first, got_second)
    alive = live[...].astype(jnp.float32)
    flip_blocks(weights, TAPS, flipped)
    pre[...] = inner[...]
    add_edges(pre, low[:, f_lanes], high[:, f_lanes], weights, edge_window)
    first_pre = pre[...]
    gate = jax.nn.sigmoid(first_pre)
    hidden = (alive * (first_pre * gate)).astype(jnp.bfloat16)
    slope = alive * (gate * (1.0 + first_pre * (1.0 - gate)))
    build_window(window, 0, lambda z: wide_plane(full, low, high, z, g_lanes))
    back = (conv_flipped(window, flipped) * slope).astype(jnp.bfloat16)
    hb[...] = jnp.concatenate([hidden, back], axis=1)
    core = lax.axis_index("drift") % 2

    def write(to, values, lanes):
        to[0:ROWS, :] = values
        for z in range(4):
            start = ROWS + z * WIDE
            to[start : start + WIDE, :] = wide_plane(full, low, high, z, lanes)

    @pl.when(core == 0)
    def _():
        write(keep, hidden, g_lanes)
        write(send, back, f_lanes)

    @pl.when(core != 0)
    def _():
        write(keep, back, f_lanes)
        write(send, hidden, g_lanes)


def add_terms(part, window, total, fresh):
    build_window(window, 0, lambda z: part[ROWS + z * WIDE : ROWS + (z + 1) * WIDE, :])
    left = part[0:ROWS, :].astype(jnp.float32).T.astype(jnp.bfloat16)
    for ox in range(3):
        shifted = window[:, ox * J : ox * J + PLANE, :].reshape(ROWS, 1152)
        product = dot(left, shifted)
        for k in range(9):
            start = 128 * (9 * ox + k)
            term = product[:, 128 * k : 128 * (k + 1)]
            total[start : start + 128, :] = term if fresh else total[start : start + 128, :] + term


def own_terms_kernel(mine, total, window):
    rows = TAPS * CHANNELS
    if total.shape[0] > rows:
        total[rows:, :] = jnp.zeros((total.shape[0] - rows, 128), jnp.float32)
    add_terms(mine, window, total, True)


def terms_kernel(chunk, mine, theirs, hb, *refs):
    *sends, own, first, second, window, total = refs
    total[...] = mine[...]
    add_terms(theirs, window, total, False)
    me = lax.axis_index("drift") // 2
    own[...] = total[pl.ds(pl.multiple_of(me * chunk, 16), chunk), :]
    for step, out in enumerate(sends):
        start = pl.multiple_of((me ^ (step + 1)) * chunk, 16)
        out[...] = total[pl.ds(start, chunk), :].astype(jnp.bfloat16)
    z, x = face_indices()
    start = z * PLANE + x * J
    low, high = (dot(one_hot(start + j, ROWS), hb[...]).astype(jnp.bfloat16) for j in (1, NY))
    write_by_parity("wire", low, high, first, second)


def split_kernel(unit, count, after, own, *refs):
    received, (*sends, rest, total) = refs[:count], refs[count:]
    summed = own[...]
    for part in received:
        summed = summed + part[...].astype(jnp.float32)
    total[...] = summed
    me = lax.axis_index("wire")
    rest[...] = total[pl.ds(pl.multiple_of(me * unit, 16), unit), :]
    for step, out in enumerate(sends):
        start = pl.multiple_of((me ^ (step + 1)) * unit, 16)
        out[...] = total[pl.ds(start, unit), :].astype(jnp.bfloat16)


def sum_kernel(scale, after_first, after_second, own, *refs):
    *received, out = refs
    summed = own[...]
    for part in received:
        summed = summed + part[...].astype(jnp.float32)
    out[...] = (summed * scale).astype(jnp.bfloat16)


def joined_kernel(unit, after, *refs):
    *parts, out = refs
    me = lax.axis_index("wire")
    for step, part in enumerate(parts):
        start = pl.multiple_of((me ^ step) * unit, 16)
        out[pl.ds(start, unit), :] = part[...]


def final_kernel(steps, blocks, after, *refs):
    mine, theirs = refs[: len(steps)], refs[len(steps) : 2 * len(steps)]
    first, second, staged, sems = refs[-4:]
    me = lax.axis_index("drift") // 2
    even = lax.axis_index("drift") % 2 == 0

    def copies(n, i):
        tap = (me ^ steps[n]) * blocks + i
        here = n * blocks + i
        safe = jnp.minimum(tap, TAPS - 1)
        return tap < TAPS, (
            pltpu.make_async_copy(staged.at[0, here], second.at[TAPS - 1 - safe], sems.at[0, here]),
            pltpu.make_async_copy(staged.at[1, here], first.at[safe], sems.at[1, here]),
        )

    for n in range(len(steps)):
        a, b = mine[n][...], theirs[n][...]
        for_second = jnp.where(even, a, b).astype(jnp.float32)
        for_first = jnp.where(even, b, a).astype(jnp.float32)
        for i in range(blocks):
            here = n * blocks + i
            staged[0, here] = for_second[128 * i : 128 * (i + 1), :]
            staged[1, here] = for_first[128 * i : 128 * (i + 1), :].T
            used, pair = copies(n, i)

            @pl.when(used)
            def _():
                for copy in pair:
                    copy.start()

    for n in range(len(steps)):
        for i in range(blocks):
            used, pair = copies(n, i)

            @pl.when(used)
            def _():
                for copy in pair:
                    copy.wait()


def second_kernel(field, flip, lists, counts, hb, got_first, got_second, base, live, weights, output, done, window, *flipped):
    low, high = read_by_parity("drift", got_first, got_second)
    lanes = slice(128 * field, 128 * (field + 1))
    build_window(window, 0, lambda z: wide_plane(hb, low, high, z, lanes))
    if flip:
        flip_blocks(weights, 0, *flipped)
        value = conv_flipped(window, *flipped)
    else:
        value = conv(window, weights, TAPS)
    result = (live[...].astype(jnp.float32) * (base[:, lanes].astype(jnp.float32) + value)).astype(jnp.bfloat16)
    slots = position_slots(lists, counts)
    count = output.shape[0]
    pieces = []
    row = iota((count, 128), 0)
    for c in range(ROWS // 128):
        col = iota((8, 128), 1) + 128 * c
        z = (col >= PLANE).astype(jnp.int32) + (col >= 2 * PLANE) + (col >= 3 * PLANE)
        rest = col - PLANE * z
        x, j = rest >> 4, rest & 15
        source = slot_rows(slots, z, x, j - 1, (j >= 1) & (j <= NY))
        source = jnp.broadcast_to(source[0:1, :], (count, 128))
        pieces.append(jnp.where(row == source, 1.0, 0.0).astype(jnp.bfloat16))
    output[...] = dot(jnp.concatenate(pieces, axis=1), result).astype(jnp.bfloat16)
    done[...] = jnp.zeros_like(done)


def pairs(value_first, value_second, axis):
    drift, wire = lax.axis_size("drift"), lax.axis_size("wire")
    count = lax.axis_size(axis)
    first = [(i, i ^ 1) for i in range(count) if i ^ 1 < count]
    second = {i: i + 1 if i % 2 else i - 1 for i in range(1, count - 1)}
    if axis == "drift":
        second.update({0: count - 1, count - 1: 0})
        got_second = lax.ppermute(value_second, axis, sorted(second.items()))
    else:
        moves = [
            (d * wire + w, d * wire + second[w] if w in second else (d ^ 1) * wire + w)
            for d in range(drift)
            for w in range(wire)
        ]
        got_second = lax.ppermute(value_second, ("drift", "wire"), moves)
    got_first = lax.ppermute(value_first, axis, first)
    return got_first, got_second


def on_device(features, first_weight, second_weight, cotangent, counts, kernel_map, send_lists):
    drift, wire = lax.axis_size("drift"), lax.axis_size("wire")
    chips = drift // 2
    blocks = -(-TAPS // chips)
    chunk = blocks * CHANNELS
    unit = chunk // wire
    rows = TAPS * CHANNELS
    f, g = features[0, 0], cotangent[0, 0]
    slots = f.shape[0]
    padded = -(-slots // 128) * 128
    conv_scratch = [pltpu.VMEM((4, WIDE, 1152), jnp.bfloat16), pltpu.VMEM((128, rows), jnp.bfloat16)]
    faces_scratch = pltpu.VMEM((128, 256), jnp.bfloat16)
    face, slab, grid = bf16(FACE, 256), bf16(SLAB, 256), bf16(ROWS, 256)

    def swap_core(value):
        return lax.ppermute(value, "drift", [(i, i ^ 1) for i in range(drift)])

    def to_chip(value, step):
        return lax.ppermute(value, "drift", [(i, i ^ (2 * step)) for i in range(drift)])

    def to_wire(value, step):
        return lax.ppermute(value, "wire", [(i, i ^ step) for i in range(wire)])

    pair = jnp.concatenate([f, g], axis=1)
    weights = jnp.concatenate([first_weight, second_weight], axis=0)
    *faces, placed, live = call(
        place_kernel,
        (face, face, grid, bf16(ROWS, 128)),
        [SMEM] * 2 + [VMEM],
        [pltpu.VMEM((padded, 256), jnp.bfloat16)],
    )(counts, send_lists, pair)
    faces = pairs(*faces, "wire")
    full, *slabs = call(insert_faces, (grid, slab, slab), [VMEM] * 3, [faces_scratch])(placed, *faces)
    slabs = pairs(*slabs, "drift")
    message = bf16(ROWS + 4 * WIDE, 128)
    inner = call(inner_kernel, f32(ROWS, 128), [VMEM] * 2, conv_scratch[:1])(full, weights)
    hb, keep, send = call(
        first_kernel,
        (grid, message, message),
        [VMEM] * 6,
        conv_scratch + [pltpu.VMEM((4, J, 1152), jnp.bfloat16), pltpu.VMEM((ROWS, 128), jnp.float32)],
    )(full, *slabs, live, weights, inner)
    got = swap_core(send)
    term_window = pltpu.VMEM((4, WIDE, 1152), jnp.bfloat16)
    terms = f32(chunk * chips, 128)
    own_terms = call(own_terms_kernel, terms, [VMEM], [term_window])(keep)
    *sends, own, face_first, face_second = call(
        functools.partial(terms_kernel, chunk),
        tuple([bf16(chunk, 128)] * (chips - 1) + [f32(chunk, 128), face, face]),
        [VMEM] * 3,
        [term_window, pltpu.VMEM(terms.shape, jnp.float32)],
    )(own_terms, got, hb)
    parts = [to_chip(s, k + 1) for k, s in enumerate(sends)]
    faces = pairs(face_first, face_second, "wire")
    hb_full, *hb_slabs = call(insert_faces, (grid, slab, slab), [VMEM] * 3, [faces_scratch])(hb, *faces)
    inserted = hb_slabs[0]
    hb_slabs = pairs(*hb_slabs, "drift")
    def second(field, flip):
        return call(
            functools.partial(second_kernel, field, flip),
            (bf16(slots, 128), f32(8, 128)),
            [SMEM] * 2 + [VMEM] * 6,
            conv_scratch if flip else conv_scratch[:1],
        )(send_lists, counts, hb_full, *hb_slabs, full, live, weights)

    grad_features, grad_done = second(1, True)
    output, output_done = second(0, False)
    *sends, own = call(
        functools.partial(split_kernel, unit, chips - 1),
        tuple([bf16(unit, 128)] * (wire - 1) + [f32(unit, 128)]),
        [VMEM] * (1 + chips),
        [pltpu.VMEM((chunk, 128), jnp.float32)],
    )(inserted, own, *parts)

    received = [to_wire(s, k + 1) for k, s in enumerate(sends)]
    scale = 1.0 / math.sqrt(float(drift * wire * slots))
    summed = call(functools.partial(sum_kernel, scale), bf16(unit, 128), [VMEM] * (2 + wire))(
        *hb_slabs, own, *received
    )
    pieces = [summed] + [to_wire(summed, k) for k in range(1, wire)]
    mine = call(functools.partial(joined_kernel, unit), bf16(chunk, 128), [VMEM] * (1 + wire))(grad_done, *pieces)
    mine = [mine] + [to_chip(mine, k) for k in range(1, chips)]
    grads = ()
    early = max(1, chips - 2)
    for steps in [tuple(range(early))] + [(k,) for k in range(early, chips)]:
        staged = blocks * len(steps)
        grads = call(
            functools.partial(final_kernel, steps, blocks),
            (f32(TAPS, 128, 128), f32(TAPS, 128, 128)),
            [VMEM] * (1 + 2 * len(steps)) + [HBM] * len(grads),
            [pltpu.VMEM((2, staged, 128, 128), jnp.float32), pltpu.SemaphoreType.DMA((2, staged))],
            50 * 10**9,
            HBM,
            {1 + 2 * len(steps): 0, 2 + 2 * len(steps): 1} if grads else {},
        )(output_done, *(mine[k] for k in steps), *(swap_core(mine[k]) for k in steps), *grads)
    grad_first, grad_second = grads
    return output[None, None], grad_features[None, None], grad_first, grad_second


def solution(mesh):
    placed = (
        P("drift", "wire", None, None),
        P(),
        P(),
        P("drift", "wire", None, None),
        P("drift", "wire"),
        P("drift", "wire", None, None),
        P("drift", "wire", None),
    )
    return jax.shard_map(
        on_device,
        mesh=mesh,
        in_specs=placed,
        out_specs=(P("drift", "wire", None, None), P("drift", "wire", None, None), P(), P()),
        check_vma=False,
    )
```

```python
import functools
import math

import jax
import jax.numpy as jnp
from jax import lax
from jax.experimental import pallas as pl
from jax.experimental.pallas import tpu as pltpu
from jax.sharding import PartitionSpec as P

BX = 3
BW = 3
NX = 4 * BX
NY = 4 * BW
J = 16
PLANE = NX * J
WIDE = (NX + 2) * J
ROWS = 4 * PLANE
FACE = 4 * NX
SLAB = 4 * J
CHANNELS = 128
TAPS = 27
VMEM = pl.BlockSpec(memory_space=pltpu.VMEM)
HBM = pl.BlockSpec(memory_space=pltpu.HBM)
SMEM = pl.BlockSpec(memory_space=pltpu.SMEM)
LISTED = {0: 0, 1: 1, 2: 2, 3: 7, 5: 10, 6: 3, 7: 4, 8: 5}


def call(kernel, out_shape, in_specs, scratch=(), flops=0, out_spec=VMEM, aliases={}, vmem=40):
    return pl.pallas_call(
        kernel,
        out_shape=out_shape,
        in_specs=in_specs,
        out_specs=out_spec if isinstance(out_spec, tuple) else jax.tree.map(lambda _: out_spec, out_shape),
        scratch_shapes=list(scratch),
        input_output_aliases=aliases,
        compiler_params=pltpu.CompilerParams(vmem_limit_bytes=vmem * 1024 * 1024),
        cost_estimate=pl.CostEstimate(
            flops=flops, bytes_accessed=0, transcendentals=0
        ),
    )


def bf16(*shape):
    return jax.ShapeDtypeStruct(shape, jnp.bfloat16)


def f32(*shape):
    return jax.ShapeDtypeStruct(shape, jnp.float32)


def iota(shape, dim):
    return lax.broadcasted_iota(jnp.int32, shape, dim)


def position_slots(lists, counts):
    slots = {p: lists[0, 0, i] for p, i in LISTED.items()}
    present = {p: (s < 9).astype(jnp.int32) for p, s in slots.items()}
    before = present[0] + present[1] + present[2] + present[3]
    others = before + present[5] + present[6] + present[7] + present[8]
    slots[4] = jnp.where(counts[0, 0] > others, before, 9)
    return slots


def slot_rows(slots, z, x, y, valid):
    position = (x >> 2) * BW + (y >> 2)
    slot = jnp.full(position.shape, 9, jnp.int32)
    for p, s in slots.items():
        slot = jnp.where(position == p, s, slot)
    row = slot * 64 + (x & 3) * 16 + (y & 3) * 4 + z
    return jnp.where(valid & (slot < 9), row, -1)


def one_hot(rows, width):
    lane = iota(rows.shape, 1)
    parts = [jnp.where(rows == lane + 128 * c, 1.0, 0.0).astype(jnp.bfloat16) for c in range(width // 128)]
    return jnp.concatenate(parts, axis=1)


def dot(a, b):
    return jnp.dot(a, b, preferred_element_type=jnp.float32)


def grid_indices():
    shape = (4, NX, J, 128)
    z, x, j = (iota(shape, d).reshape(ROWS, 128) for d in range(3))
    return z, x, j


def face_indices():
    r = iota((FACE, 128), 0)
    z = (r >= NX).astype(jnp.int32) + (r >= 2 * NX) + (r >= 3 * NX)
    return z, r - NX * z


def write_by_parity(axis, low, high, first, second):
    even = lax.axis_index(axis) % 2 == 0
    first[...] = jnp.where(even, high, low)
    second[...] = jnp.where(even, low, high)


def read_by_parity(axis, first, second):
    me, count = lax.axis_index(axis), lax.axis_size(axis)
    even = me % 2 == 0
    a, b = first[...], second[...]
    nothing = jnp.zeros_like(a)
    low = jnp.where(me > 0, jnp.where(even, b, a), nothing)
    high = jnp.where(me < count - 1, jnp.where(even, a, b), nothing)
    return low, high


def place_kernel(counts, lists, pair, first, second, out, live, both):
    count = pair.shape[0]
    both[0:count, :] = pair[...]
    both[count:, :] = jnp.zeros((both.shape[0] - count, 256), jnp.bfloat16)
    slots = position_slots(lists, counts)
    z, x = face_indices()
    low, high = (
        dot(
            one_hot(slot_rows(slots, z, x, jnp.full_like(x, y), x >= 0), both.shape[0]), both[...]
        ).astype(jnp.bfloat16)
        for y in (0, NY - 1)
    )
    write_by_parity("wire", low, high, first, second)
    z, x, j = grid_indices()
    rows = slot_rows(slots, z, x, j - 1, (j >= 1) & (j <= NY))
    live[...] = (rows >= 0).astype(jnp.bfloat16)
    out[...] = dot(one_hot(rows, both.shape[0]), both[...]).astype(jnp.bfloat16)


def insert_faces(placed, got_first, got_second, out, slab_first, slab_second, faces):
    low, high = read_by_parity("wire", got_first, got_second)
    faces[0:FACE, :] = low
    faces[FACE : 2 * FACE, :] = high
    faces[2 * FACE :, :] = jnp.zeros((faces.shape[0] - 2 * FACE, 256), jnp.bfloat16)
    z, x, j = grid_indices()
    rows = z * NX + x
    rows = jnp.where(j == 0, rows, jnp.where(j == NY + 1, rows + FACE, -1))
    full = (placed[...].astype(jnp.float32) + dot(one_hot(rows, 128), faces[...])).astype(jnp.bfloat16)
    out[...] = full
    low = jnp.concatenate([full[z * PLANE : z * PLANE + J, :] for z in range(4)], axis=0)
    high = jnp.concatenate([full[(z + 1) * PLANE - J : (z + 1) * PLANE, :] for z in range(4)], axis=0)
    write_by_parity("drift", low, high, slab_first, slab_second)


def build_window(window, base, plane_of):
    for zi in range(4):
        plane = plane_of(zi)
        wide = plane.astype(jnp.float32)
        before = pltpu.roll(wide, 1, 0).astype(jnp.bfloat16)
        after = pltpu.roll(wide, plane.shape[0] - 1, 0).astype(jnp.bfloat16)
        for oy, shifted in enumerate((before, plane, after)):
            for z in range(max(0, zi - 1), min(3, zi + 1) + 1):
                lane = 128 * (3 * oy + zi - z + 1)
                window[base + z, :, lane : lane + 128] = shifted
    empty = jnp.zeros((plane.shape[0], 128), jnp.bfloat16)
    for oy in range(3):
        window[base, :, 384 * oy : 384 * oy + 128] = empty
        window[base + 3, :, 384 * oy + 256 : 384 * oy + 384] = empty


def wide_plane(full, low, high, z, lanes):
    return jnp.concatenate(
        [
            low[z * J : (z + 1) * J, lanes],
            full[z * PLANE : (z + 1) * PLANE, lanes],
            high[z * J : (z + 1) * J, lanes],
        ],
        axis=0,
    )


def conv(window, weights, base):
    total = None
    for ox in range(3):
        rows = window[:, ox * J : ox * J + PLANE, :].reshape(ROWS, 1152)
        term = dot(rows, weights[base + 9 * ox : base + 9 * (ox + 1)].reshape(1152, 128))
        total = term if total is None else total + term
    return total


def flip_blocks(weights, base, flipped):
    for k in range(TAPS):
        flipped[:, 128 * k : 128 * (k + 1)] = weights[base + TAPS - 1 - k]


def conv_flipped(window, flipped):
    total = None
    for ox in range(3):
        rows = window[:, ox * J : ox * J + PLANE, :].reshape(ROWS, 1152)
        term = lax.dot_general(
            rows,
            flipped[:, 1152 * ox : 1152 * (ox + 1)],
            (((1,), (1,)), ((), ())),
            preferred_element_type=jnp.float32,
        )
        total = term if total is None else total + term
    return total


def inner_kernel(full, weights, pre, window):
    edge = jnp.zeros((SLAB, 128), jnp.bfloat16)
    build_window(window, 0, lambda z: wide_plane(full, edge, edge, z, slice(0, 128)))
    pre[...] = conv(window, weights, 0)


def add_edges(pre, low, high, weights, edge_window):
    for ox, x, slab in ((0, 0, low), (2, NX - 1, high)):
        build_window(edge_window, 0, lambda z: slab[z * J : (z + 1) * J, :])
        taps = weights[9 * ox : 9 * (ox + 1)].reshape(1152, 128)
        term = dot(edge_window[...].reshape(SLAB, 1152), taps)
        for z in range(4):
            start = z * PLANE + x * J
            pre[start : start + J, :] += term[z * J : (z + 1) * J, :]


def first_kernel(full, got_first, got_second, live, weights, inner, hb, keep, send, window, flipped, edge_window, pre):
    f_lanes, g_lanes = slice(0, 128), slice(128, 256)
    low, high = read_by_parity("drift", got_first, got_second)
    alive = live[...].astype(jnp.float32)
    flip_blocks(weights, TAPS, flipped)
    pre[...] = inner[...]
    add_edges(pre, low[:, f_lanes], high[:, f_lanes], weights, edge_window)
    first_pre = pre[...]
    gate = jax.nn.sigmoid(first_pre)
    hidden = (alive * (first_pre * gate)).astype(jnp.bfloat16)
    slope = alive * (gate * (1.0 + first_pre * (1.0 - gate)))
    build_window(window, 0, lambda z: wide_plane(full, low, high, z, g_lanes))
    back = (conv_flipped(window, flipped) * slope).astype(jnp.bfloat16)
    hb[...] = jnp.concatenate([hidden, back], axis=1)
    core = lax.axis_index("drift") % 2

    def write(to, values, lanes):
        to[0:ROWS, :] = values
        for z in range(4):
            start = ROWS + z * WIDE
            to[start : start + WIDE, :] = wide_plane(full, low, high, z, lanes)

    @pl.when(core == 0)
    def _():
        write(keep, hidden, g_lanes)
        write(send, back, f_lanes)

    @pl.when(core != 0)
    def _():
        write(keep, back, f_lanes)
        write(send, hidden, g_lanes)


def chip_mask(kind, core):
    if isinstance(kind, int):
        return kind
    first = 1 + core
    return {"own": 0, "first": first, "second": 3 - first, "opposite": 3}[kind]


def add_terms(part, window, total, fresh):
    build_window(window, 0, lambda z: part[ROWS + z * WIDE : ROWS + (z + 1) * WIDE, :])
    left = part[0:ROWS, :].astype(jnp.float32).T.astype(jnp.bfloat16)
    for ox in range(3):
        shifted = window[:, ox * J : ox * J + PLANE, :].reshape(ROWS, 1152)
        product = dot(left, shifted)
        for k in range(9):
            start = 128 * (9 * ox + k)
            term = product[:, 128 * k : 128 * (k + 1)]
            total[start : start + 128, :] = term if fresh else total[start : start + 128, :] + term


def own_terms_kernel(mine, total, window):
    rows = TAPS * CHANNELS
    if total.shape[0] > rows:
        total[rows:, :] = jnp.zeros((total.shape[0] - rows, 128), jnp.float32)
    add_terms(mine, window, total, True)


def terms_kernel(chunk, kinds, mine, theirs, hb, *refs):
    *outs, first, second, window, total = refs
    total[...] = mine[...]
    add_terms(theirs, window, total, False)
    me, core = lax.axis_index("drift") // 2, lax.axis_index("drift") % 2
    for kind, out in zip(kinds, outs):
        start = pl.multiple_of((me ^ chip_mask(kind, core)) * chunk, 128)
        out[...] = total[pl.ds(start, chunk), :].astype(out.dtype)
    z, x = face_indices()
    start = z * PLANE + x * J
    low, high = (dot(one_hot(start + j, ROWS), hb[...]).astype(jnp.bfloat16) for j in (1, NY))
    write_by_parity("wire", low, high, first, second)


def passed_on_kernel(partial, received, out):
    out[...] = (partial[...] + received[...].astype(jnp.float32)).astype(jnp.bfloat16)


def relay_kernel(after, value, out):
    out[...] = value[...]


def split_kernel(unit, count, after, own, *refs):
    received, (*sends, rest, total) = refs[:count], refs[count:]
    summed = own[...]
    for part in received:
        summed = summed + part[...].astype(jnp.float32)
    total[...] = summed
    me = lax.axis_index("wire")
    rest[...] = total[pl.ds(pl.multiple_of(me * unit, 16), unit), :]
    for step, out in enumerate(sends):
        start = pl.multiple_of((me ^ (step + 1)) * unit, 16)
        out[...] = total[pl.ds(start, unit), :].astype(jnp.bfloat16)


def sum_kernel(scale, after_inner, after_first, after_second, own, *refs):
    *received, out = refs
    summed = own[...]
    for part in received:
        summed = summed + part[...].astype(jnp.float32)
    out[...] = (summed * scale).astype(jnp.bfloat16)


def joined_kernel(unit, *refs):
    *parts, out = refs
    me = lax.axis_index("wire")
    for step, part in enumerate(parts):
        start = pl.multiple_of((me ^ step) * unit, 16)
        out[pl.ds(start, unit), :] = part[...]


def final_kernel(items, blocks, want_done, *refs):
    parts = refs[: len(items)]
    first, second, *done, staged, sems = refs[len(refs) - 4 - want_done :]
    me = lax.axis_index("drift") // 2
    for ref in done:
        ref[...] = jnp.zeros_like(ref)

    def write(core):
        copies = []
        for part, (kind, mine) in zip(parts, items):
            source = core if mine else 1 - core
            value = part[...].astype(jnp.float32)
            count, here = part.shape[0] // 128, len(copies)
            for i in range(count):
                block = value[128 * i : 128 * (i + 1), :]
                staged[here + i] = block.T if source else block
            chunk = me ^ chip_mask(kind, source)
            for i in range(count):
                tap = chunk * blocks + i
                safe = jnp.minimum(tap, TAPS - 1)
                to = first.at[safe] if source else second.at[TAPS - 1 - safe]
                copies.append((tap < TAPS, pltpu.make_async_copy(staged.at[here + i], to, sems.at[here + i])))
                pl.when(copies[-1][0])(copies[-1][1].start)
        for used, copy in copies:
            pl.when(used)(copy.wait)

    even = lax.axis_index("drift") % 2 == 0
    pl.when(even)(lambda: write(0))
    pl.when(jnp.logical_not(even))(lambda: write(1))


def second_inner_kernel(hb, weights, inner, done, window, flipped):
    edge = jnp.zeros((SLAB, 256), jnp.bfloat16)
    flip_blocks(weights, 0, flipped)
    build_window(window, 0, lambda z: wide_plane(hb, edge, edge, z, slice(0, 128)))
    inner[0] = conv(window, weights, TAPS)
    build_window(window, 0, lambda z: wide_plane(hb, edge, edge, z, slice(128, 256)))
    inner[1] = conv_flipped(window, flipped)
    done[...] = jnp.zeros_like(done)


def second_kernel(
    lists, counts, inner, got_first, got_second, base, live, weights, held, output, grad, passed, edge_window, pre, taps
):
    low, high = read_by_parity("drift", got_first, got_second)
    results = []
    for field in (0, 1):
        lanes = slice(128 * field, 128 * (field + 1))
        pre[...] = inner[field]
        if field:
            for k in (*range(9), *range(18, 27)):
                taps[k] = weights[TAPS - 1 - k].astype(jnp.float32).T.astype(jnp.bfloat16)
            add_edges(pre, low[:, lanes], high[:, lanes], taps, edge_window)
        else:
            add_edges(pre, low[:, lanes], high[:, lanes], weights.at[TAPS:], edge_window)
        value = base[:, lanes].astype(jnp.float32) + pre[...]
        results.append((live[...].astype(jnp.float32) * value).astype(jnp.bfloat16))
    both = jnp.concatenate(results, axis=1)
    slots = position_slots(lists, counts)
    count = output.shape[0]
    pieces = []
    row = iota((count, 128), 0)
    for c in range(ROWS // 128):
        col = iota((8, 128), 1) + 128 * c
        z = (col >= PLANE).astype(jnp.int32) + (col >= 2 * PLANE) + (col >= 3 * PLANE)
        rest = col - PLANE * z
        x, j = rest >> 4, rest & 15
        source = slot_rows(slots, z, x, j - 1, (j >= 1) & (j <= NY))
        source = jnp.broadcast_to(source[0:1, :], (count, 128))
        pieces.append(jnp.where(row == source, 1.0, 0.0).astype(jnp.bfloat16))
    by_slot = dot(jnp.concatenate(pieces, axis=1), both).astype(jnp.bfloat16)
    output[...] = by_slot[:, 0:128]
    grad[...] = by_slot[:, 128:256]
    passed[...] = held[...]


def pairs(value_first, value_second, axis):
    drift, wire = lax.axis_size("drift"), lax.axis_size("wire")
    count = lax.axis_size(axis)
    first = [(i, i ^ 1) for i in range(count) if i ^ 1 < count]
    second = {i: i + 1 if i % 2 else i - 1 for i in range(1, count - 1)}
    if axis == "drift":
        second.update({0: count - 1, count - 1: 0})
        got_second = lax.ppermute(value_second, axis, sorted(second.items()))
    else:
        moves = [
            (d * wire + w, d * wire + second[w] if w in second else (d ^ 1) * wire + w)
            for d in range(drift)
            for w in range(wire)
        ]
        got_second = lax.ppermute(value_second, ("drift", "wire"), moves)
    got_first = lax.ppermute(value_first, axis, first)
    return got_first, got_second


def on_device(features, first_weight, second_weight, cotangent, counts, kernel_map, send_lists):
    drift, wire = lax.axis_size("drift"), lax.axis_size("wire")
    chips = drift // 2
    blocks = -(-TAPS // chips)
    chunk = blocks * CHANNELS
    unit = chunk // wire
    rows = TAPS * CHANNELS
    f, g = features[0, 0], cotangent[0, 0]
    slots = f.shape[0]
    padded = -(-slots // 128) * 128
    conv_scratch = [pltpu.VMEM((4, WIDE, 1152), jnp.bfloat16), pltpu.VMEM((128, rows), jnp.bfloat16)]
    edge_window = pltpu.VMEM((4, J, 1152), jnp.bfloat16)
    faces_scratch = pltpu.VMEM((128, 256), jnp.bfloat16)
    face, slab, grid = bf16(FACE, 256), bf16(SLAB, 256), bf16(ROWS, 256)

    def swap_core(value):
        return lax.ppermute(value, "drift", [(i, i ^ 1) for i in range(drift)])

    def to_chip(value, kind):
        return lax.ppermute(value, "drift", [(i, i ^ (2 * chip_mask(kind, i % 2))) for i in range(drift)])

    def to_wire(value, step):
        return lax.ppermute(value, "wire", [(i, i ^ step) for i in range(wire)])

    pair = jnp.concatenate([f, g], axis=1)
    weights = jnp.concatenate([first_weight, second_weight], axis=0)
    *faces, placed, live = call(
        place_kernel,
        (face, face, grid, bf16(ROWS, 128)),
        [SMEM] * 2 + [VMEM],
        [pltpu.VMEM((padded, 256), jnp.bfloat16)],
    )(counts, send_lists, pair)
    faces = pairs(*faces, "wire")
    full, *slabs = call(insert_faces, (grid, slab, slab), [VMEM] * 3, [faces_scratch])(placed, *faces)
    slabs = pairs(*slabs, "drift")
    message = bf16(ROWS + 4 * WIDE, 128)
    inner = call(inner_kernel, f32(ROWS, 128), [VMEM] * 2, conv_scratch[:1])(full, weights)
    hb, keep, send = call(
        first_kernel,
        (grid, message, message),
        [VMEM] * 6,
        conv_scratch + [edge_window, pltpu.VMEM((ROWS, 128), jnp.float32)],
    )(full, *slabs, live, weights, inner)
    got = swap_core(send)
    term_window = pltpu.VMEM((4, WIDE, 1152), jnp.bfloat16)
    terms = f32(chunk * chips, 128)
    own_terms = call(own_terms_kernel, terms, [VMEM], [term_window])(keep)
    four = chips == 4
    kinds = ("opposite", "first", "second", "own") if four else (*range(1, chips), 0)
    shapes = [f32(chunk, 128) if k in ("second", "own", 0) else bf16(chunk, 128) for k in kinds]
    *sends, own, face_first, face_second = call(
        functools.partial(terms_kernel, chunk, kinds),
        (*shapes, face, face),
        [VMEM] * 3,
        [term_window, pltpu.VMEM(terms.shape, jnp.float32)],
    )(own_terms, got, hb)
    if four:
        opposite, first, second_part = sends
        passed = to_chip(opposite, "first")
        parts = [to_chip(first, "first")]
        passed = call(passed_on_kernel, bf16(chunk, 128), [VMEM] * 2)(second_part, passed)
        parts.append(to_chip(passed, "second"))
    else:
        parts = [to_chip(value, k) for k, value in zip(kinds, sends)]
    faces = pairs(face_first, face_second, "wire")
    hb_full, *hb_slabs = call(insert_faces, (grid, slab, slab), [VMEM] * 3, [faces_scratch])(hb, *faces)
    inserted = hb_slabs[0]
    hb_slabs = pairs(*hb_slabs, "drift")
    token = f32(8, 128)
    inner, inner_done = call(second_inner_kernel, (f32(2, ROWS, 128), token), [VMEM] * 2, conv_scratch)(hb_full, weights)
    *sends, own = call(
        functools.partial(split_kernel, unit, len(parts)),
        tuple([bf16(unit, 128)] * (wire - 1) + [f32(unit, 128)]),
        [VMEM] * (2 + len(parts)),
        [pltpu.VMEM((chunk, 128), jnp.float32)],
    )(inserted, own, *parts)

    received = [to_wire(s, k + 1) for k, s in enumerate(sends)]
    scale = 1.0 / math.sqrt(float(drift * wire * slots))
    summed = call(functools.partial(sum_kernel, scale), bf16(unit, 128), [VMEM] * (3 + wire))(
        inner_done, *hb_slabs, own, *received
    )
    pieces = [summed] + [to_wire(summed, k) for k in range(1, wire)]
    mine = call(functools.partial(joined_kernel, unit), bf16(chunk, 128), [VMEM] * wire)(*pieces)
    output, grad_features, passed = call(
        second_kernel,
        (bf16(slots, 128), bf16(slots, 128), bf16(chunk, 128)),
        [SMEM] * 2 + [VMEM] * 7,
        [edge_window, pltpu.VMEM((ROWS, 128), jnp.float32), pltpu.VMEM((TAPS, 128, 128), jnp.bfloat16)],
    )(send_lists, counts, inner, *hb_slabs, full, live, weights, mine)
    if four:
        brought = {"own": mine, "first": to_chip(mine, "first"), "second": to_chip(passed, "second")}
        brought["opposite"] = to_chip(brought["first"], "second")
        early = [
            [("own", True), ("own", False), ("first", True)],
            [("second", True), ("first", False), ("second", False)],
        ]
        last = "opposite"
    else:
        brought = {k: to_chip(passed if k > 1 else mine, k) if k else mine for k in range(chips)}
        last = chips - 1
        early = [[(k, True) for k in range(last)] + [(k, False) for k in range(last)]]
    late = [[(last, True)], [(last, False)]]
    swapped = {kind: swap_core(value) for kind, value in brought.items() if kind != last}
    grads = ()
    for n, items in enumerate(early + late):
        if n == len(early):
            held = call(relay_kernel, bf16(*brought[last].shape), [VMEM] * 2)(done, brought[last])
            swapped[last] = swap_core(held)
        values = [(brought if own_core else swapped)[kind] for kind, own_core in items]
        staged = sum(value.shape[0] for value in values) // CHANNELS
        want_done = n == len(early) - 1
        *grads, done = (
            *call(
                functools.partial(final_kernel, items, blocks, want_done),
                (f32(TAPS, 128, 128), f32(TAPS, 128, 128)) + (token,) * want_done,
                [VMEM] * len(items) + [HBM] * len(grads),
                [pltpu.VMEM((staged, 128, 128), jnp.float32), pltpu.SemaphoreType.DMA((staged,))],
                50 * 10**9,
                (HBM, HBM) + (VMEM,) * want_done,
                {len(items): 0, len(items) + 1: 1} if grads else {},
            )(*values, *grads),
            *(() if want_done else (None,)),
        )
    grad_first, grad_second = grads
    return output[None, None], grad_features[None, None], grad_first, grad_second


def solution(mesh):
    placed = (
        P("drift", "wire", None, None),
        P(),
        P(),
        P("drift", "wire", None, None),
        P("drift", "wire"),
        P("drift", "wire", None, None),
        P("drift", "wire", None),
    )
    return jax.shard_map(
        on_device,
        mesh=mesh,
        in_specs=placed,
        out_specs=(P("drift", "wire", None, None), P("drift", "wire", None, None), P(), P()),
        check_vma=False,
    )
```

```python
import functools
import math

import jax
import jax.numpy as jnp
from jax import lax
from jax.experimental import pallas as pl
from jax.experimental.pallas import tpu as pltpu
from jax.sharding import PartitionSpec as P

BX = 3
BW = 3
NX = 4 * BX
NY = 4 * BW
J = 16
PLANE = NX * J
WIDE = (NX + 2) * J
ROWS = 4 * PLANE
FACE = 4 * NX
SLAB = 4 * J
CHANNELS = 128
TAPS = 27
VMEM = pl.BlockSpec(memory_space=pltpu.VMEM)
HBM = pl.BlockSpec(memory_space=pltpu.HBM)
SMEM = pl.BlockSpec(memory_space=pltpu.SMEM)
LISTED = {0: 0, 1: 1, 2: 2, 3: 7, 5: 10, 6: 3, 7: 4, 8: 5}


def call(kernel, out_shape, in_specs, scratch=(), flops=0, out_spec=VMEM, aliases={}, vmem=40):
    return pl.pallas_call(
        kernel,
        out_shape=out_shape,
        in_specs=in_specs,
        out_specs=out_spec if isinstance(out_spec, tuple) else jax.tree.map(lambda _: out_spec, out_shape),
        scratch_shapes=list(scratch),
        input_output_aliases=aliases,
        compiler_params=pltpu.CompilerParams(vmem_limit_bytes=vmem * 1024 * 1024),
        cost_estimate=pl.CostEstimate(
            flops=flops, bytes_accessed=0, transcendentals=0
        ),
    )


def bf16(*shape):
    return jax.ShapeDtypeStruct(shape, jnp.bfloat16)


def f32(*shape):
    return jax.ShapeDtypeStruct(shape, jnp.float32)


def iota(shape, dim):
    return lax.broadcasted_iota(jnp.int32, shape, dim)


def position_slots(listed, count):
    slots = {p: listed(i) for p, i in LISTED.items()}
    present = {p: (s < 9).astype(jnp.int32) for p, s in slots.items()}
    before = present[0] + present[1] + present[2] + present[3]
    others = before + present[5] + present[6] + present[7] + present[8]
    slots[4] = jnp.where(count > others, before, 9)
    return slots


def slot_rows(slots, z, x, y, valid):
    position = (x >> 2) * BW + (y >> 2)
    slot = jnp.full(position.shape, 9, jnp.int32)
    for p, s in slots.items():
        slot = jnp.where(position == p, s, slot)
    row = slot * 64 + (x & 3) * 16 + (y & 3) * 4 + z
    return jnp.where(valid & (slot < 9), row, -1)


def one_hot(rows, width):
    lane = iota(rows.shape, 1)
    parts = [jnp.where(rows == lane + 128 * c, 1.0, 0.0).astype(jnp.bfloat16) for c in range(width // 128)]
    return jnp.concatenate(parts, axis=1)


def dot(a, b):
    return jnp.dot(a, b, preferred_element_type=jnp.float32)


def grid_indices():
    shape = (4, NX, J, 128)
    z, x, j = (iota(shape, d).reshape(ROWS, 128) for d in range(3))
    return z, x, j


def face_indices():
    r = iota((FACE, 128), 0)
    z = (r >= NX).astype(jnp.int32) + (r >= 2 * NX) + (r >= 3 * NX)
    return z, r - NX * z


def write_by_parity(axis, low, high, first, second):
    even = lax.axis_index(axis) % 2 == 0
    first[...] = jnp.where(even, high, low)
    second[...] = jnp.where(even, low, high)


def read_by_parity(axis, first, second):
    me, count = lax.axis_index(axis), lax.axis_size(axis)
    even = me % 2 == 0
    a, b = first[...], second[...]
    nothing = jnp.zeros_like(a)
    low = jnp.where(me > 0, jnp.where(even, b, a), nothing)
    high = jnp.where(me < count - 1, jnp.where(even, a, b), nothing)
    return low, high


def place_kernel(counts, lists, pair, first, second, out, live, both):
    count = pair.shape[0]
    both[0:count, :] = pair[...]
    both[count:, :] = jnp.zeros((both.shape[0] - count, 256), jnp.bfloat16)
    entries = lists[0]

    def entry(i):
        return jnp.sum(jnp.where(iota(entries.shape, 1) == i, entries, 0), axis=1, keepdims=True)

    slots = position_slots(entry, counts[...])
    z, x = face_indices()
    low, high = (
        dot(
            one_hot(slot_rows(slots, z, x, jnp.full_like(x, y), x >= 0), both.shape[0]), both[...]
        ).astype(jnp.bfloat16)
        for y in (0, NY - 1)
    )
    write_by_parity("wire", low, high, first, second)
    z, x, j = grid_indices()
    rows = slot_rows(slots, z, x, j - 1, (j >= 1) & (j <= NY))
    live[...] = (rows >= 0).astype(jnp.bfloat16)
    out[...] = dot(one_hot(rows, both.shape[0]), both[...]).astype(jnp.bfloat16)


def insert_faces(placed, got_first, got_second, out, slab_first, slab_second, faces):
    low, high = read_by_parity("wire", got_first, got_second)
    faces[0:FACE, :] = low
    faces[FACE : 2 * FACE, :] = high
    faces[2 * FACE :, :] = jnp.zeros((faces.shape[0] - 2 * FACE, 256), jnp.bfloat16)
    z, x, j = grid_indices()
    rows = z * NX + x
    rows = jnp.where(j == 0, rows, jnp.where(j == NY + 1, rows + FACE, -1))
    full = (placed[...].astype(jnp.float32) + dot(one_hot(rows, 128), faces[...])).astype(jnp.bfloat16)
    out[...] = full
    low = jnp.concatenate([full[z * PLANE : z * PLANE + J, :] for z in range(4)], axis=0)
    high = jnp.concatenate([full[(z + 1) * PLANE - J : (z + 1) * PLANE, :] for z in range(4)], axis=0)
    write_by_parity("drift", low, high, slab_first, slab_second)


def build_window(window, base, plane_of):
    for zi in range(4):
        plane = plane_of(zi)
        wide = plane.astype(jnp.float32)
        before = pltpu.roll(wide, 1, 0).astype(jnp.bfloat16)
        after = pltpu.roll(wide, plane.shape[0] - 1, 0).astype(jnp.bfloat16)
        for oy, shifted in enumerate((before, plane, after)):
            for z in range(max(0, zi - 1), min(3, zi + 1) + 1):
                lane = 128 * (3 * oy + zi - z + 1)
                window[base + z, :, lane : lane + 128] = shifted
    empty = jnp.zeros((plane.shape[0], 128), jnp.bfloat16)
    for oy in range(3):
        window[base, :, 384 * oy : 384 * oy + 128] = empty
        window[base + 3, :, 384 * oy + 256 : 384 * oy + 384] = empty


def wide_plane(full, low, high, z, lanes):
    return jnp.concatenate(
        [
            low[z * J : (z + 1) * J, lanes],
            full[z * PLANE : (z + 1) * PLANE, lanes],
            high[z * J : (z + 1) * J, lanes],
        ],
        axis=0,
    )


def conv(window, weights, base):
    total = None
    for ox in range(3):
        rows = window[:, ox * J : ox * J + PLANE, :].reshape(ROWS, 1152)
        term = dot(rows, weights[base + 9 * ox : base + 9 * (ox + 1)].reshape(1152, 128))
        total = term if total is None else total + term
    return total


def flip_blocks(weights, base, flipped):
    for k in range(TAPS):
        flipped[:, 128 * k : 128 * (k + 1)] = weights[base + TAPS - 1 - k]


def conv_flipped(window, flipped):
    total = None
    for ox in range(3):
        rows = window[:, ox * J : ox * J + PLANE, :].reshape(ROWS, 1152)
        term = lax.dot_general(
            rows,
            flipped[:, 1152 * ox : 1152 * (ox + 1)],
            (((1,), (1,)), ((), ())),
            preferred_element_type=jnp.float32,
        )
        total = term if total is None else total + term
    return total


def inner_kernel(full, weights, pre, window):
    edge = jnp.zeros((SLAB, 128), jnp.bfloat16)
    build_window(window, 0, lambda z: wide_plane(full, edge, edge, z, slice(0, 128)))
    pre[...] = conv(window, weights, 0)


def add_edges(pre, low, high, weights, edge_window):
    for ox, x, slab in ((0, 0, low), (2, NX - 1, high)):
        build_window(edge_window, 0, lambda z: slab[z * J : (z + 1) * J, :])
        taps = weights[9 * ox : 9 * (ox + 1)].reshape(1152, 128)
        term = dot(edge_window[...].reshape(SLAB, 1152), taps)
        for z in range(4):
            start = z * PLANE + x * J
            pre[start : start + J, :] += term[z * J : (z + 1) * J, :]


def first_kernel(full, got_first, got_second, live, weights, inner, hb, keep, send, window, flipped, edge_window, pre):
    f_lanes, g_lanes = slice(0, 128), slice(128, 256)
    low, high = read_by_parity("drift", got_first, got_second)
    alive = live[...].astype(jnp.float32)
    flip_blocks(weights, TAPS, flipped)
    pre[...] = inner[...]
    add_edges(pre, low[:, f_lanes], high[:, f_lanes], weights, edge_window)
    first_pre = pre[...]
    gate = jax.nn.sigmoid(first_pre)
    hidden = (alive * (first_pre * gate)).astype(jnp.bfloat16)
    slope = alive * (gate * (1.0 + first_pre * (1.0 - gate)))
    build_window(window, 0, lambda z: wide_plane(full, low, high, z, g_lanes))
    back = (conv_flipped(window, flipped) * slope).astype(jnp.bfloat16)
    hb[...] = jnp.concatenate([hidden, back], axis=1)
    core = lax.axis_index("drift") % 2

    def write(to, values, lanes):
        to[0:ROWS, :] = values
        for z in range(4):
            start = ROWS + z * WIDE
            to[start : start + WIDE, :] = wide_plane(full, low, high, z, lanes)

    @pl.when(core == 0)
    def _():
        write(keep, hidden, g_lanes)
        write(send, back, f_lanes)

    @pl.when(core != 0)
    def _():
        write(keep, back, f_lanes)
        write(send, hidden, g_lanes)


def chip_mask(kind, core):
    if isinstance(kind, int):
        return kind
    first = 1 + core
    return {"own": 0, "first": first, "second": 3 - first, "opposite": 3}[kind]


def left_rows(part):
    return part[0:ROWS, :].astype(jnp.float32).T.astype(jnp.bfloat16)


def term_planes(part):
    return lambda z: part[ROWS + z * WIDE : ROWS + (z + 1) * WIDE, :]


def add_terms(left, window, add_block):
    for ox in range(3):
        shifted = window[:, ox * J : ox * J + PLANE, :].reshape(ROWS, 1152)
        product = dot(left, shifted)
        for k in range(9):
            add_block(128 * (9 * ox + k), product[:, 128 * k : 128 * (k + 1)])


def own_terms_kernel(mine, total, window):
    rows = TAPS * CHANNELS
    if total.shape[0] > rows:
        total[rows:, :] = jnp.zeros((total.shape[0] - rows, 128), jnp.float32)
    build_window(window, 0, term_planes(mine))

    def put(start, block):
        total[start : start + 128, :] = block

    add_terms(left_rows(mine), window, put)


def lead_terms_kernel(blocks, kind, mine, theirs, out, left, window):
    build_window(window, 0, term_planes(theirs))
    left[...] = left_rows(theirs)
    me, core = lax.axis_index("drift") // 2, lax.axis_index("drift") % 2
    lead = (me ^ chip_mask(kind, core)) * blocks
    columns = []
    for i in range(blocks):
        tap = jnp.minimum(lead + i, TAPS - 1)
        row = pl.multiple_of(tap // 9 * J, J)
        lane = pl.multiple_of(tap % 9 * 128, 128)
        columns.append(window[:, pl.ds(row, PLANE), pl.ds(lane, 128)].reshape(ROWS, 128))
    product = dot(left[...], jnp.concatenate(columns, axis=1))
    for i in range(blocks):
        held = mine[pl.ds(pl.multiple_of((lead + i) * 128, 128), 128), :]
        term = product[:, 128 * i : 128 * (i + 1)]
        out[128 * i : 128 * (i + 1), :] = (held + jnp.where(lead + i < TAPS, term, 0.0)).astype(out.dtype)


def terms_kernel(chunk, kinds, mine, left, window, hb, *refs):
    *outs, first, second, total = refs
    rows = TAPS * CHANNELS
    if total.shape[0] > rows:
        total[rows:, :] = mine[rows:, :]

    def put(start, block):
        total[start : start + 128, :] = mine[start : start + 128, :] + block

    add_terms(left[...], window, put)
    me, core = lax.axis_index("drift") // 2, lax.axis_index("drift") % 2
    for kind, out in zip(kinds, outs):
        start = pl.multiple_of((me ^ chip_mask(kind, core)) * chunk, 128)
        out[...] = total[pl.ds(start, chunk), :].astype(out.dtype)
    z, x = face_indices()
    start = z * PLANE + x * J
    low, high = (dot(one_hot(start + j, ROWS), hb[...]).astype(jnp.bfloat16) for j in (1, NY))
    write_by_parity("wire", low, high, first, second)


def passed_on_kernel(partial, received, out):
    out[...] = (partial[...] + received[...].astype(jnp.float32)).astype(jnp.bfloat16)


def relay_kernel(after, value, out):
    out[...] = value[...]


def split_kernel(unit, count, after, own, *refs):
    received, (*sends, rest, total) = refs[:count], refs[count:]
    summed = own[...]
    for part in received:
        summed = summed + part[...].astype(jnp.float32)
    total[...] = summed
    me = lax.axis_index("wire")
    rest[...] = total[pl.ds(pl.multiple_of(me * unit, 16), unit), :]
    for step, out in enumerate(sends):
        start = pl.multiple_of((me ^ (step + 1)) * unit, 16)
        out[...] = total[pl.ds(start, unit), :].astype(jnp.bfloat16)


def sum_kernel(scale, after_inner, after_first, after_second, own, *refs):
    *received, out = refs
    summed = own[...]
    for part in received:
        summed = summed + part[...].astype(jnp.float32)
    out[...] = (summed * scale).astype(jnp.bfloat16)


def joined_kernel(unit, after, *refs):
    *parts, out = refs
    me = lax.axis_index("wire")
    for step, part in enumerate(parts):
        start = pl.multiple_of((me ^ step) * unit, 16)
        out[pl.ds(start, unit), :] = part[...]


def final_kernel(items, blocks, want_done, *refs):
    parts = refs[: len(items)]
    first, second, *done, staged, sems = refs[len(refs) - 4 - want_done :]
    me = lax.axis_index("drift") // 2
    for ref in done:
        ref[...] = jnp.zeros_like(ref)

    def write(core):
        copies = []
        for part, (kind, mine) in zip(parts, items):
            source = core if mine else 1 - core
            value = part[...].astype(jnp.float32)
            count, here = part.shape[0] // 128, len(copies)
            for i in range(count):
                block = value[128 * i : 128 * (i + 1), :]
                staged[here + i] = block.T if source else block
            chunk = me ^ chip_mask(kind, source)
            for i in range(count):
                tap = chunk * blocks + i
                safe = jnp.minimum(tap, TAPS - 1)
                to = first.at[safe] if source else second.at[TAPS - 1 - safe]
                copies.append((tap < TAPS, pltpu.make_async_copy(staged.at[here + i], to, sems.at[here + i])))
                pl.when(copies[-1][0])(copies[-1][1].start)
        for used, copy in copies:
            pl.when(used)(copy.wait)

    even = lax.axis_index("drift") % 2 == 0
    pl.when(even)(lambda: write(0))
    pl.when(jnp.logical_not(even))(lambda: write(1))


def second_inner_kernel(field, hb, weights, inner, done, window, *flipped):
    edge = jnp.zeros((SLAB, 256), jnp.bfloat16)
    build_window(window, 0, lambda z: wide_plane(hb, edge, edge, z, slice(128 * field, 128 * (field + 1))))
    if field:
        flip_blocks(weights, 0, *flipped)
        inner[...] = conv_flipped(window, *flipped)
    else:
        inner[...] = conv(window, weights, TAPS)
    done[...] = jnp.zeros_like(done)


def second_kernel(
    lists, counts, inner_hidden, inner_back, got_first, got_second, base, live, weights, held, output, grad, passed, edge_window, pre, taps
):
    low, high = read_by_parity("drift", got_first, got_second)
    results = []
    for field in (0, 1):
        lanes = slice(128 * field, 128 * (field + 1))
        pre[...] = inner_back[...] if field else inner_hidden[...]
        if field:
            for k in (*range(9), *range(18, 27)):
                taps[k] = weights[TAPS - 1 - k].astype(jnp.float32).T.astype(jnp.bfloat16)
            add_edges(pre, low[:, lanes], high[:, lanes], taps, edge_window)
        else:
            add_edges(pre, low[:, lanes], high[:, lanes], weights.at[TAPS:], edge_window)
        value = base[:, lanes].astype(jnp.float32) + pre[...]
        results.append((live[...].astype(jnp.float32) * value).astype(jnp.bfloat16))
    both = jnp.concatenate(results, axis=1)
    slots = position_slots(lambda i: lists[0, 0, i], counts[0, 0])
    count = output.shape[0]
    pieces = []
    row = iota((count, 128), 0)
    for c in range(ROWS // 128):
        col = iota((8, 128), 1) + 128 * c
        z = (col >= PLANE).astype(jnp.int32) + (col >= 2 * PLANE) + (col >= 3 * PLANE)
        rest = col - PLANE * z
        x, j = rest >> 4, rest & 15
        source = slot_rows(slots, z, x, j - 1, (j >= 1) & (j <= NY))
        source = jnp.broadcast_to(source[0:1, :], (count, 128))
        pieces.append(jnp.where(row == source, 1.0, 0.0).astype(jnp.bfloat16))
    by_slot = dot(jnp.concatenate(pieces, axis=1), both).astype(jnp.bfloat16)
    output[...] = by_slot[:, 0:128]
    grad[...] = by_slot[:, 128:256]
    passed[...] = held[...]


def pairs(value_first, value_second, axis):
    drift, wire = lax.axis_size("drift"), lax.axis_size("wire")
    count = lax.axis_size(axis)
    first = [(i, i ^ 1) for i in range(count) if i ^ 1 < count]
    second = {i: i + 1 if i % 2 else i - 1 for i in range(1, count - 1)}
    if axis == "drift":
        second.update({0: count - 1, count - 1: 0})
        got_second = lax.ppermute(value_second, axis, sorted(second.items()))
    else:
        moves = [
            (d * wire + w, d * wire + second[w] if w in second else (d ^ 1) * wire + w)
            for d in range(drift)
            for w in range(wire)
        ]
        got_second = lax.ppermute(value_second, ("drift", "wire"), moves)
    got_first = lax.ppermute(value_first, axis, first)
    return got_first, got_second


def on_device(features, first_weight, second_weight, cotangent, counts, kernel_map, send_lists):
    drift, wire = lax.axis_size("drift"), lax.axis_size("wire")
    chips = drift // 2
    blocks = -(-TAPS // chips)
    chunk = blocks * CHANNELS
    unit = chunk // wire
    rows = TAPS * CHANNELS
    f, g = features[0, 0], cotangent[0, 0]
    slots = f.shape[0]
    padded = -(-slots // 128) * 128
    conv_scratch = [pltpu.VMEM((4, WIDE, 1152), jnp.bfloat16), pltpu.VMEM((128, rows), jnp.bfloat16)]
    edge_window = pltpu.VMEM((4, J, 1152), jnp.bfloat16)
    faces_scratch = pltpu.VMEM((128, 256), jnp.bfloat16)
    face, slab, grid = bf16(FACE, 256), bf16(SLAB, 256), bf16(ROWS, 256)

    def swap_core(value):
        return lax.ppermute(value, "drift", [(i, i ^ 1) for i in range(drift)])

    def to_chip(value, kind):
        return lax.ppermute(value, "drift", [(i, i ^ (2 * chip_mask(kind, i % 2))) for i in range(drift)])

    def to_wire(value, step):
        return lax.ppermute(value, "wire", [(i, i ^ step) for i in range(wire)])

    pair = jnp.concatenate([f, g], axis=1)
    weights = jnp.concatenate([first_weight, second_weight], axis=0)
    *faces, placed, live = call(
        place_kernel,
        (face, face, grid, bf16(ROWS, 128)),
        [VMEM] * 3,
        [pltpu.VMEM((padded, 256), jnp.bfloat16)],
    )(counts, send_lists, pair)
    faces = pairs(*faces, "wire")
    full, *slabs = call(insert_faces, (grid, slab, slab), [VMEM] * 3, [faces_scratch])(placed, *faces)
    slabs = pairs(*slabs, "drift")
    message = bf16(ROWS + 4 * WIDE, 128)
    inner = call(inner_kernel, f32(ROWS, 128), [VMEM] * 2, conv_scratch[:1])(full, weights)
    hb, keep, send = call(
        first_kernel,
        (grid, message, message),
        [VMEM] * 6,
        conv_scratch + [edge_window, pltpu.VMEM((ROWS, 128), jnp.float32)],
    )(full, *slabs, live, weights, inner)
    got = swap_core(send)
    term_window = pltpu.VMEM((4, WIDE, 1152), jnp.bfloat16)
    terms = f32(chunk * chips, 128)
    own_terms = call(own_terms_kernel, terms, [VMEM], [term_window])(keep)
    four = chips == 4
    kinds = ("opposite", "first", "second", "own") if four else (*range(1, chips), 0)
    shapes = [f32(chunk, 128) if k in ("second", "own", 0) else bf16(chunk, 128) for k in kinds]
    lead, left, held_window = call(
        functools.partial(lead_terms_kernel, blocks, kinds[0]),
        (shapes[0], bf16(128, ROWS), bf16(4, WIDE, 1152)),
        [VMEM] * 2,
    )(own_terms, got)
    *sends, own, face_first, face_second = call(
        functools.partial(terms_kernel, chunk, kinds[1:]),
        (*shapes[1:], face, face),
        [VMEM] * 4,
        [pltpu.VMEM(terms.shape, jnp.float32)],
    )(own_terms, left, held_window, hb)
    sends = [lead] + sends
    if four:
        opposite, first, second_part = sends
        passed = to_chip(opposite, "first")
        parts = [to_chip(first, "first")]
        passed = call(passed_on_kernel, bf16(chunk, 128), [VMEM] * 2)(second_part, passed)
        parts.append(to_chip(passed, "second"))
    else:
        parts = [to_chip(value, k) for k, value in zip(kinds, sends)]
    faces = pairs(face_first, face_second, "wire")
    hb_full, *hb_slabs = call(insert_faces, (grid, slab, slab), [VMEM] * 3, [faces_scratch])(hb, *faces)
    inserted = hb_slabs[0]
    hb_slabs = pairs(*hb_slabs, "drift")
    token = f32(8, 128)
    (inner_hidden, hidden_done), (inner_back, back_done) = (
        call(
            functools.partial(second_inner_kernel, field),
            (f32(ROWS, 128), token),
            [VMEM] * 2,
            conv_scratch[: 1 + field],
        )(hb_full, weights)
        for field in (0, 1)
    )
    *sends, own = call(
        functools.partial(split_kernel, unit, len(parts)),
        tuple([bf16(unit, 128)] * (wire - 1) + [f32(unit, 128)]),
        [VMEM] * (2 + len(parts)),
        [pltpu.VMEM((chunk, 128), jnp.float32)],
    )(inserted, own, *parts)

    received = [to_wire(s, k + 1) for k, s in enumerate(sends)]
    scale = 1.0 / math.sqrt(float(drift * wire * slots))
    summed = call(functools.partial(sum_kernel, scale), bf16(unit, 128), [VMEM] * (3 + wire))(
        hidden_done, *hb_slabs, own, *received
    )
    pieces = [summed] + [to_wire(summed, k) for k in range(1, wire)]
    mine = call(functools.partial(joined_kernel, unit), bf16(chunk, 128), [VMEM] * (1 + wire))(back_done, *pieces)
    output, grad_features, passed = call(
        second_kernel,
        (bf16(slots, 128), bf16(slots, 128), bf16(chunk, 128)),
        [SMEM] * 2 + [VMEM] * 8,
        [edge_window, pltpu.VMEM((ROWS, 128), jnp.float32), pltpu.VMEM((TAPS, 128, 128), jnp.bfloat16)],
    )(send_lists, counts, inner_hidden, inner_back, *hb_slabs, full, live, weights, mine)
    if four:
        brought = {"own": mine, "first": to_chip(mine, "first"), "second": to_chip(passed, "second")}
        brought["opposite"] = to_chip(brought["first"], "second")
        early = [
            [("own", True), ("own", False), ("first", True)],
            [("second", True), ("first", False), ("second", False)],
        ]
        last = "opposite"
    else:
        brought = {k: to_chip(passed if k > 1 else mine, k) if k else mine for k in range(chips)}
        last = chips - 1
        early = [[(k, True) for k in range(last)] + [(k, False) for k in range(last)]]
    late = [[(last, True)], [(last, False)]]
    swapped = {kind: swap_core(value) for kind, value in brought.items() if kind != last}
    grads = ()
    for n, items in enumerate(early + late):
        if n == len(early):
            held = call(relay_kernel, bf16(*brought[last].shape), [VMEM] * 2)(done, brought[last])
            swapped[last] = swap_core(held)
        values = [(brought if own_core else swapped)[kind] for kind, own_core in items]
        staged = sum(value.shape[0] for value in values) // CHANNELS
        want_done = n == len(early) - 1
        *grads, done = (
            *call(
                functools.partial(final_kernel, items, blocks, want_done),
                (f32(TAPS, 128, 128), f32(TAPS, 128, 128)) + (token,) * want_done,
                [VMEM] * len(items) + [HBM] * len(grads),
                [pltpu.VMEM((staged, 128, 128), jnp.float32), pltpu.SemaphoreType.DMA((staged,))],
                50 * 10**9,
                (HBM, HBM) + (VMEM,) * want_done,
                {len(items): 0, len(items) + 1: 1} if grads else {},
            )(*values, *grads),
            *(() if want_done else (None,)),
        )
    grad_first, grad_second = grads
    return output[None, None], grad_features[None, None], grad_first, grad_second


def solution(mesh):
    placed = (
        P("drift", "wire", None, None),
        P(),
        P(),
        P("drift", "wire", None, None),
        P("drift", "wire"),
        P("drift", "wire", None, None),
        P("drift", "wire", None),
    )
    return jax.shard_map(
        on_device,
        mesh=mesh,
        in_specs=placed,
        out_specs=(P("drift", "wire", None, None), P("drift", "wire", None, None), P(), P()),
        check_vma=False,
    )
```

```python
import functools
import math

import jax
import jax.numpy as jnp
from jax import lax
from jax.experimental import pallas as pl
from jax.experimental.pallas import tpu as pltpu
from jax.sharding import PartitionSpec as P

BX = 3
BW = 3
NX = 4 * BX
NY = 4 * BW
J = 16
PLANE = NX * J
WIDE = (NX + 2) * J
ROWS = 4 * PLANE
FACE = 4 * NX
SLAB = 4 * J
CHANNELS = 128
TAPS = 27
VMEM = pl.BlockSpec(memory_space=pltpu.VMEM)
HBM = pl.BlockSpec(memory_space=pltpu.HBM)
SMEM = pl.BlockSpec(memory_space=pltpu.SMEM)
LISTED = {0: 0, 1: 1, 2: 2, 3: 7, 5: 10, 6: 3, 7: 4, 8: 5}


def call(kernel, out_shape, in_specs, scratch=(), flops=0, out_spec=VMEM, aliases={}, vmem=40):
    return pl.pallas_call(
        kernel,
        out_shape=out_shape,
        in_specs=in_specs,
        out_specs=out_spec if isinstance(out_spec, tuple) else jax.tree.map(lambda _: out_spec, out_shape),
        scratch_shapes=list(scratch),
        input_output_aliases=aliases,
        compiler_params=pltpu.CompilerParams(vmem_limit_bytes=vmem * 1024 * 1024),
        cost_estimate=pl.CostEstimate(
            flops=flops, bytes_accessed=0, transcendentals=0
        ),
    )


def bf16(*shape):
    return jax.ShapeDtypeStruct(shape, jnp.bfloat16)


def f32(*shape):
    return jax.ShapeDtypeStruct(shape, jnp.float32)


def iota(shape, dim):
    return lax.broadcasted_iota(jnp.int32, shape, dim)


def position_slots(listed, count):
    slots = {p: listed(i) for p, i in LISTED.items()}
    present = {p: (s < 9).astype(jnp.int32) for p, s in slots.items()}
    before = present[0] + present[1] + present[2] + present[3]
    others = before + present[5] + present[6] + present[7] + present[8]
    slots[4] = jnp.where(count > others, before, 9)
    return slots


def slot_rows(slots, z, x, y, valid):
    position = (x >> 2) * BW + (y >> 2)
    slot = jnp.full(position.shape, 9, jnp.int32)
    for p, s in slots.items():
        slot = jnp.where(position == p, s, slot)
    row = slot * 64 + (x & 3) * 16 + (y & 3) * 4 + z
    return jnp.where(valid & (slot < 9), row, -1)


def one_hot(rows, width):
    lane = iota(rows.shape, 1)
    parts = [jnp.where(rows == lane + 128 * c, 1.0, 0.0).astype(jnp.bfloat16) for c in range(width // 128)]
    return jnp.concatenate(parts, axis=1)


def dot(a, b):
    return jnp.dot(a, b, preferred_element_type=jnp.float32)


def grid_indices():
    shape = (4, NX, J, 128)
    z, x, j = (iota(shape, d).reshape(ROWS, 128) for d in range(3))
    return z, x, j


def face_indices():
    r = iota((FACE, 128), 0)
    z = (r >= NX).astype(jnp.int32) + (r >= 2 * NX) + (r >= 3 * NX)
    return z, r - NX * z


def write_by_parity(axis, low, high, first, second):
    even = lax.axis_index(axis) % 2 == 0
    first[...] = jnp.where(even, high, low)
    second[...] = jnp.where(even, low, high)


def read_by_parity(axis, first, second):
    me, count = lax.axis_index(axis), lax.axis_size(axis)
    even = me % 2 == 0
    a, b = first[...], second[...]
    nothing = jnp.zeros_like(a)
    low = jnp.where(me > 0, jnp.where(even, b, a), nothing)
    high = jnp.where(me < count - 1, jnp.where(even, a, b), nothing)
    return low, high


def place_kernel(counts, lists, pair, first, second, out, live, both):
    count = pair.shape[0]
    both[0:count, :] = pair[...]
    both[count:, :] = jnp.zeros((both.shape[0] - count, 256), jnp.bfloat16)
    entries = lists[0]

    def entry(i):
        return jnp.sum(jnp.where(iota(entries.shape, 1) == i, entries, 0), axis=1, keepdims=True)

    slots = position_slots(entry, counts[...])
    z, x = face_indices()
    low, high = (
        dot(
            one_hot(slot_rows(slots, z, x, jnp.full_like(x, y), x >= 0), both.shape[0]), both[...]
        ).astype(jnp.bfloat16)
        for y in (0, NY - 1)
    )
    write_by_parity("wire", low, high, first, second)
    z, x, j = grid_indices()
    rows = slot_rows(slots, z, x, j - 1, (j >= 1) & (j <= NY))
    live[...] = (rows >= 0).astype(jnp.bfloat16)
    out[...] = dot(one_hot(rows, both.shape[0]), both[...]).astype(jnp.bfloat16)


def insert_faces(placed, got_first, got_second, out, slab_first, slab_second, faces):
    low, high = read_by_parity("wire", got_first, got_second)
    faces[0:FACE, :] = low
    faces[FACE : 2 * FACE, :] = high
    faces[2 * FACE :, :] = jnp.zeros((faces.shape[0] - 2 * FACE, 256), jnp.bfloat16)
    z, x, j = grid_indices()
    rows = z * NX + x
    rows = jnp.where(j == 0, rows, jnp.where(j == NY + 1, rows + FACE, -1))
    full = (placed[...].astype(jnp.float32) + dot(one_hot(rows, 128), faces[...])).astype(jnp.bfloat16)
    out[...] = full
    low = jnp.concatenate([full[z * PLANE : z * PLANE + J, :] for z in range(4)], axis=0)
    high = jnp.concatenate([full[(z + 1) * PLANE - J : (z + 1) * PLANE, :] for z in range(4)], axis=0)
    write_by_parity("drift", low, high, slab_first, slab_second)


def build_window(window, base, plane_of):
    for zi in range(4):
        plane = plane_of(zi)
        wide = plane.astype(jnp.float32)
        before = pltpu.roll(wide, 1, 0).astype(jnp.bfloat16)
        after = pltpu.roll(wide, plane.shape[0] - 1, 0).astype(jnp.bfloat16)
        for oy, shifted in enumerate((before, plane, after)):
            for z in range(max(0, zi - 1), min(3, zi + 1) + 1):
                lane = 128 * (3 * oy + zi - z + 1)
                window[base + z, :, lane : lane + 128] = shifted
    empty = jnp.zeros((plane.shape[0], 128), jnp.bfloat16)
    for oy in range(3):
        window[base, :, 384 * oy : 384 * oy + 128] = empty
        window[base + 3, :, 384 * oy + 256 : 384 * oy + 384] = empty


def wide_plane(full, low, high, z, lanes):
    return jnp.concatenate(
        [
            low[z * J : (z + 1) * J, lanes],
            full[z * PLANE : (z + 1) * PLANE, lanes],
            high[z * J : (z + 1) * J, lanes],
        ],
        axis=0,
    )


def conv(window, weights, base):
    total = None
    for ox in range(3):
        rows = window[:, ox * J : ox * J + PLANE, :].reshape(ROWS, 1152)
        term = dot(rows, weights[base + 9 * ox : base + 9 * (ox + 1)].reshape(1152, 128))
        total = term if total is None else total + term
    return total


def flip_blocks(weights, base, flipped):
    for k in range(TAPS):
        flipped[:, 128 * k : 128 * (k + 1)] = weights[base + TAPS - 1 - k]


def conv_flipped(window, flipped):
    total = None
    for ox in range(3):
        rows = window[:, ox * J : ox * J + PLANE, :].reshape(ROWS, 1152)
        term = lax.dot_general(
            rows,
            flipped[:, 1152 * ox : 1152 * (ox + 1)],
            (((1,), (1,)), ((), ())),
            preferred_element_type=jnp.float32,
        )
        total = term if total is None else total + term
    return total


def inner_kernel(full, weights, pre, window):
    edge = jnp.zeros((SLAB, 128), jnp.bfloat16)
    build_window(window, 0, lambda z: wide_plane(full, edge, edge, z, slice(0, 128)))
    pre[...] = conv(window, weights, 0)


def add_edges(pre, low, high, weights, edge_window):
    for ox, x, slab in ((0, 0, low), (2, NX - 1, high)):
        build_window(edge_window, 0, lambda z: slab[z * J : (z + 1) * J, :])
        taps = weights[9 * ox : 9 * (ox + 1)].reshape(1152, 128)
        term = dot(edge_window[...].reshape(SLAB, 1152), taps)
        for z in range(4):
            start = z * PLANE + x * J
            pre[start : start + J, :] += term[z * J : (z + 1) * J, :]


def first_kernel(full, got_first, got_second, live, weights, inner, hb, keep, send, window, flipped, edge_window, pre):
    f_lanes, g_lanes = slice(0, 128), slice(128, 256)
    low, high = read_by_parity("drift", got_first, got_second)
    alive = live[...].astype(jnp.float32)
    flip_blocks(weights, TAPS, flipped)
    pre[...] = inner[...]
    add_edges(pre, low[:, f_lanes], high[:, f_lanes], weights, edge_window)
    first_pre = pre[...]
    gate = jax.nn.sigmoid(first_pre)
    hidden = (alive * (first_pre * gate)).astype(jnp.bfloat16)
    slope = alive * (gate * (1.0 + first_pre * (1.0 - gate)))
    build_window(window, 0, lambda z: wide_plane(full, low, high, z, g_lanes))
    back = (conv_flipped(window, flipped) * slope).astype(jnp.bfloat16)
    hb[...] = jnp.concatenate([hidden, back], axis=1)
    core = lax.axis_index("drift") % 2

    def write(to, values, lanes):
        to[0:ROWS, :] = values
        for z in range(4):
            start = ROWS + z * WIDE
            to[start : start + WIDE, :] = wide_plane(full, low, high, z, lanes)

    @pl.when(core == 0)
    def _():
        write(keep, hidden, g_lanes)
        write(send, back, f_lanes)

    @pl.when(core != 0)
    def _():
        write(keep, back, f_lanes)
        write(send, hidden, g_lanes)


def chip_mask(kind, core):
    if isinstance(kind, int):
        return kind
    first = 1 + core
    return {"own": 0, "first": first, "second": 3 - first, "opposite": 3}[kind]


def left_rows(part):
    return part[0:ROWS, :].astype(jnp.float32).T.astype(jnp.bfloat16)


def term_planes(part):
    return lambda z: part[ROWS + z * WIDE : ROWS + (z + 1) * WIDE, :]


def add_terms(left, window, add_block):
    for ox in range(3):
        shifted = window[:, ox * J : ox * J + PLANE, :].reshape(ROWS, 1152)
        product = dot(left, shifted)
        for k in range(9):
            add_block(128 * (9 * ox + k), product[:, 128 * k : 128 * (k + 1)])


def own_terms_kernel(mine, total, window):
    rows = TAPS * CHANNELS
    if total.shape[0] > rows:
        total[rows:, :] = jnp.zeros((total.shape[0] - rows, 128), jnp.float32)
    build_window(window, 0, term_planes(mine))

    def put(start, block):
        total[start : start + 128, :] = block

    add_terms(left_rows(mine), window, put)


def lead_terms_kernel(blocks, kind, mine, theirs, out, left, window):
    build_window(window, 0, term_planes(theirs))
    left[...] = left_rows(theirs)
    me, core = lax.axis_index("drift") // 2, lax.axis_index("drift") % 2
    lead = (me ^ chip_mask(kind, core)) * blocks
    columns = []
    for i in range(blocks):
        tap = jnp.minimum(lead + i, TAPS - 1)
        row = pl.multiple_of(tap // 9 * J, J)
        lane = pl.multiple_of(tap % 9 * 128, 128)
        columns.append(window[:, pl.ds(row, PLANE), pl.ds(lane, 128)].reshape(ROWS, 128))
    product = dot(left[...], jnp.concatenate(columns, axis=1))
    for i in range(blocks):
        held = mine[pl.ds(pl.multiple_of((lead + i) * 128, 128), 128), :]
        term = product[:, 128 * i : 128 * (i + 1)]
        out[128 * i : 128 * (i + 1), :] = (held + jnp.where(lead + i < TAPS, term, 0.0)).astype(out.dtype)


def terms_kernel(chunk, kinds, mine, left, window, hb, *refs):
    *outs, first, second, total = refs
    rows = TAPS * CHANNELS
    if total.shape[0] > rows:
        total[rows:, :] = mine[rows:, :]

    def put(start, block):
        total[start : start + 128, :] = mine[start : start + 128, :] + block

    add_terms(left[...], window, put)
    me, core = lax.axis_index("drift") // 2, lax.axis_index("drift") % 2
    for kind, out in zip(kinds, outs):
        start = pl.multiple_of((me ^ chip_mask(kind, core)) * chunk, 128)
        out[...] = total[pl.ds(start, chunk), :].astype(out.dtype)
    z, x = face_indices()
    start = z * PLANE + x * J
    low, high = (dot(one_hot(start + j, ROWS), hb[...]).astype(jnp.bfloat16) for j in (1, NY))
    write_by_parity("wire", low, high, first, second)


def passed_on_kernel(partial, received, out):
    out[...] = (partial[...] + received[...].astype(jnp.float32)).astype(jnp.bfloat16)


def relay_kernel(after, value, out):
    out[...] = value[...]


def split_kernel(unit, count, after, own, *refs):
    received, (*sends, rest, total) = refs[:count], refs[count:]
    summed = own[...]
    for part in received:
        summed = summed + part[...].astype(jnp.float32)
    total[...] = summed
    me = lax.axis_index("wire")
    rest[...] = total[pl.ds(pl.multiple_of(me * unit, 16), unit), :]
    for step, out in enumerate(sends):
        start = pl.multiple_of((me ^ (step + 1)) * unit, 16)
        out[...] = total[pl.ds(start, unit), :].astype(jnp.bfloat16)


def sum_kernel(scale, after, own, *refs):
    *received, out = refs
    summed = own[...]
    for part in received:
        summed = summed + part[...].astype(jnp.float32)
    out[...] = (summed * scale).astype(jnp.bfloat16)


def joined_kernel(unit, after, *refs):
    *parts, out = refs
    me = lax.axis_index("wire")
    for step, part in enumerate(parts):
        start = pl.multiple_of((me ^ step) * unit, 16)
        out[pl.ds(start, unit), :] = part[...]


def final_kernel(items, blocks, want_done, *refs):
    parts = refs[: len(items)]
    first, second, *done, staged, sems = refs[len(refs) - 4 - want_done :]
    me = lax.axis_index("drift") // 2
    for ref in done:
        ref[...] = jnp.zeros_like(ref)

    def write(core):
        copies = []
        for part, (kind, mine) in zip(parts, items):
            source = core if mine else 1 - core
            value = part[...].astype(jnp.float32)
            count, here = part.shape[0] // 128, len(copies)
            for i in range(count):
                block = value[128 * i : 128 * (i + 1), :]
                staged[here + i] = block.T if source else block
            chunk = me ^ chip_mask(kind, source)
            for i in range(count):
                tap = chunk * blocks + i
                safe = jnp.minimum(tap, TAPS - 1)
                to = first.at[safe] if source else second.at[TAPS - 1 - safe]
                copies.append((tap < TAPS, pltpu.make_async_copy(staged.at[here + i], to, sems.at[here + i])))
                pl.when(copies[-1][0])(copies[-1][1].start)
        for used, copy in copies:
            pl.when(used)(copy.wait)

    even = lax.axis_index("drift") % 2 == 0
    pl.when(even)(lambda: write(0))
    pl.when(jnp.logical_not(even))(lambda: write(1))


def second_inner_kernel(field, hb, weights, inner, done, window, *flipped):
    edge = jnp.zeros((SLAB, 256), jnp.bfloat16)
    build_window(window, 0, lambda z: wide_plane(hb, edge, edge, z, slice(128 * field, 128 * (field + 1))))
    if field:
        flip_blocks(weights, 0, *flipped)
        inner[...] = conv_flipped(window, *flipped)
    else:
        inner[...] = conv(window, weights, TAPS)
    done[...] = jnp.zeros_like(done)


def second_kernel(
    lists, counts, inner_hidden, inner_back, got_first, got_second, base, live, weights, held, output, grad, passed, edge_window, pre, taps
):
    low, high = read_by_parity("drift", got_first, got_second)
    results = []
    for field in (0, 1):
        lanes = slice(128 * field, 128 * (field + 1))
        pre[...] = inner_back[...] if field else inner_hidden[...]
        if field:
            for k in (*range(9), *range(18, 27)):
                taps[k] = weights[TAPS - 1 - k].astype(jnp.float32).T.astype(jnp.bfloat16)
            add_edges(pre, low[:, lanes], high[:, lanes], taps, edge_window)
        else:
            add_edges(pre, low[:, lanes], high[:, lanes], weights.at[TAPS:], edge_window)
        value = base[:, lanes].astype(jnp.float32) + pre[...]
        results.append((live[...].astype(jnp.float32) * value).astype(jnp.bfloat16))
    both = jnp.concatenate(results, axis=1)
    slots = position_slots(lambda i: lists[0, 0, i], counts[0, 0])
    count = output.shape[0]
    pieces = []
    row = iota((count, 128), 0)
    for c in range(ROWS // 128):
        col = iota((8, 128), 1) + 128 * c
        z = (col >= PLANE).astype(jnp.int32) + (col >= 2 * PLANE) + (col >= 3 * PLANE)
        rest = col - PLANE * z
        x, j = rest >> 4, rest & 15
        source = slot_rows(slots, z, x, j - 1, (j >= 1) & (j <= NY))
        source = jnp.broadcast_to(source[0:1, :], (count, 128))
        pieces.append(jnp.where(row == source, 1.0, 0.0).astype(jnp.bfloat16))
    by_slot = dot(jnp.concatenate(pieces, axis=1), both).astype(jnp.bfloat16)
    output[...] = by_slot[:, 0:128]
    grad[...] = by_slot[:, 128:256]
    passed[...] = held[...]


def pairs(value_first, value_second, axis):
    drift, wire = lax.axis_size("drift"), lax.axis_size("wire")
    count = lax.axis_size(axis)
    first = [(i, i ^ 1) for i in range(count) if i ^ 1 < count]
    second = {i: i + 1 if i % 2 else i - 1 for i in range(1, count - 1)}
    if axis == "drift":
        second.update({0: count - 1, count - 1: 0})
        got_second = lax.ppermute(value_second, axis, sorted(second.items()))
    else:
        moves = [
            (d * wire + w, d * wire + second[w] if w in second else (d ^ 1) * wire + w)
            for d in range(drift)
            for w in range(wire)
        ]
        got_second = lax.ppermute(value_second, ("drift", "wire"), moves)
    got_first = lax.ppermute(value_first, axis, first)
    return got_first, got_second


def on_device(features, first_weight, second_weight, cotangent, counts, kernel_map, send_lists):
    drift, wire = lax.axis_size("drift"), lax.axis_size("wire")
    chips = drift // 2
    blocks = -(-TAPS // chips)
    chunk = blocks * CHANNELS
    unit = chunk // wire
    rows = TAPS * CHANNELS
    f, g = features[0, 0], cotangent[0, 0]
    slots = f.shape[0]
    padded = -(-slots // 128) * 128
    conv_scratch = [pltpu.VMEM((4, WIDE, 1152), jnp.bfloat16), pltpu.VMEM((128, rows), jnp.bfloat16)]
    edge_window = pltpu.VMEM((4, J, 1152), jnp.bfloat16)
    faces_scratch = pltpu.VMEM((128, 256), jnp.bfloat16)
    face, slab, grid = bf16(FACE, 256), bf16(SLAB, 256), bf16(ROWS, 256)

    def swap_core(value):
        return lax.ppermute(value, "drift", [(i, i ^ 1) for i in range(drift)])

    def to_chip(value, kind):
        return lax.ppermute(value, "drift", [(i, i ^ (2 * chip_mask(kind, i % 2))) for i in range(drift)])

    def to_wire(value, step):
        return lax.ppermute(value, "wire", [(i, i ^ step) for i in range(wire)])

    pair = jnp.concatenate([f, g], axis=1)
    weights = jnp.concatenate([first_weight, second_weight], axis=0)
    *faces, placed, live = call(
        place_kernel,
        (face, face, grid, bf16(ROWS, 128)),
        [VMEM] * 3,
        [pltpu.VMEM((padded, 256), jnp.bfloat16)],
    )(counts, send_lists, pair)
    faces = pairs(*faces, "wire")
    full, *slabs = call(insert_faces, (grid, slab, slab), [VMEM] * 3, [faces_scratch])(placed, *faces)
    slabs = pairs(*slabs, "drift")
    message = bf16(ROWS + 4 * WIDE, 128)
    inner = call(inner_kernel, f32(ROWS, 128), [VMEM] * 2, conv_scratch[:1])(full, weights)
    hb, keep, send = call(
        first_kernel,
        (grid, message, message),
        [VMEM] * 6,
        conv_scratch + [edge_window, pltpu.VMEM((ROWS, 128), jnp.float32)],
    )(full, *slabs, live, weights, inner)
    got = swap_core(send)
    term_window = pltpu.VMEM((4, WIDE, 1152), jnp.bfloat16)
    terms = f32(chunk * chips, 128)
    own_terms = call(own_terms_kernel, terms, [VMEM], [term_window])(keep)
    four = chips == 4
    kinds = ("opposite", "first", "second", "own") if four else (*range(1, chips), 0)
    shapes = [f32(chunk, 128) if k in ("second", "own", 0) else bf16(chunk, 128) for k in kinds]
    lead, left, held_window = call(
        functools.partial(lead_terms_kernel, blocks, kinds[0]),
        (shapes[0], bf16(128, ROWS), bf16(4, WIDE, 1152)),
        [VMEM] * 2,
    )(own_terms, got)
    *sends, own, face_first, face_second = call(
        functools.partial(terms_kernel, chunk, kinds[1:]),
        (*shapes[1:], face, face),
        [VMEM] * 4,
        [pltpu.VMEM(terms.shape, jnp.float32)],
    )(own_terms, left, held_window, hb)
    sends = [lead] + sends
    if four:
        opposite, first, second_part = sends
        passed = to_chip(opposite, "first")
        parts = [to_chip(first, "first")]
        passed = call(passed_on_kernel, bf16(chunk, 128), [VMEM] * 2)(second_part, passed)
        parts.append(to_chip(passed, "second"))
    else:
        parts = [to_chip(value, k) for k, value in zip(kinds, sends)]
    faces = pairs(face_first, face_second, "wire")
    hb_full, *hb_slabs = call(insert_faces, (grid, slab, slab), [VMEM] * 3, [faces_scratch])(hb, *faces)
    inserted = hb_slabs[0]
    hb_slabs = pairs(*hb_slabs, "drift")
    token = f32(8, 128)
    (inner_hidden, hidden_done), (inner_back, back_done) = (
        call(
            functools.partial(second_inner_kernel, field),
            (f32(ROWS, 128), token),
            [VMEM] * 2,
            conv_scratch[: 1 + field],
        )(hb_full, weights)
        for field in (0, 1)
    )
    *sends, own = call(
        functools.partial(split_kernel, unit, len(parts)),
        tuple([bf16(unit, 128)] * (wire - 1) + [f32(unit, 128)]),
        [VMEM] * (2 + len(parts)),
        [pltpu.VMEM((chunk, 128), jnp.float32)],
    )(inserted, own, *parts)

    received = [to_wire(sends[k - 1], k) for k in reversed(range(1, wire))]
    scale = 1.0 / math.sqrt(float(drift * wire * slots))
    summed = call(functools.partial(sum_kernel, scale), bf16(unit, 128), [VMEM] * (1 + wire))(
        hidden_done, own, *received
    )
    pieces = [summed] + [to_wire(summed, k) for k in range(1, wire)]
    mine = call(functools.partial(joined_kernel, unit), bf16(chunk, 128), [VMEM] * (1 + wire))(back_done, *pieces)
    output, grad_features, passed = call(
        second_kernel,
        (bf16(slots, 128), bf16(slots, 128), bf16(chunk, 128)),
        [SMEM] * 2 + [VMEM] * 8,
        [edge_window, pltpu.VMEM((ROWS, 128), jnp.float32), pltpu.VMEM((TAPS, 128, 128), jnp.bfloat16)],
    )(send_lists, counts, inner_hidden, inner_back, *hb_slabs, full, live, weights, mine)
    if four:
        brought = {"own": mine, "first": to_chip(mine, "first"), "second": to_chip(passed, "second")}
        brought["opposite"] = to_chip(brought["first"], "second")
        early = [
            [("own", True), ("own", False), ("first", True)],
            [("second", True), ("first", False), ("second", False)],
        ]
        last = "opposite"
    else:
        brought = {k: to_chip(passed if k > 1 else mine, k) if k else mine for k in range(chips)}
        last = chips - 1
        early = [[(k, True) for k in range(last)] + [(k, False) for k in range(last)]]
    late = [[(last, True)], [(last, False)]]
    swapped = {kind: swap_core(value) for kind, value in brought.items() if kind != last}
    grads = ()
    for n, items in enumerate(early + late):
        if n == len(early):
            held = call(relay_kernel, bf16(*brought[last].shape), [VMEM] * 2)(done, brought[last])
            swapped[last] = swap_core(held)
        values = [(brought if own_core else swapped)[kind] for kind, own_core in items]
        staged = sum(value.shape[0] for value in values) // CHANNELS
        want_done = n == len(early) - 1
        *grads, done = (
            *call(
                functools.partial(final_kernel, items, blocks, want_done),
                (f32(TAPS, 128, 128), f32(TAPS, 128, 128)) + (token,) * want_done,
                [VMEM] * len(items) + [HBM] * len(grads),
                [pltpu.VMEM((staged, 128, 128), jnp.float32), pltpu.SemaphoreType.DMA((staged,))],
                50 * 10**9,
                (HBM, HBM) + (VMEM,) * want_done,
                {len(items): 0, len(items) + 1: 1} if grads else {},
            )(*values, *grads),
            *(() if want_done else (None,)),
        )
    grad_first, grad_second = grads
    return output[None, None], grad_features[None, None], grad_first, grad_second


def solution(mesh):
    placed = (
        P("drift", "wire", None, None),
        P(),
        P(),
        P("drift", "wire", None, None),
        P("drift", "wire"),
        P("drift", "wire", None, None),
        P("drift", "wire", None),
    )
    return jax.shard_map(
        on_device,
        mesh=mesh,
        in_specs=placed,
        out_specs=(P("drift", "wire", None, None), P("drift", "wire", None, None), P(), P()),
        check_vma=False,
    )
```

```python
import functools
import math

import jax
import jax.numpy as jnp
from jax import lax
from jax.experimental import pallas as pl
from jax.experimental.pallas import tpu as pltpu
from jax.sharding import PartitionSpec as P

BX = 3
BW = 3
NX = 4 * BX
NY = 4 * BW
J = 16
PLANE = NX * J
WIDE = (NX + 2) * J
ROWS = 4 * PLANE
FACE = 4 * NX
SLAB = 4 * J
CHANNELS = 128
TAPS = 27
VMEM = pl.BlockSpec(memory_space=pltpu.VMEM)
HBM = pl.BlockSpec(memory_space=pltpu.HBM)
SMEM = pl.BlockSpec(memory_space=pltpu.SMEM)
LISTED = {0: 0, 1: 1, 2: 2, 3: 7, 5: 10, 6: 3, 7: 4, 8: 5}


def call(kernel, out_shape, in_specs, scratch=(), flops=0, out_spec=VMEM, aliases={}, vmem=40):
    return pl.pallas_call(
        kernel,
        out_shape=out_shape,
        in_specs=in_specs,
        out_specs=out_spec if isinstance(out_spec, tuple) else jax.tree.map(lambda _: out_spec, out_shape),
        scratch_shapes=list(scratch),
        input_output_aliases=aliases,
        compiler_params=pltpu.CompilerParams(vmem_limit_bytes=vmem * 1024 * 1024),
        cost_estimate=pl.CostEstimate(
            flops=flops, bytes_accessed=0, transcendentals=0
        ),
    )


def bf16(*shape):
    return jax.ShapeDtypeStruct(shape, jnp.bfloat16)


def f32(*shape):
    return jax.ShapeDtypeStruct(shape, jnp.float32)


def iota(shape, dim):
    return lax.broadcasted_iota(jnp.int32, shape, dim)


def position_slots(listed, count):
    slots = {p: listed(i) for p, i in LISTED.items()}
    present = {p: (s < 9).astype(jnp.int32) for p, s in slots.items()}
    before = present[0] + present[1] + present[2] + present[3]
    others = before + present[5] + present[6] + present[7] + present[8]
    slots[4] = jnp.where(count > others, before, 9)
    return slots


def slot_rows(slots, z, x, y, valid):
    position = (x >> 2) * BW + (y >> 2)
    slot = jnp.full(position.shape, 9, jnp.int32)
    for p, s in slots.items():
        slot = jnp.where(position == p, s, slot)
    row = slot * 64 + (x & 3) * 16 + (y & 3) * 4 + z
    return jnp.where(valid & (slot < 9), row, -1)


def one_hot(rows, width):
    lane = iota(rows.shape, 1)
    parts = [jnp.where(rows == lane + 128 * c, 1.0, 0.0).astype(jnp.bfloat16) for c in range(width // 128)]
    return jnp.concatenate(parts, axis=1)


def dot(a, b):
    return jnp.dot(a, b, preferred_element_type=jnp.float32)


def grid_indices():
    shape = (4, NX, J, 128)
    z, x, j = (iota(shape, d).reshape(ROWS, 128) for d in range(3))
    return z, x, j


def face_indices():
    r = iota((FACE, 128), 0)
    z = (r >= NX).astype(jnp.int32) + (r >= 2 * NX) + (r >= 3 * NX)
    return z, r - NX * z


def write_by_parity(axis, low, high, first, second):
    even = lax.axis_index(axis) % 2 == 0
    first[...] = jnp.where(even, high, low)
    second[...] = jnp.where(even, low, high)


def read_by_parity(axis, first, second):
    me, count = lax.axis_index(axis), lax.axis_size(axis)
    even = me % 2 == 0
    a, b = first[...], second[...]
    nothing = jnp.zeros_like(a)
    low = jnp.where(me > 0, jnp.where(even, b, a), nothing)
    high = jnp.where(me < count - 1, jnp.where(even, a, b), nothing)
    return low, high


def load_slots(counts, lists, pair, both):
    count = pair.shape[0]
    both[0:count, :] = pair[...]
    both[count:, :] = jnp.zeros((both.shape[0] - count, 256), jnp.bfloat16)
    entries = lists[0]

    def entry(i):
        return jnp.sum(jnp.where(iota(entries.shape, 1) == i, entries, 0), axis=1, keepdims=True)

    return position_slots(entry, counts[...])


def faces_kernel(counts, lists, pair, first, second, both):
    slots = load_slots(counts, lists, pair, both)
    z, x = face_indices()
    low, high = (
        dot(
            one_hot(slot_rows(slots, z, x, jnp.full_like(x, y), x >= 0), both.shape[0]), both[...]
        ).astype(jnp.bfloat16)
        for y in (0, NY - 1)
    )
    write_by_parity("wire", low, high, first, second)


def place_kernel(counts, lists, pair, out, live, both):
    slots = load_slots(counts, lists, pair, both)
    z, x, j = grid_indices()
    rows = slot_rows(slots, z, x, j - 1, (j >= 1) & (j <= NY))
    live[...] = (rows >= 0).astype(jnp.bfloat16)
    out[...] = dot(one_hot(rows, both.shape[0]), both[...]).astype(jnp.bfloat16)


def insert_faces(placed, got_second, got_first, out, slab_first, slab_second, faces):
    low, high = read_by_parity("wire", got_first, got_second)
    faces[0:FACE, :] = low
    faces[FACE : 2 * FACE, :] = high
    faces[2 * FACE :, :] = jnp.zeros((faces.shape[0] - 2 * FACE, 256), jnp.bfloat16)
    z, x, j = grid_indices()
    rows = z * NX + x
    rows = jnp.where(j == 0, rows, jnp.where(j == NY + 1, rows + FACE, -1))
    full = (placed[...].astype(jnp.float32) + dot(one_hot(rows, 128), faces[...])).astype(jnp.bfloat16)
    out[...] = full
    low = jnp.concatenate([full[z * PLANE : z * PLANE + J, :] for z in range(4)], axis=0)
    high = jnp.concatenate([full[(z + 1) * PLANE - J : (z + 1) * PLANE, :] for z in range(4)], axis=0)
    write_by_parity("drift", low, high, slab_first, slab_second)


def build_window(window, base, plane_of):
    for zi in range(4):
        plane = plane_of(zi)
        wide = plane.astype(jnp.float32)
        before = pltpu.roll(wide, 1, 0).astype(jnp.bfloat16)
        after = pltpu.roll(wide, plane.shape[0] - 1, 0).astype(jnp.bfloat16)
        for oy, shifted in enumerate((before, plane, after)):
            for z in range(max(0, zi - 1), min(3, zi + 1) + 1):
                lane = 128 * (3 * oy + zi - z + 1)
                window[base + z, :, lane : lane + 128] = shifted
    empty = jnp.zeros((plane.shape[0], 128), jnp.bfloat16)
    for oy in range(3):
        window[base, :, 384 * oy : 384 * oy + 128] = empty
        window[base + 3, :, 384 * oy + 256 : 384 * oy + 384] = empty


def wide_plane(full, low, high, z, lanes):
    return jnp.concatenate(
        [
            low[z * J : (z + 1) * J, lanes],
            full[z * PLANE : (z + 1) * PLANE, lanes],
            high[z * J : (z + 1) * J, lanes],
        ],
        axis=0,
    )


def conv(window, weights, base):
    total = None
    for ox in range(3):
        rows = window[:, ox * J : ox * J + PLANE, :].reshape(ROWS, 1152)
        term = dot(rows, weights[base + 9 * ox : base + 9 * (ox + 1)].reshape(1152, 128))
        total = term if total is None else total + term
    return total


def flip_blocks(weights, base, flipped):
    for k in range(TAPS):
        flipped[:, 128 * k : 128 * (k + 1)] = weights[base + TAPS - 1 - k]


def conv_flipped(window, flipped):
    total = None
    for ox in range(3):
        rows = window[:, ox * J : ox * J + PLANE, :].reshape(ROWS, 1152)
        term = lax.dot_general(
            rows,
            flipped[:, 1152 * ox : 1152 * (ox + 1)],
            (((1,), (1,)), ((), ())),
            preferred_element_type=jnp.float32,
        )
        total = term if total is None else total + term
    return total


def inner_kernel(full, weights, pre, window):
    edge = jnp.zeros((SLAB, 128), jnp.bfloat16)
    build_window(window, 0, lambda z: wide_plane(full, edge, edge, z, slice(0, 128)))
    pre[...] = conv(window, weights, 0)


def add_edges(pre, low, high, weights, edge_window):
    for ox, x, slab in ((0, 0, low), (2, NX - 1, high)):
        build_window(edge_window, 0, lambda z: slab[z * J : (z + 1) * J, :])
        taps = weights[9 * ox : 9 * (ox + 1)].reshape(1152, 128)
        term = dot(edge_window[...].reshape(SLAB, 1152), taps)
        for z in range(4):
            start = z * PLANE + x * J
            pre[start : start + J, :] += term[z * J : (z + 1) * J, :]


def first_kernel(full, got_first, got_second, live, weights, inner, hb, keep, send, window, flipped, edge_window, pre):
    f_lanes, g_lanes = slice(0, 128), slice(128, 256)
    low, high = read_by_parity("drift", got_first, got_second)
    alive = live[...].astype(jnp.float32)
    flip_blocks(weights, TAPS, flipped)
    pre[...] = inner[...]
    add_edges(pre, low[:, f_lanes], high[:, f_lanes], weights, edge_window)
    first_pre = pre[...]
    gate = jax.nn.sigmoid(first_pre)
    hidden = (alive * (first_pre * gate)).astype(jnp.bfloat16)
    slope = alive * (gate * (1.0 + first_pre * (1.0 - gate)))
    build_window(window, 0, lambda z: wide_plane(full, low, high, z, g_lanes))
    back = (conv_flipped(window, flipped) * slope).astype(jnp.bfloat16)
    hb[...] = jnp.concatenate([hidden, back], axis=1)
    core = lax.axis_index("drift") % 2

    def write(to, values, lanes):
        to[0:ROWS, :] = values
        for z in range(4):
            start = ROWS + z * WIDE
            to[start : start + WIDE, :] = wide_plane(full, low, high, z, lanes)

    @pl.when(core == 0)
    def _():
        write(keep, hidden, g_lanes)
        write(send, back, f_lanes)

    @pl.when(core != 0)
    def _():
        write(keep, back, f_lanes)
        write(send, hidden, g_lanes)


def chip_mask(kind, core):
    if isinstance(kind, int):
        return kind
    first = 1 + core
    return {"own": 0, "first": first, "second": 3 - first, "opposite": 3}[kind]


def left_rows(part):
    return part[0:ROWS, :].astype(jnp.float32).T.astype(jnp.bfloat16)


def term_planes(part):
    return lambda z: part[ROWS + z * WIDE : ROWS + (z + 1) * WIDE, :]


def add_terms(left, window, add_block):
    for ox in range(3):
        shifted = window[:, ox * J : ox * J + PLANE, :].reshape(ROWS, 1152)
        product = dot(left, shifted)
        for k in range(9):
            add_block(128 * (9 * ox + k), product[:, 128 * k : 128 * (k + 1)])


def own_terms_kernel(mine, total, window):
    rows = TAPS * CHANNELS
    if total.shape[0] > rows:
        total[rows:, :] = jnp.zeros((total.shape[0] - rows, 128), jnp.float32)
    build_window(window, 0, term_planes(mine))

    def put(start, block):
        total[start : start + 128, :] = block

    add_terms(left_rows(mine), window, put)


def lead_terms_kernel(blocks, kind, mine, theirs, out, left, window):
    build_window(window, 0, term_planes(theirs))
    left[...] = left_rows(theirs)
    me, core = lax.axis_index("drift") // 2, lax.axis_index("drift") % 2
    lead = (me ^ chip_mask(kind, core)) * blocks
    columns = []
    for i in range(blocks):
        tap = jnp.minimum(lead + i, TAPS - 1)
        row = pl.multiple_of(tap // 9 * J, J)
        lane = pl.multiple_of(tap % 9 * 128, 128)
        columns.append(window[:, pl.ds(row, PLANE), pl.ds(lane, 128)].reshape(ROWS, 128))
    product = dot(left[...], jnp.concatenate(columns, axis=1))
    for i in range(blocks):
        held = mine[pl.ds(pl.multiple_of((lead + i) * 128, 128), 128), :]
        term = product[:, 128 * i : 128 * (i + 1)]
        out[128 * i : 128 * (i + 1), :] = (held + jnp.where(lead + i < TAPS, term, 0.0)).astype(out.dtype)


def terms_kernel(chunk, kinds, mine, left, window, hb, *refs):
    *outs, first, second, total = refs
    rows = TAPS * CHANNELS
    if total.shape[0] > rows:
        total[rows:, :] = mine[rows:, :]

    def put(start, block):
        total[start : start + 128, :] = mine[start : start + 128, :] + block

    add_terms(left[...], window, put)
    me, core = lax.axis_index("drift") // 2, lax.axis_index("drift") % 2
    for kind, out in zip(kinds, outs):
        start = pl.multiple_of((me ^ chip_mask(kind, core)) * chunk, 128)
        out[...] = total[pl.ds(start, chunk), :].astype(out.dtype)
    z, x = face_indices()
    start = z * PLANE + x * J
    low, high = (dot(one_hot(start + j, ROWS), hb[...]).astype(jnp.bfloat16) for j in (1, NY))
    write_by_parity("wire", low, high, first, second)


def passed_on_kernel(partial, received, out):
    out[...] = (partial[...] + received[...].astype(jnp.float32)).astype(jnp.bfloat16)


def relay_kernel(after, value, out):
    out[...] = value[...]


def split_kernel(unit, count, after, own, *refs):
    received, (*sends, rest, total) = refs[:count], refs[count:]
    summed = own[...]
    for part in received:
        summed = summed + part[...].astype(jnp.float32)
    total[...] = summed
    me = lax.axis_index("wire")
    rest[...] = total[pl.ds(pl.multiple_of(me * unit, 16), unit), :]
    for step, out in enumerate(sends):
        start = pl.multiple_of((me ^ (step + 1)) * unit, 16)
        out[...] = total[pl.ds(start, unit), :].astype(jnp.bfloat16)


def sum_kernel(scale, after, own, *refs):
    *received, out = refs
    summed = own[...]
    for part in received:
        summed = summed + part[...].astype(jnp.float32)
    out[...] = (summed * scale).astype(jnp.bfloat16)


def joined_kernel(unit, after, *refs):
    *parts, out = refs
    me = lax.axis_index("wire")
    for step, part in enumerate(parts):
        start = pl.multiple_of((me ^ step) * unit, 16)
        out[pl.ds(start, unit), :] = part[...]


def final_kernel(items, blocks, want_done, *refs):
    parts = refs[: len(items)]
    first, second, *done, staged, sems = refs[len(refs) - 4 - want_done :]
    me = lax.axis_index("drift") // 2
    for ref in done:
        ref[...] = jnp.zeros_like(ref)

    def write(core):
        copies = []
        for part, (kind, mine) in zip(parts, items):
            source = core if mine else 1 - core
            count, here = part.shape[0] // 128, len(copies)
            chunk = me ^ chip_mask(kind, source)
            for i in range(count):
                block = part[128 * i : 128 * (i + 1), :].astype(jnp.float32)
                staged[here + i] = block.T if source else block
                tap = chunk * blocks + i
                safe = jnp.minimum(tap, TAPS - 1)
                to = first.at[safe] if source else second.at[TAPS - 1 - safe]
                copies.append((tap < TAPS, pltpu.make_async_copy(staged.at[here + i], to, sems.at[here + i])))
                pl.when(copies[-1][0])(copies[-1][1].start)
        for used, copy in copies:
            pl.when(used)(copy.wait)

    even = lax.axis_index("drift") % 2 == 0
    pl.when(even)(lambda: write(0))
    pl.when(jnp.logical_not(even))(lambda: write(1))


def second_inner_kernel(field, hb, weights, inner, done, window, *flipped):
    edge = jnp.zeros((SLAB, 256), jnp.bfloat16)
    build_window(window, 0, lambda z: wide_plane(hb, edge, edge, z, slice(128 * field, 128 * (field + 1))))
    if field:
        flip_blocks(weights, 0, *flipped)
        inner[...] = conv_flipped(window, *flipped)
    else:
        inner[...] = conv(window, weights, TAPS)
    done[...] = jnp.zeros_like(done)


def second_kernel(
    lists, counts, inner_hidden, inner_back, got_first, got_second, base, live, weights, held, output, grad, passed, edge_window, pre, taps
):
    low, high = read_by_parity("drift", got_first, got_second)
    results = []
    for field in (0, 1):
        lanes = slice(128 * field, 128 * (field + 1))
        pre[...] = inner_back[...] if field else inner_hidden[...]
        if field:
            for k in (*range(9), *range(18, 27)):
                taps[k] = weights[TAPS - 1 - k].astype(jnp.float32).T.astype(jnp.bfloat16)
            add_edges(pre, low[:, lanes], high[:, lanes], taps, edge_window)
        else:
            add_edges(pre, low[:, lanes], high[:, lanes], weights.at[TAPS:], edge_window)
        value = base[:, lanes].astype(jnp.float32) + pre[...]
        results.append((live[...].astype(jnp.float32) * value).astype(jnp.bfloat16))
    both = jnp.concatenate(results, axis=1)
    slots = position_slots(lambda i: lists[0, 0, i], counts[0, 0])
    count = output.shape[0]
    pieces = []
    row = iota((count, 128), 0)
    for c in range(ROWS // 128):
        col = iota((8, 128), 1) + 128 * c
        z = (col >= PLANE).astype(jnp.int32) + (col >= 2 * PLANE) + (col >= 3 * PLANE)
        rest = col - PLANE * z
        x, j = rest >> 4, rest & 15
        source = slot_rows(slots, z, x, j - 1, (j >= 1) & (j <= NY))
        source = jnp.broadcast_to(source[0:1, :], (count, 128))
        pieces.append(jnp.where(row == source, 1.0, 0.0).astype(jnp.bfloat16))
    by_slot = dot(jnp.concatenate(pieces, axis=1), both).astype(jnp.bfloat16)
    output[...] = by_slot[:, 0:128]
    grad[...] = by_slot[:, 128:256]
    passed[...] = held[...]


def pairs(value_first, value_second, axis):
    drift, wire = lax.axis_size("drift"), lax.axis_size("wire")
    count = lax.axis_size(axis)
    first = [(i, i ^ 1) for i in range(count) if i ^ 1 < count]
    second = {i: i + 1 if i % 2 else i - 1 for i in range(1, count - 1)}
    if axis == "drift":
        second.update({0: count - 1, count - 1: 0})
        got_second = lax.ppermute(value_second, axis, sorted(second.items()))
    else:
        moves = [
            (d * wire + w, d * wire + second[w] if w in second else (d ^ 1) * wire + w)
            for d in range(drift)
            for w in range(wire)
        ]
        got_second = lax.ppermute(value_second, ("drift", "wire"), moves)
    got_first = lax.ppermute(value_first, axis, first)
    return got_first, got_second


def on_device(features, first_weight, second_weight, cotangent, counts, kernel_map, send_lists):
    drift, wire = lax.axis_size("drift"), lax.axis_size("wire")
    chips = drift // 2
    blocks = -(-TAPS // chips)
    chunk = blocks * CHANNELS
    unit = chunk // wire
    rows = TAPS * CHANNELS
    f, g = features[0, 0], cotangent[0, 0]
    slots = f.shape[0]
    padded = -(-slots // 128) * 128
    conv_scratch = [pltpu.VMEM((4, WIDE, 1152), jnp.bfloat16), pltpu.VMEM((128, rows), jnp.bfloat16)]
    edge_window = pltpu.VMEM((4, J, 1152), jnp.bfloat16)
    faces_scratch = pltpu.VMEM((128, 256), jnp.bfloat16)
    face, slab, grid = bf16(FACE, 256), bf16(SLAB, 256), bf16(ROWS, 256)

    def swap_core(value):
        return lax.ppermute(value, "drift", [(i, i ^ 1) for i in range(drift)])

    def to_chip(value, kind):
        return lax.ppermute(value, "drift", [(i, i ^ (2 * chip_mask(kind, i % 2))) for i in range(drift)])

    def to_wire(value, step):
        return lax.ppermute(value, "wire", [(i, i ^ step) for i in range(wire)])

    pair = jnp.concatenate([f, g], axis=1)
    weights = jnp.concatenate([first_weight, second_weight], axis=0)
    pair_scratch = [pltpu.VMEM((padded, 256), jnp.bfloat16)]
    faces = call(faces_kernel, (face, face), [VMEM] * 3, pair_scratch)(counts, send_lists, pair)
    placed, live = call(place_kernel, (grid, bf16(ROWS, 128)), [VMEM] * 3, pair_scratch)(counts, send_lists, pair)
    faces = pairs(*faces, "wire")
    full, *slabs = call(insert_faces, (grid, slab, slab), [VMEM] * 3, [faces_scratch])(placed, *faces[::-1])
    slabs = pairs(*slabs, "drift")
    message = bf16(ROWS + 4 * WIDE, 128)
    inner = call(inner_kernel, f32(ROWS, 128), [VMEM] * 2, conv_scratch[:1])(full, weights)
    hb, keep, send = call(
        first_kernel,
        (grid, message, message),
        [VMEM] * 6,
        conv_scratch + [edge_window, pltpu.VMEM((ROWS, 128), jnp.float32)],
    )(full, *slabs, live, weights, inner)
    got = swap_core(send)
    term_window = pltpu.VMEM((4, WIDE, 1152), jnp.bfloat16)
    terms = f32(chunk * chips, 128)
    own_terms = call(own_terms_kernel, terms, [VMEM], [term_window])(keep)
    four = chips == 4
    kinds = ("opposite", "first", "second", "own") if four else (*range(1, chips), 0)
    shapes = [f32(chunk, 128) if k in ("second", "own", 0) else bf16(chunk, 128) for k in kinds]
    lead, left, held_window = call(
        functools.partial(lead_terms_kernel, blocks, kinds[0]),
        (shapes[0], bf16(128, ROWS), bf16(4, WIDE, 1152)),
        [VMEM] * 2,
    )(own_terms, got)
    *sends, own, face_first, face_second = call(
        functools.partial(terms_kernel, chunk, kinds[1:]),
        (*shapes[1:], face, face),
        [VMEM] * 4,
        [pltpu.VMEM(terms.shape, jnp.float32)],
    )(own_terms, left, held_window, hb)
    sends = [lead] + sends
    if four:
        opposite, first, second_part = sends
        passed = to_chip(opposite, "first")
        parts = [to_chip(first, "first")]
        passed = call(passed_on_kernel, bf16(chunk, 128), [VMEM] * 2)(second_part, passed)
        parts.append(to_chip(passed, "second"))
    else:
        parts = [to_chip(value, k) for k, value in zip(kinds, sends)]
    faces = pairs(face_first, face_second, "wire")
    hb_full, *hb_slabs = call(insert_faces, (grid, slab, slab), [VMEM] * 3, [faces_scratch])(hb, *faces[::-1])
    inserted = hb_slabs[0]
    hb_slabs = pairs(*hb_slabs, "drift")
    token = f32(8, 128)
    (inner_hidden, hidden_done), (inner_back, back_done) = (
        call(
            functools.partial(second_inner_kernel, field),
            (f32(ROWS, 128), token),
            [VMEM] * 2,
            conv_scratch[: 1 + field],
        )(hb_full, weights)
        for field in (0, 1)
    )
    *sends, own = call(
        functools.partial(split_kernel, unit, len(parts)),
        tuple([bf16(unit, 128)] * (wire - 1) + [f32(unit, 128)]),
        [VMEM] * (2 + len(parts)),
        [pltpu.VMEM((chunk, 128), jnp.float32)],
    )(inserted, own, *parts)

    received = [to_wire(sends[k - 1], k) for k in reversed(range(1, wire))]
    scale = 1.0 / math.sqrt(float(drift * wire * slots))
    summed = call(functools.partial(sum_kernel, scale), bf16(unit, 128), [VMEM] * (1 + wire))(
        hidden_done, own, *received
    )
    pieces = [summed] + [to_wire(summed, k) for k in range(1, wire)]
    mine = call(functools.partial(joined_kernel, unit), bf16(chunk, 128), [VMEM] * (1 + wire))(back_done, *pieces)
    output, grad_features, passed = call(
        second_kernel,
        (bf16(slots, 128), bf16(slots, 128), bf16(chunk, 128)),
        [SMEM] * 2 + [VMEM] * 8,
        [edge_window, pltpu.VMEM((ROWS, 128), jnp.float32), pltpu.VMEM((TAPS, 128, 128), jnp.bfloat16)],
    )(send_lists, counts, inner_hidden, inner_back, *hb_slabs, full, live, weights, mine)
    if four:
        brought = {"own": mine, "first": to_chip(mine, "first"), "second": to_chip(passed, "second")}
        brought["opposite"] = to_chip(brought["first"], "second")
        early = [
            [("own", True), ("own", False), ("first", True)],
            [("second", True), ("first", False), ("second", False)],
        ]
        last = "opposite"
    else:
        brought = {k: to_chip(passed if k > 1 else mine, k) if k else mine for k in range(chips)}
        last = chips - 1
        early = [[(k, True) for k in range(last)] + [(k, False) for k in range(last)]]
    late = [[(last, True)], [(last, False)]]
    swapped = {kind: swap_core(value) for kind, value in brought.items() if kind != last}
    grads = ()
    for n, items in enumerate(early + late):
        if n == len(early):
            held = call(relay_kernel, bf16(*brought[last].shape), [VMEM] * 2)(done, brought[last])
            swapped[last] = swap_core(held)
        values = [(brought if own_core else swapped)[kind] for kind, own_core in items]
        staged = sum(value.shape[0] for value in values) // CHANNELS
        want_done = n == len(early) - 1
        *grads, done = (
            *call(
                functools.partial(final_kernel, items, blocks, want_done),
                (f32(TAPS, 128, 128), f32(TAPS, 128, 128)) + (token,) * want_done,
                [VMEM] * len(items) + [HBM] * len(grads),
                [pltpu.VMEM((staged, 128, 128), jnp.float32), pltpu.SemaphoreType.DMA((staged,))],
                50 * 10**9,
                (HBM, HBM) + (VMEM,) * want_done,
                {len(items): 0, len(items) + 1: 1} if grads else {},
            )(*values, *grads),
            *(() if want_done else (None,)),
        )
    grad_first, grad_second = grads
    return output[None, None], grad_features[None, None], grad_first, grad_second


def solution(mesh):
    placed = (
        P("drift", "wire", None, None),
        P(),
        P(),
        P("drift", "wire", None, None),
        P("drift", "wire"),
        P("drift", "wire", None, None),
        P("drift", "wire", None),
    )
    return jax.shard_map(
        on_device,
        mesh=mesh,
        in_specs=placed,
        out_specs=(P("drift", "wire", None, None), P("drift", "wire", None, None), P(), P()),
        check_vma=False,
    )
```

```python
import functools
import math

import jax
import jax.numpy as jnp
from jax import lax
from jax.experimental import pallas as pl
from jax.experimental.pallas import tpu as pltpu
from jax.sharding import PartitionSpec as P

BX = 3
BW = 3
NX = 4 * BX
NY = 4 * BW
J = 16
PLANE = NX * J
WIDE = (NX + 2) * J
ROWS = 4 * PLANE
FACE = 4 * NX
SLAB = 4 * J
CHANNELS = 128
TAPS = 27
VMEM = pl.BlockSpec(memory_space=pltpu.VMEM)
HBM = pl.BlockSpec(memory_space=pltpu.HBM)
SMEM = pl.BlockSpec(memory_space=pltpu.SMEM)
LISTED = {0: 0, 1: 1, 2: 2, 3: 7, 5: 10, 6: 3, 7: 4, 8: 5}


def call(kernel, out_shape, in_specs, scratch=(), flops=0, out_spec=VMEM, aliases={}, vmem=40):
    return pl.pallas_call(
        kernel,
        out_shape=out_shape,
        in_specs=in_specs,
        out_specs=out_spec if isinstance(out_spec, tuple) else jax.tree.map(lambda _: out_spec, out_shape),
        scratch_shapes=list(scratch),
        input_output_aliases=aliases,
        compiler_params=pltpu.CompilerParams(vmem_limit_bytes=vmem * 1024 * 1024),
        cost_estimate=pl.CostEstimate(
            flops=flops, bytes_accessed=0, transcendentals=0
        ),
    )


def bf16(*shape):
    return jax.ShapeDtypeStruct(shape, jnp.bfloat16)


def f32(*shape):
    return jax.ShapeDtypeStruct(shape, jnp.float32)


def iota(shape, dim):
    return lax.broadcasted_iota(jnp.int32, shape, dim)


def position_slots(listed, count):
    slots = {p: listed(i) for p, i in LISTED.items()}
    present = {p: (s < 9).astype(jnp.int32) for p, s in slots.items()}
    before = present[0] + present[1] + present[2] + present[3]
    others = before + present[5] + present[6] + present[7] + present[8]
    slots[4] = jnp.where(count > others, before, 9)
    return slots


def slot_rows(slots, z, x, y, valid):
    position = (x >> 2) * BW + (y >> 2)
    slot = jnp.full(position.shape, 9, jnp.int32)
    for p, s in slots.items():
        slot = jnp.where(position == p, s, slot)
    row = slot * 64 + (x & 3) * 16 + (y & 3) * 4 + z
    return jnp.where(valid & (slot < 9), row, -1)


def one_hot(rows, width):
    lane = iota(rows.shape, 1)
    parts = [jnp.where(rows == lane + 128 * c, 1.0, 0.0).astype(jnp.bfloat16) for c in range(width // 128)]
    return jnp.concatenate(parts, axis=1)


def dot(a, b):
    return jnp.dot(a, b, preferred_element_type=jnp.float32)


def grid_indices():
    shape = (4, NX, J, 128)
    z, x, j = (iota(shape, d).reshape(ROWS, 128) for d in range(3))
    return z, x, j


def face_indices():
    r = iota((FACE, 128), 0)
    z = (r >= NX).astype(jnp.int32) + (r >= 2 * NX) + (r >= 3 * NX)
    return z, r - NX * z


def write_by_parity(axis, low, high, first, second):
    even = lax.axis_index(axis) % 2 == 0
    first[...] = jnp.where(even, high, low)
    second[...] = jnp.where(even, low, high)


def read_by_parity(axis, first, second):
    me, count = lax.axis_index(axis), lax.axis_size(axis)
    even = me % 2 == 0
    a, b = first[...], second[...]
    nothing = jnp.zeros_like(a)
    low = jnp.where(me > 0, jnp.where(even, b, a), nothing)
    high = jnp.where(me < count - 1, jnp.where(even, a, b), nothing)
    return low, high


def load_slots(counts, lists, pair, both):
    count = pair.shape[0]
    both[0:count, :] = pair[...]
    both[count:, :] = jnp.zeros((both.shape[0] - count, 256), jnp.bfloat16)
    entries = lists[0]

    def entry(i):
        return jnp.sum(jnp.where(iota(entries.shape, 1) == i, entries, 0), axis=1, keepdims=True)

    return position_slots(entry, counts[...])


def faces_kernel(counts, lists, pair, first, second, both):
    slots = load_slots(counts, lists, pair, both)
    z, x = face_indices()
    low, high = (
        dot(
            one_hot(slot_rows(slots, z, x, jnp.full_like(x, y), x >= 0), both.shape[0]), both[...]
        ).astype(jnp.bfloat16)
        for y in (0, NY - 1)
    )
    write_by_parity("wire", low, high, first, second)


def place_kernel(counts, lists, pair, out, live, both):
    slots = load_slots(counts, lists, pair, both)
    z, x, j = grid_indices()
    rows = slot_rows(slots, z, x, j - 1, (j >= 1) & (j <= NY))
    live[...] = (rows >= 0).astype(jnp.bfloat16)
    out[...] = dot(one_hot(rows, both.shape[0]), both[...]).astype(jnp.bfloat16)


def insert_faces(placed, got_second, got_first, out, slab_first, slab_second, faces):
    low, high = read_by_parity("wire", got_first, got_second)
    faces[0:FACE, :] = low
    faces[FACE : 2 * FACE, :] = high
    faces[2 * FACE :, :] = jnp.zeros((faces.shape[0] - 2 * FACE, 256), jnp.bfloat16)
    z, x, j = grid_indices()
    rows = z * NX + x
    rows = jnp.where(j == 0, rows, jnp.where(j == NY + 1, rows + FACE, -1))
    full = (placed[...].astype(jnp.float32) + dot(one_hot(rows, 128), faces[...])).astype(jnp.bfloat16)
    out[...] = full
    low = jnp.concatenate([full[z * PLANE : z * PLANE + J, :] for z in range(4)], axis=0)
    high = jnp.concatenate([full[(z + 1) * PLANE - J : (z + 1) * PLANE, :] for z in range(4)], axis=0)
    write_by_parity("drift", low, high, slab_first, slab_second)


def insert_hidden_faces(placed, got_first, got_second, *refs):
    insert_faces(placed, got_second, got_first, *refs)


def build_window(window, base, plane_of):
    for zi in range(4):
        plane = plane_of(zi)
        wide = plane.astype(jnp.float32)
        before = pltpu.roll(wide, 1, 0).astype(jnp.bfloat16)
        after = pltpu.roll(wide, plane.shape[0] - 1, 0).astype(jnp.bfloat16)
        for oy, shifted in enumerate((before, plane, after)):
            for z in range(max(0, zi - 1), min(3, zi + 1) + 1):
                lane = 128 * (3 * oy + zi - z + 1)
                window[base + z, :, lane : lane + 128] = shifted
    empty = jnp.zeros((plane.shape[0], 128), jnp.bfloat16)
    for oy in range(3):
        window[base, :, 384 * oy : 384 * oy + 128] = empty
        window[base + 3, :, 384 * oy + 256 : 384 * oy + 384] = empty


def wide_plane(full, low, high, z, lanes):
    return jnp.concatenate(
        [
            low[z * J : (z + 1) * J, lanes],
            full[z * PLANE : (z + 1) * PLANE, lanes],
            high[z * J : (z + 1) * J, lanes],
        ],
        axis=0,
    )


def conv(window, weights, base):
    total = None
    for ox in range(3):
        rows = window[:, ox * J : ox * J + PLANE, :].reshape(ROWS, 1152)
        term = dot(rows, weights[base + 9 * ox : base + 9 * (ox + 1)].reshape(1152, 128))
        total = term if total is None else total + term
    return total


def flip_blocks(weights, base, flipped):
    for k in range(TAPS):
        flipped[:, 128 * k : 128 * (k + 1)] = weights[base + TAPS - 1 - k]


def conv_flipped(window, flipped):
    total = None
    for ox in range(3):
        rows = window[:, ox * J : ox * J + PLANE, :].reshape(ROWS, 1152)
        term = lax.dot_general(
            rows,
            flipped[:, 1152 * ox : 1152 * (ox + 1)],
            (((1,), (1,)), ((), ())),
            preferred_element_type=jnp.float32,
        )
        total = term if total is None else total + term
    return total


def inner_kernel(full, weights, pre, window):
    edge = jnp.zeros((SLAB, 128), jnp.bfloat16)
    build_window(window, 0, lambda z: wide_plane(full, edge, edge, z, slice(0, 128)))
    pre[...] = conv(window, weights, 0)


def add_edges(pre, low, high, weights, edge_window):
    for ox, x, slab in ((0, 0, low), (2, NX - 1, high)):
        build_window(edge_window, 0, lambda z: slab[z * J : (z + 1) * J, :])
        taps = weights[9 * ox : 9 * (ox + 1)].reshape(1152, 128)
        term = dot(edge_window[...].reshape(SLAB, 1152), taps)
        for z in range(4):
            start = z * PLANE + x * J
            pre[start : start + J, :] += term[z * J : (z + 1) * J, :]


def first_kernel(full, got_first, got_second, live, weights, inner, hb, keep, send, window, flipped, edge_window, pre):
    f_lanes, g_lanes = slice(0, 128), slice(128, 256)
    low, high = read_by_parity("drift", got_first, got_second)
    alive = live[...].astype(jnp.float32)
    flip_blocks(weights, TAPS, flipped)
    pre[...] = inner[...]
    add_edges(pre, low[:, f_lanes], high[:, f_lanes], weights, edge_window)
    first_pre = pre[...]
    gate = jax.nn.sigmoid(first_pre)
    hidden = (alive * (first_pre * gate)).astype(jnp.bfloat16)
    slope = alive * (gate * (1.0 + first_pre * (1.0 - gate)))
    build_window(window, 0, lambda z: wide_plane(full, low, high, z, g_lanes))
    back = (conv_flipped(window, flipped) * slope).astype(jnp.bfloat16)
    hb[...] = jnp.concatenate([hidden, back], axis=1)
    core = lax.axis_index("drift") % 2

    def write(to, values, lanes):
        to[0:ROWS, :] = values
        for z in range(4):
            start = ROWS + z * WIDE
            to[start : start + WIDE, :] = wide_plane(full, low, high, z, lanes)

    @pl.when(core == 0)
    def _():
        write(keep, hidden, g_lanes)
        write(send, back, f_lanes)

    @pl.when(core != 0)
    def _():
        write(keep, back, f_lanes)
        write(send, hidden, g_lanes)


def chip_mask(kind, core):
    if isinstance(kind, int):
        return kind
    first = 1 + core
    return {"own": 0, "first": first, "second": 3 - first, "opposite": 3}[kind]


def left_rows(part):
    return part[0:ROWS, :].astype(jnp.float32).T.astype(jnp.bfloat16)


def term_planes(part):
    return lambda z: part[ROWS + z * WIDE : ROWS + (z + 1) * WIDE, :]


def add_terms(left, window, add_block):
    for ox in range(3):
        shifted = window[:, ox * J : ox * J + PLANE, :].reshape(ROWS, 1152)
        product = dot(left, shifted)
        for k in range(9):
            add_block(128 * (9 * ox + k), product[:, 128 * k : 128 * (k + 1)])


def own_terms_kernel(mine, total, window):
    rows = TAPS * CHANNELS
    if total.shape[0] > rows:
        total[rows:, :] = jnp.zeros((total.shape[0] - rows, 128), jnp.float32)
    build_window(window, 0, term_planes(mine))

    def put(start, block):
        total[start : start + 128, :] = block

    add_terms(left_rows(mine), window, put)


def lead_terms_kernel(blocks, kind, mine, theirs, out, left, window):
    build_window(window, 0, term_planes(theirs))
    left[...] = left_rows(theirs)
    me, core = lax.axis_index("drift") // 2, lax.axis_index("drift") % 2
    lead = (me ^ chip_mask(kind, core)) * blocks
    columns = []
    for i in range(blocks):
        tap = jnp.minimum(lead + i, TAPS - 1)
        row = pl.multiple_of(tap // 9 * J, J)
        lane = pl.multiple_of(tap % 9 * 128, 128)
        columns.append(window[:, pl.ds(row, PLANE), pl.ds(lane, 128)].reshape(ROWS, 128))
    product = dot(left[...], jnp.concatenate(columns, axis=1))
    for i in range(blocks):
        held = mine[pl.ds(pl.multiple_of((lead + i) * 128, 128), 128), :]
        term = product[:, 128 * i : 128 * (i + 1)]
        out[128 * i : 128 * (i + 1), :] = (held + jnp.where(lead + i < TAPS, term, 0.0)).astype(out.dtype)


def terms_kernel(chunk, kinds, mine, left, window, hb, *refs):
    *outs, first, second, total = refs
    rows = TAPS * CHANNELS
    if total.shape[0] > rows:
        total[rows:, :] = mine[rows:, :]

    def put(start, block):
        total[start : start + 128, :] = mine[start : start + 128, :] + block

    add_terms(left[...], window, put)
    me, core = lax.axis_index("drift") // 2, lax.axis_index("drift") % 2
    for kind, out in zip(kinds, outs):
        start = pl.multiple_of((me ^ chip_mask(kind, core)) * chunk, 128)
        out[...] = total[pl.ds(start, chunk), :].astype(out.dtype)
    z, x = face_indices()
    start = z * PLANE + x * J
    low, high = (dot(one_hot(start + j, ROWS), hb[...]).astype(jnp.bfloat16) for j in (1, NY))
    write_by_parity("wire", low, high, first, second)


def passed_on_kernel(partial, received, out):
    out[...] = (partial[...] + received[...].astype(jnp.float32)).astype(jnp.bfloat16)


def relay_kernel(after, value, out):
    out[...] = value[...]


def split_kernel(unit, count, after, own, *refs):
    received, (*sends, rest, total) = refs[:count], refs[count:]
    summed = own[...]
    for part in received:
        summed = summed + part[...].astype(jnp.float32)
    total[...] = summed
    me = lax.axis_index("wire")
    rest[...] = total[pl.ds(pl.multiple_of(me * unit, 16), unit), :]
    for step, out in enumerate(sends):
        start = pl.multiple_of((me ^ (step + 1)) * unit, 16)
        out[...] = total[pl.ds(start, unit), :].astype(jnp.bfloat16)


def sum_kernel(scale, after, own, *refs):
    *received, out = refs
    summed = own[...]
    for part in received:
        summed = summed + part[...].astype(jnp.float32)
    out[...] = (summed * scale).astype(jnp.bfloat16)


def joined_kernel(unit, after, *refs):
    *parts, out = refs
    me = lax.axis_index("wire")
    for step, part in enumerate(parts):
        start = pl.multiple_of((me ^ step) * unit, 16)
        out[pl.ds(start, unit), :] = part[...]


def final_kernel(items, blocks, want_done, *refs):
    parts = refs[: len(items)]
    first, second, *done, staged, sems = refs[len(refs) - 4 - want_done :]
    me = lax.axis_index("drift") // 2
    for ref in done:
        ref[...] = jnp.zeros_like(ref)

    def write(core):
        copies = []
        for part, (kind, mine) in zip(parts, items):
            source = core if mine else 1 - core
            count, here = part.shape[0] // 128, len(copies)
            chunk = me ^ chip_mask(kind, source)
            for i in range(count):
                block = part[128 * i : 128 * (i + 1), :].astype(jnp.float32)
                staged[here + i] = block.T if source else block
                tap = chunk * blocks + i
                safe = jnp.minimum(tap, TAPS - 1)
                to = first.at[safe] if source else second.at[TAPS - 1 - safe]
                copies.append((tap < TAPS, pltpu.make_async_copy(staged.at[here + i], to, sems.at[here + i])))
                pl.when(copies[-1][0])(copies[-1][1].start)
        for used, copy in copies:
            pl.when(used)(copy.wait)

    even = lax.axis_index("drift") % 2 == 0
    pl.when(even)(lambda: write(0))
    pl.when(jnp.logical_not(even))(lambda: write(1))


def second_inner_kernel(field, hb, weights, inner, done, window, *flipped):
    edge = jnp.zeros((SLAB, 256), jnp.bfloat16)
    build_window(window, 0, lambda z: wide_plane(hb, edge, edge, z, slice(128 * field, 128 * (field + 1))))
    if field:
        flip_blocks(weights, 0, *flipped)
        inner[...] = conv_flipped(window, *flipped)
    else:
        inner[...] = conv(window, weights, TAPS)
    done[...] = jnp.zeros_like(done)


def second_kernel(
    lists, counts, inner_hidden, inner_back, got_first, got_second, base, live, weights, held, output, grad, passed, edge_window, pre, taps
):
    low, high = read_by_parity("drift", got_first, got_second)
    results = []
    for field in (0, 1):
        lanes = slice(128 * field, 128 * (field + 1))
        pre[...] = inner_back[...] if field else inner_hidden[...]
        if field:
            for k in (*range(9), *range(18, 27)):
                taps[k] = weights[TAPS - 1 - k].astype(jnp.float32).T.astype(jnp.bfloat16)
            add_edges(pre, low[:, lanes], high[:, lanes], taps, edge_window)
        else:
            add_edges(pre, low[:, lanes], high[:, lanes], weights.at[TAPS:], edge_window)
        value = base[:, lanes].astype(jnp.float32) + pre[...]
        results.append((live[...].astype(jnp.float32) * value).astype(jnp.bfloat16))
    both = jnp.concatenate(results, axis=1)
    slots = position_slots(lambda i: lists[0, 0, i], counts[0, 0])
    count = output.shape[0]
    pieces = []
    row = iota((count, 128), 0)
    for c in range(ROWS // 128):
        col = iota((8, 128), 1) + 128 * c
        z = (col >= PLANE).astype(jnp.int32) + (col >= 2 * PLANE) + (col >= 3 * PLANE)
        rest = col - PLANE * z
        x, j = rest >> 4, rest & 15
        source = slot_rows(slots, z, x, j - 1, (j >= 1) & (j <= NY))
        source = jnp.broadcast_to(source[0:1, :], (count, 128))
        pieces.append(jnp.where(row == source, 1.0, 0.0).astype(jnp.bfloat16))
    by_slot = dot(jnp.concatenate(pieces, axis=1), both).astype(jnp.bfloat16)
    output[...] = by_slot[:, 0:128]
    grad[...] = by_slot[:, 128:256]
    passed[...] = held[...]


def pairs(value_first, value_second, axis):
    drift, wire = lax.axis_size("drift"), lax.axis_size("wire")
    count = lax.axis_size(axis)
    first = [(i, i ^ 1) for i in range(count) if i ^ 1 < count]
    second = {i: i + 1 if i % 2 else i - 1 for i in range(1, count - 1)}
    if axis == "drift":
        second.update({0: count - 1, count - 1: 0})
        got_second = lax.ppermute(value_second, axis, sorted(second.items()))
    else:
        moves = [
            (d * wire + w, d * wire + second[w] if w in second else (d ^ 1) * wire + w)
            for d in range(drift)
            for w in range(wire)
        ]
        got_second = lax.ppermute(value_second, ("drift", "wire"), moves)
    got_first = lax.ppermute(value_first, axis, first)
    return got_first, got_second


def on_device(features, first_weight, second_weight, cotangent, counts, kernel_map, send_lists):
    drift, wire = lax.axis_size("drift"), lax.axis_size("wire")
    chips = drift // 2
    blocks = -(-TAPS // chips)
    chunk = blocks * CHANNELS
    unit = chunk // wire
    rows = TAPS * CHANNELS
    f, g = features[0, 0], cotangent[0, 0]
    slots = f.shape[0]
    padded = -(-slots // 128) * 128
    conv_scratch = [pltpu.VMEM((4, WIDE, 1152), jnp.bfloat16), pltpu.VMEM((128, rows), jnp.bfloat16)]
    edge_window = pltpu.VMEM((4, J, 1152), jnp.bfloat16)
    faces_scratch = pltpu.VMEM((128, 256), jnp.bfloat16)
    face, slab, grid = bf16(FACE, 256), bf16(SLAB, 256), bf16(ROWS, 256)

    def swap_core(value):
        return lax.ppermute(value, "drift", [(i, i ^ 1) for i in range(drift)])

    def to_chip(value, kind):
        return lax.ppermute(value, "drift", [(i, i ^ (2 * chip_mask(kind, i % 2))) for i in range(drift)])

    def to_wire(value, step):
        return lax.ppermute(value, "wire", [(i, i ^ step) for i in range(wire)])

    pair = jnp.concatenate([f, g], axis=1)
    weights = jnp.concatenate([first_weight, second_weight], axis=0)
    pair_scratch = [pltpu.VMEM((padded, 256), jnp.bfloat16)]
    faces = call(faces_kernel, (face, face), [VMEM] * 3, pair_scratch)(counts, send_lists, pair)
    placed, live = call(place_kernel, (grid, bf16(ROWS, 128)), [VMEM] * 3, pair_scratch)(counts, send_lists, pair)
    faces = pairs(*faces, "wire")
    full, *slabs = call(insert_faces, (grid, slab, slab), [VMEM] * 3, [faces_scratch])(placed, *faces[::-1])
    slabs = pairs(*slabs, "drift")
    message = bf16(ROWS + 4 * WIDE, 128)
    inner = call(inner_kernel, f32(ROWS, 128), [VMEM] * 2, conv_scratch[:1])(full, weights)
    hb, keep, send = call(
        first_kernel,
        (grid, message, message),
        [VMEM] * 6,
        conv_scratch + [edge_window, pltpu.VMEM((ROWS, 128), jnp.float32)],
    )(full, *slabs, live, weights, inner)
    got = swap_core(send)
    term_window = pltpu.VMEM((4, WIDE, 1152), jnp.bfloat16)
    terms = f32(chunk * chips, 128)
    own_terms = call(own_terms_kernel, terms, [VMEM], [term_window])(keep)
    four = chips == 4
    kinds = ("opposite", "first", "second", "own") if four else (*range(1, chips), 0)
    shapes = [f32(chunk, 128) if k in ("second", "own", 0) else bf16(chunk, 128) for k in kinds]
    lead, left, held_window = call(
        functools.partial(lead_terms_kernel, blocks, kinds[0]),
        (shapes[0], bf16(128, ROWS), bf16(4, WIDE, 1152)),
        [VMEM] * 2,
    )(own_terms, got)
    *sends, own, face_first, face_second = call(
        functools.partial(terms_kernel, chunk, kinds[1:]),
        (*shapes[1:], face, face),
        [VMEM] * 4,
        [pltpu.VMEM(terms.shape, jnp.float32)],
    )(own_terms, left, held_window, hb)
    sends = [lead] + sends
    if four:
        opposite, first, second_part = sends
        passed = to_chip(opposite, "first")
        parts = [to_chip(first, "first")]
        passed = call(passed_on_kernel, bf16(chunk, 128), [VMEM] * 2)(second_part, passed)
        parts.append(to_chip(passed, "second"))
    else:
        parts = [to_chip(value, k) for k, value in zip(kinds, sends)]
    faces = pairs(face_first, face_second, "wire")
    hb_full, *hb_slabs = call(insert_hidden_faces, (grid, slab, slab), [VMEM] * 3, [faces_scratch])(hb, *faces)
    inserted = hb_slabs[0]
    hb_slabs = pairs(*hb_slabs, "drift")
    token = f32(8, 128)
    (inner_hidden, hidden_done), (inner_back, back_done) = (
        call(
            functools.partial(second_inner_kernel, field),
            (f32(ROWS, 128), token),
            [VMEM] * 2,
            conv_scratch[: 1 + field],
        )(hb_full, weights)
        for field in (0, 1)
    )
    *sends, own = call(
        functools.partial(split_kernel, unit, len(parts)),
        tuple([bf16(unit, 128)] * (wire - 1) + [f32(unit, 128)]),
        [VMEM] * (2 + len(parts)),
        [pltpu.VMEM((chunk, 128), jnp.float32)],
    )(inserted, own, *parts)

    received = [to_wire(sends[k - 1], k) for k in reversed(range(1, wire))]
    scale = 1.0 / math.sqrt(float(drift * wire * slots))
    summed = call(functools.partial(sum_kernel, scale), bf16(unit, 128), [VMEM] * (1 + wire))(
        hidden_done, own, *received
    )
    pieces = [summed] + [to_wire(summed, k) for k in range(1, wire)]
    mine = call(functools.partial(joined_kernel, unit), bf16(chunk, 128), [VMEM] * (1 + wire))(back_done, *pieces)
    output, grad_features, passed = call(
        second_kernel,
        (bf16(slots, 128), bf16(slots, 128), bf16(chunk, 128)),
        [SMEM] * 2 + [VMEM] * 8,
        [edge_window, pltpu.VMEM((ROWS, 128), jnp.float32), pltpu.VMEM((TAPS, 128, 128), jnp.bfloat16)],
    )(send_lists, counts, inner_hidden, inner_back, *hb_slabs, full, live, weights, mine)
    if four:
        brought = {"own": mine, "first": to_chip(mine, "first"), "second": to_chip(passed, "second")}
        brought["opposite"] = to_chip(brought["first"], "second")
        early = [
            [("own", True), ("own", False), ("first", True)],
            [("second", True), ("first", False), ("second", False)],
        ]
        last = "opposite"
    else:
        brought = {k: to_chip(passed if k > 1 else mine, k) if k else mine for k in range(chips)}
        last = chips - 1
        early = [[(k, True) for k in range(last)] + [(k, False) for k in range(last)]]
    late = [[(last, True)], [(last, False)]]
    swapped = {kind: swap_core(value) for kind, value in brought.items() if kind != last}
    grads = ()
    for n, items in enumerate(early + late):
        if n == len(early):
            held = call(relay_kernel, bf16(*brought[last].shape), [VMEM] * 2)(done, brought[last])
            swapped[last] = swap_core(held)
        values = [(brought if own_core else swapped)[kind] for kind, own_core in items]
        staged = sum(value.shape[0] for value in values) // CHANNELS
        want_done = n == len(early) - 1
        *grads, done = (
            *call(
                functools.partial(final_kernel, items, blocks, want_done),
                (f32(TAPS, 128, 128), f32(TAPS, 128, 128)) + (token,) * want_done,
                [VMEM] * len(items) + [HBM] * len(grads),
                [pltpu.VMEM((staged, 128, 128), jnp.float32), pltpu.SemaphoreType.DMA((staged,))],
                50 * 10**9,
                (HBM, HBM) + (VMEM,) * want_done,
                {len(items): 0, len(items) + 1: 1} if grads else {},
            )(*values, *grads),
            *(() if want_done else (None,)),
        )
    grad_first, grad_second = grads
    return output[None, None], grad_features[None, None], grad_first, grad_second


def solution(mesh):
    placed = (
        P("drift", "wire", None, None),
        P(),
        P(),
        P("drift", "wire", None, None),
        P("drift", "wire"),
        P("drift", "wire", None, None),
        P("drift", "wire", None),
    )
    return jax.shard_map(
        on_device,
        mesh=mesh,
        in_specs=placed,
        out_specs=(P("drift", "wire", None, None), P("drift", "wire", None, None), P(), P()),
        check_vma=False,
    )
```

```python
import functools
import math

import jax
import jax.numpy as jnp
from jax import lax
from jax.experimental import pallas as pl
from jax.experimental.pallas import tpu as pltpu
from jax.sharding import PartitionSpec as P

BX = 3
BW = 3
NX = 4 * BX
NY = 4 * BW
J = 16
PLANE = NX * J
WIDE = (NX + 2) * J
ROWS = 4 * PLANE
FACE = 4 * NX
SLAB = 4 * J
CHANNELS = 128
TAPS = 27
VMEM = pl.BlockSpec(memory_space=pltpu.VMEM)
HBM = pl.BlockSpec(memory_space=pltpu.HBM)
SMEM = pl.BlockSpec(memory_space=pltpu.SMEM)
LISTED = {0: 0, 1: 1, 2: 2, 3: 7, 5: 10, 6: 3, 7: 4, 8: 5}


def call(kernel, out_shape, in_specs, scratch=(), flops=0, out_spec=VMEM, aliases={}, vmem=40):
    return pl.pallas_call(
        kernel,
        out_shape=out_shape,
        in_specs=in_specs,
        out_specs=out_spec if isinstance(out_spec, tuple) else jax.tree.map(lambda _: out_spec, out_shape),
        scratch_shapes=list(scratch),
        input_output_aliases=aliases,
        compiler_params=pltpu.CompilerParams(vmem_limit_bytes=vmem * 1024 * 1024),
        cost_estimate=pl.CostEstimate(
            flops=flops, bytes_accessed=0, transcendentals=0
        ),
    )


def bf16(*shape):
    return jax.ShapeDtypeStruct(shape, jnp.bfloat16)


def f32(*shape):
    return jax.ShapeDtypeStruct(shape, jnp.float32)


def iota(shape, dim):
    return lax.broadcasted_iota(jnp.int32, shape, dim)


def position_slots(listed, count):
    slots = {p: listed(i) for p, i in LISTED.items()}
    present = {p: (s < 9).astype(jnp.int32) for p, s in slots.items()}
    before = present[0] + present[1] + present[2] + present[3]
    others = before + present[5] + present[6] + present[7] + present[8]
    slots[4] = jnp.where(count > others, before, 9)
    return slots


def slot_rows(slots, z, x, y, valid):
    position = (x >> 2) * BW + (y >> 2)
    slot = jnp.full(position.shape, 9, jnp.int32)
    for p, s in slots.items():
        slot = jnp.where(position == p, s, slot)
    row = slot * 64 + (x & 3) * 16 + (y & 3) * 4 + z
    return jnp.where(valid & (slot < 9), row, -1)


def one_hot(rows, width):
    lane = iota(rows.shape, 1)
    parts = [jnp.where(rows == lane + 128 * c, 1.0, 0.0).astype(jnp.bfloat16) for c in range(width // 128)]
    return jnp.concatenate(parts, axis=1)


def dot(a, b):
    return jnp.dot(a, b, preferred_element_type=jnp.float32)


def grid_indices():
    shape = (4, NX, J, 128)
    z, x, j = (iota(shape, d).reshape(ROWS, 128) for d in range(3))
    return z, x, j


def face_indices():
    r = iota((FACE, 128), 0)
    z = (r >= NX).astype(jnp.int32) + (r >= 2 * NX) + (r >= 3 * NX)
    return z, r - NX * z


def write_by_parity(axis, low, high, first, second):
    even = lax.axis_index(axis) % 2 == 0
    first[...] = jnp.where(even, high, low)
    second[...] = jnp.where(even, low, high)


def read_by_parity(axis, first, second):
    me, count = lax.axis_index(axis), lax.axis_size(axis)
    even = me % 2 == 0
    a, b = first[...], second[...]
    nothing = jnp.zeros_like(a)
    low = jnp.where(me > 0, jnp.where(even, b, a), nothing)
    high = jnp.where(me < count - 1, jnp.where(even, a, b), nothing)
    return low, high


def entry_of(lists):
    entries = lists[0]

    def entry(i):
        return jnp.sum(jnp.where(iota(entries.shape, 1) == i, entries, 0), axis=1, keepdims=True)

    return entry


def faces_kernel(lists, f, g, first, second, held, both, sems):
    count = f.shape[0]
    copies = [
        pltpu.make_async_copy(lists, held, sems.at[0]),
        pltpu.make_async_copy(f, both.at[pl.ds(0, count), pl.ds(0, 128)], sems.at[1]),
        pltpu.make_async_copy(g, both.at[pl.ds(0, count), pl.ds(128, 128)], sems.at[2]),
    ]
    for copy in copies:
        copy.start()
    both[count:, :] = jnp.zeros((both.shape[0] - count, 256), jnp.bfloat16)
    z, x = face_indices()
    copies[0].wait()
    slots = position_slots(entry_of(held), 0)
    picks = [
        one_hot(slot_rows(slots, z, x, jnp.full_like(x, y), x >= 0), both.shape[0]) for y in (0, NY - 1)
    ]
    for copy in copies[1:]:
        copy.wait()
    low, high = (dot(pick, both[...]).astype(jnp.bfloat16) for pick in picks)
    write_by_parity("wire", low, high, first, second)


def place_kernel(counts, lists, pair, out, live, both):
    count = pair.shape[0]
    both[0:count, :] = pair[...]
    both[count:, :] = jnp.zeros((both.shape[0] - count, 256), jnp.bfloat16)
    slots = position_slots(entry_of(lists), counts[...])
    z, x, j = grid_indices()
    rows = slot_rows(slots, z, x, j - 1, (j >= 1) & (j <= NY))
    live[...] = (rows >= 0).astype(jnp.bfloat16)
    out[...] = dot(one_hot(rows, both.shape[0]), both[...]).astype(jnp.bfloat16)


def insert_faces(placed, got_second, got_first, out, slab_first, slab_second, faces):
    low, high = read_by_parity("wire", got_first, got_second)
    faces[0:FACE, :] = low
    faces[FACE : 2 * FACE, :] = high
    faces[2 * FACE :, :] = jnp.zeros((faces.shape[0] - 2 * FACE, 256), jnp.bfloat16)
    z, x, j = grid_indices()
    rows = z * NX + x
    rows = jnp.where(j == 0, rows, jnp.where(j == NY + 1, rows + FACE, -1))
    full = (placed[...].astype(jnp.float32) + dot(one_hot(rows, 128), faces[...])).astype(jnp.bfloat16)
    out[...] = full
    low = jnp.concatenate([full[z * PLANE : z * PLANE + J, :] for z in range(4)], axis=0)
    high = jnp.concatenate([full[(z + 1) * PLANE - J : (z + 1) * PLANE, :] for z in range(4)], axis=0)
    write_by_parity("drift", low, high, slab_first, slab_second)


def insert_hidden_faces(placed, got_first, got_second, *refs):
    insert_faces(placed, got_second, got_first, *refs)


def build_window(window, base, plane_of):
    for zi in range(4):
        plane = plane_of(zi)
        wide = plane.astype(jnp.float32)
        before = pltpu.roll(wide, 1, 0).astype(jnp.bfloat16)
        after = pltpu.roll(wide, plane.shape[0] - 1, 0).astype(jnp.bfloat16)
        for oy, shifted in enumerate((before, plane, after)):
            for z in range(max(0, zi - 1), min(3, zi + 1) + 1):
                lane = 128 * (3 * oy + zi - z + 1)
                window[base + z, :, lane : lane + 128] = shifted
    empty = jnp.zeros((plane.shape[0], 128), jnp.bfloat16)
    for oy in range(3):
        window[base, :, 384 * oy : 384 * oy + 128] = empty
        window[base + 3, :, 384 * oy + 256 : 384 * oy + 384] = empty


def wide_plane(full, low, high, z, lanes):
    return jnp.concatenate(
        [
            low[z * J : (z + 1) * J, lanes],
            full[z * PLANE : (z + 1) * PLANE, lanes],
            high[z * J : (z + 1) * J, lanes],
        ],
        axis=0,
    )


def conv(window, weights, base):
    total = None
    for ox in range(3):
        rows = window[:, ox * J : ox * J + PLANE, :].reshape(ROWS, 1152)
        term = dot(rows, weights[base + 9 * ox : base + 9 * (ox + 1)].reshape(1152, 128))
        total = term if total is None else total + term
    return total


def flip_blocks(weights, base, flipped):
    for k in range(TAPS):
        flipped[:, 128 * k : 128 * (k + 1)] = weights[base + TAPS - 1 - k]


def conv_flipped(window, flipped):
    total = None
    for ox in range(3):
        rows = window[:, ox * J : ox * J + PLANE, :].reshape(ROWS, 1152)
        term = lax.dot_general(
            rows,
            flipped[:, 1152 * ox : 1152 * (ox + 1)],
            (((1,), (1,)), ((), ())),
            preferred_element_type=jnp.float32,
        )
        total = term if total is None else total + term
    return total


def inner_kernel(full, weights, pre, window):
    edge = jnp.zeros((SLAB, 128), jnp.bfloat16)
    build_window(window, 0, lambda z: wide_plane(full, edge, edge, z, slice(0, 128)))
    pre[...] = conv(window, weights, 0)


def add_edges(pre, low, high, weights, edge_window):
    for ox, x, slab in ((0, 0, low), (2, NX - 1, high)):
        build_window(edge_window, 0, lambda z: slab[z * J : (z + 1) * J, :])
        taps = weights[9 * ox : 9 * (ox + 1)].reshape(1152, 128)
        term = dot(edge_window[...].reshape(SLAB, 1152), taps)
        for z in range(4):
            start = z * PLANE + x * J
            pre[start : start + J, :] += term[z * J : (z + 1) * J, :]


def first_kernel(full, got_first, got_second, live, weights, inner, hb, keep, send, window, flipped, edge_window, pre):
    f_lanes, g_lanes = slice(0, 128), slice(128, 256)
    low, high = read_by_parity("drift", got_first, got_second)
    alive = live[...].astype(jnp.float32)
    flip_blocks(weights, TAPS, flipped)
    pre[...] = inner[...]
    add_edges(pre, low[:, f_lanes], high[:, f_lanes], weights, edge_window)
    first_pre = pre[...]
    gate = jax.nn.sigmoid(first_pre)
    hidden = (alive * (first_pre * gate)).astype(jnp.bfloat16)
    slope = alive * (gate * (1.0 + first_pre * (1.0 - gate)))
    build_window(window, 0, lambda z: wide_plane(full, low, high, z, g_lanes))
    back = (conv_flipped(window, flipped) * slope).astype(jnp.bfloat16)
    hb[...] = jnp.concatenate([hidden, back], axis=1)
    core = lax.axis_index("drift") % 2

    def write(to, values, lanes):
        to[0:ROWS, :] = values
        for z in range(4):
            start = ROWS + z * WIDE
            to[start : start + WIDE, :] = wide_plane(full, low, high, z, lanes)

    @pl.when(core == 0)
    def _():
        write(keep, hidden, g_lanes)
        write(send, back, f_lanes)

    @pl.when(core != 0)
    def _():
        write(keep, back, f_lanes)
        write(send, hidden, g_lanes)


def chip_mask(kind, core):
    if isinstance(kind, int):
        return kind
    first = 1 + core
    return {"own": 0, "first": first, "second": 3 - first, "opposite": 3}[kind]


def left_rows(part):
    return part[0:ROWS, :].astype(jnp.float32).T.astype(jnp.bfloat16)


def term_planes(part):
    return lambda z: part[ROWS + z * WIDE : ROWS + (z + 1) * WIDE, :]


def add_terms(left, window, add_block):
    for ox in range(3):
        shifted = window[:, ox * J : ox * J + PLANE, :].reshape(ROWS, 1152)
        product = dot(left, shifted)
        for k in range(9):
            add_block(128 * (9 * ox + k), product[:, 128 * k : 128 * (k + 1)])


def own_terms_kernel(mine, total, window):
    rows = TAPS * CHANNELS
    if total.shape[0] > rows:
        total[rows:, :] = jnp.zeros((total.shape[0] - rows, 128), jnp.float32)
    build_window(window, 0, term_planes(mine))

    def put(start, block):
        total[start : start + 128, :] = block

    add_terms(left_rows(mine), window, put)


def lead_terms_kernel(blocks, kind, mine, theirs, out, left, window):
    build_window(window, 0, term_planes(theirs))
    left[...] = left_rows(theirs)
    me, core = lax.axis_index("drift") // 2, lax.axis_index("drift") % 2
    lead = (me ^ chip_mask(kind, core)) * blocks
    columns = []
    for i in range(blocks):
        tap = jnp.minimum(lead + i, TAPS - 1)
        row = pl.multiple_of(tap // 9 * J, J)
        lane = pl.multiple_of(tap % 9 * 128, 128)
        columns.append(window[:, pl.ds(row, PLANE), pl.ds(lane, 128)].reshape(ROWS, 128))
    product = dot(left[...], jnp.concatenate(columns, axis=1))
    for i in range(blocks):
        held = mine[pl.ds(pl.multiple_of((lead + i) * 128, 128), 128), :]
        term = product[:, 128 * i : 128 * (i + 1)]
        out[128 * i : 128 * (i + 1), :] = (held + jnp.where(lead + i < TAPS, term, 0.0)).astype(out.dtype)


def terms_kernel(chunk, kinds, mine, left, window, hb, *refs):
    *outs, first, second, total = refs
    rows = TAPS * CHANNELS
    if total.shape[0] > rows:
        total[rows:, :] = mine[rows:, :]

    def put(start, block):
        total[start : start + 128, :] = mine[start : start + 128, :] + block

    add_terms(left[...], window, put)
    me, core = lax.axis_index("drift") // 2, lax.axis_index("drift") % 2
    for kind, out in zip(kinds, outs):
        start = pl.multiple_of((me ^ chip_mask(kind, core)) * chunk, 128)
        out[...] = total[pl.ds(start, chunk), :].astype(out.dtype)
    z, x = face_indices()
    start = z * PLANE + x * J
    low, high = (dot(one_hot(start + j, ROWS), hb[...]).astype(jnp.bfloat16) for j in (1, NY))
    write_by_parity("wire", low, high, first, second)


def passed_on_kernel(partial, received, out):
    out[...] = (partial[...] + received[...].astype(jnp.float32)).astype(jnp.bfloat16)


def relay_kernel(after, value, out):
    out[...] = value[...]


def split_kernel(unit, count, after, own, *refs):
    received, (*sends, rest, total) = refs[:count], refs[count:]
    summed = own[...]
    for part in received:
        summed = summed + part[...].astype(jnp.float32)
    total[...] = summed
    me = lax.axis_index("wire")
    rest[...] = total[pl.ds(pl.multiple_of(me * unit, 16), unit), :]
    for step, out in enumerate(sends):
        start = pl.multiple_of((me ^ (step + 1)) * unit, 16)
        out[...] = total[pl.ds(start, unit), :].astype(jnp.bfloat16)


def sum_kernel(scale, after, own, *refs):
    *received, out = refs
    summed = own[...]
    for part in received:
        summed = summed + part[...].astype(jnp.float32)
    out[...] = (summed * scale).astype(jnp.bfloat16)


def joined_kernel(unit, after, *refs):
    *parts, out = refs
    me = lax.axis_index("wire")
    for step, part in enumerate(parts):
        start = pl.multiple_of((me ^ step) * unit, 16)
        out[pl.ds(start, unit), :] = part[...]


def final_kernel(items, blocks, want_done, *refs):
    parts = refs[: len(items)]
    first, second, *done, staged, sems = refs[len(refs) - 4 - want_done :]
    me = lax.axis_index("drift") // 2
    for ref in done:
        ref[...] = jnp.zeros_like(ref)

    def write(core):
        copies = []
        for part, (kind, mine) in zip(parts, items):
            source = core if mine else 1 - core
            count, here = part.shape[0] // 128, len(copies)
            chunk = me ^ chip_mask(kind, source)
            for i in range(count):
                block = part[128 * i : 128 * (i + 1), :].astype(jnp.float32)
                staged[here + i] = block.T if source else block
                tap = chunk * blocks + i
                safe = jnp.minimum(tap, TAPS - 1)
                to = first.at[safe] if source else second.at[TAPS - 1 - safe]
                copies.append((tap < TAPS, pltpu.make_async_copy(staged.at[here + i], to, sems.at[here + i])))
                pl.when(copies[-1][0])(copies[-1][1].start)
        for used, copy in copies:
            pl.when(used)(copy.wait)

    even = lax.axis_index("drift") % 2 == 0
    pl.when(even)(lambda: write(0))
    pl.when(jnp.logical_not(even))(lambda: write(1))


def second_inner_kernel(field, hb, weights, inner, done, window, *flipped):
    edge = jnp.zeros((SLAB, 256), jnp.bfloat16)
    build_window(window, 0, lambda z: wide_plane(hb, edge, edge, z, slice(128 * field, 128 * (field + 1))))
    if field:
        flip_blocks(weights, 0, *flipped)
        inner[...] = conv_flipped(window, *flipped)
    else:
        inner[...] = conv(window, weights, TAPS)
    done[...] = jnp.zeros_like(done)


def second_kernel(
    lists, counts, inner_hidden, inner_back, got_first, got_second, base, live, weights, held, output, grad, passed, edge_window, pre, taps
):
    low, high = read_by_parity("drift", got_first, got_second)
    results = []
    for field in (0, 1):
        lanes = slice(128 * field, 128 * (field + 1))
        pre[...] = inner_back[...] if field else inner_hidden[...]
        if field:
            for k in (*range(9), *range(18, 27)):
                taps[k] = weights[TAPS - 1 - k].astype(jnp.float32).T.astype(jnp.bfloat16)
            add_edges(pre, low[:, lanes], high[:, lanes], taps, edge_window)
        else:
            add_edges(pre, low[:, lanes], high[:, lanes], weights.at[TAPS:], edge_window)
        value = base[:, lanes].astype(jnp.float32) + pre[...]
        results.append((live[...].astype(jnp.float32) * value).astype(jnp.bfloat16))
    both = jnp.concatenate(results, axis=1)
    slots = position_slots(lambda i: lists[0, 0, i], counts[0, 0])
    count = output.shape[0]
    pieces = []
    row = iota((count, 128), 0)
    for c in range(ROWS // 128):
        col = iota((8, 128), 1) + 128 * c
        z = (col >= PLANE).astype(jnp.int32) + (col >= 2 * PLANE) + (col >= 3 * PLANE)
        rest = col - PLANE * z
        x, j = rest >> 4, rest & 15
        source = slot_rows(slots, z, x, j - 1, (j >= 1) & (j <= NY))
        source = jnp.broadcast_to(source[0:1, :], (count, 128))
        pieces.append(jnp.where(row == source, 1.0, 0.0).astype(jnp.bfloat16))
    by_slot = dot(jnp.concatenate(pieces, axis=1), both).astype(jnp.bfloat16)
    output[...] = by_slot[:, 0:128]
    grad[...] = by_slot[:, 128:256]
    passed[...] = held[...]


def pairs(value_first, value_second, axis):
    drift, wire = lax.axis_size("drift"), lax.axis_size("wire")
    count = lax.axis_size(axis)
    first = [(i, i ^ 1) for i in range(count) if i ^ 1 < count]
    second = {i: i + 1 if i % 2 else i - 1 for i in range(1, count - 1)}
    if axis == "drift":
        second.update({0: count - 1, count - 1: 0})
        got_second = lax.ppermute(value_second, axis, sorted(second.items()))
    else:
        moves = [
            (d * wire + w, d * wire + second[w] if w in second else (d ^ 1) * wire + w)
            for d in range(drift)
            for w in range(wire)
        ]
        got_second = lax.ppermute(value_second, ("drift", "wire"), moves)
    got_first = lax.ppermute(value_first, axis, first)
    return got_first, got_second


def on_device(features, first_weight, second_weight, cotangent, counts, kernel_map, send_lists):
    drift, wire = lax.axis_size("drift"), lax.axis_size("wire")
    chips = drift // 2
    blocks = -(-TAPS // chips)
    chunk = blocks * CHANNELS
    unit = chunk // wire
    rows = TAPS * CHANNELS
    f, g = features[0, 0], cotangent[0, 0]
    slots = f.shape[0]
    padded = -(-slots // 128) * 128
    conv_scratch = [pltpu.VMEM((4, WIDE, 1152), jnp.bfloat16), pltpu.VMEM((128, rows), jnp.bfloat16)]
    edge_window = pltpu.VMEM((4, J, 1152), jnp.bfloat16)
    faces_scratch = pltpu.VMEM((128, 256), jnp.bfloat16)
    face, slab, grid = bf16(FACE, 256), bf16(SLAB, 256), bf16(ROWS, 256)

    def swap_core(value):
        return lax.ppermute(value, "drift", [(i, i ^ 1) for i in range(drift)])

    def to_chip(value, kind):
        return lax.ppermute(value, "drift", [(i, i ^ (2 * chip_mask(kind, i % 2))) for i in range(drift)])

    def to_wire(value, step):
        return lax.ppermute(value, "wire", [(i, i ^ step) for i in range(wire)])

    pair = jnp.concatenate([f, g], axis=1)
    weights = jnp.concatenate([first_weight, second_weight], axis=0)
    pair_scratch = [pltpu.VMEM((padded, 256), jnp.bfloat16)]
    faces = call(
        faces_kernel,
        (face, face),
        [HBM] * 3,
        [pltpu.VMEM(send_lists.shape, jnp.int32)] + pair_scratch + [pltpu.SemaphoreType.DMA((3,))],
        vmem=60,
    )(send_lists, f, g)
    placed, live = call(place_kernel, (grid, bf16(ROWS, 128)), [VMEM] * 3, pair_scratch)(counts, send_lists, pair)
    faces = pairs(*faces, "wire")
    full, *slabs = call(insert_faces, (grid, slab, slab), [VMEM] * 3, [faces_scratch])(placed, *faces[::-1])
    slabs = pairs(*slabs, "drift")
    message = bf16(ROWS + 4 * WIDE, 128)
    inner = call(inner_kernel, f32(ROWS, 128), [VMEM] * 2, conv_scratch[:1])(full, weights)
    hb, keep, send = call(
        first_kernel,
        (grid, message, message),
        [VMEM] * 6,
        conv_scratch + [edge_window, pltpu.VMEM((ROWS, 128), jnp.float32)],
    )(full, *slabs, live, weights, inner)
    got = swap_core(send)
    term_window = pltpu.VMEM((4, WIDE, 1152), jnp.bfloat16)
    terms = f32(chunk * chips, 128)
    own_terms = call(own_terms_kernel, terms, [VMEM], [term_window])(keep)
    four = chips == 4
    kinds = ("opposite", "first", "second", "own") if four else (*range(1, chips), 0)
    shapes = [f32(chunk, 128) if k in ("second", "own", 0) else bf16(chunk, 128) for k in kinds]
    lead, left, held_window = call(
        functools.partial(lead_terms_kernel, blocks, kinds[0]),
        (shapes[0], bf16(128, ROWS), bf16(4, WIDE, 1152)),
        [VMEM] * 2,
    )(own_terms, got)
    *sends, own, face_first, face_second = call(
        functools.partial(terms_kernel, chunk, kinds[1:]),
        (*shapes[1:], face, face),
        [VMEM] * 4,
        [pltpu.VMEM(terms.shape, jnp.float32)],
    )(own_terms, left, held_window, hb)
    sends = [lead] + sends
    if four:
        opposite, first, second_part = sends
        passed = to_chip(opposite, "first")
        parts = [to_chip(first, "first")]
        passed = call(passed_on_kernel, bf16(chunk, 128), [VMEM] * 2)(second_part, passed)
        parts.append(to_chip(passed, "second"))
    else:
        parts = [to_chip(value, k) for k, value in zip(kinds, sends)]
    faces = pairs(face_first, face_second, "wire")
    hb_full, *hb_slabs = call(insert_hidden_faces, (grid, slab, slab), [VMEM] * 3, [faces_scratch])(hb, *faces)
    inserted = hb_slabs[0]
    hb_slabs = pairs(*hb_slabs, "drift")
    token = f32(8, 128)
    (inner_hidden, hidden_done), (inner_back, back_done) = (
        call(
            functools.partial(second_inner_kernel, field),
            (f32(ROWS, 128), token),
            [VMEM] * 2,
            conv_scratch[: 1 + field],
        )(hb_full, weights)
        for field in (0, 1)
    )
    *sends, own = call(
        functools.partial(split_kernel, unit, len(parts)),
        tuple([bf16(unit, 128)] * (wire - 1) + [f32(unit, 128)]),
        [VMEM] * (2 + len(parts)),
        [pltpu.VMEM((chunk, 128), jnp.float32)],
    )(inserted, own, *parts)

    received = [to_wire(sends[k - 1], k) for k in reversed(range(1, wire))]
    scale = 1.0 / math.sqrt(float(drift * wire * slots))
    summed = call(functools.partial(sum_kernel, scale), bf16(unit, 128), [VMEM] * (1 + wire))(
        hidden_done, own, *received
    )
    pieces = [summed] + [to_wire(summed, k) for k in range(1, wire)]
    mine = call(functools.partial(joined_kernel, unit), bf16(chunk, 128), [VMEM] * (1 + wire))(back_done, *pieces)
    output, grad_features, passed = call(
        second_kernel,
        (bf16(slots, 128), bf16(slots, 128), bf16(chunk, 128)),
        [SMEM] * 2 + [VMEM] * 8,
        [edge_window, pltpu.VMEM((ROWS, 128), jnp.float32), pltpu.VMEM((TAPS, 128, 128), jnp.bfloat16)],
    )(send_lists, counts, inner_hidden, inner_back, *hb_slabs, full, live, weights, mine)
    if four:
        brought = {"own": mine, "first": to_chip(mine, "first"), "second": to_chip(passed, "second")}
        brought["opposite"] = to_chip(brought["first"], "second")
        early = [
            [("own", True), ("own", False), ("first", True)],
            [("second", True), ("first", False), ("second", False)],
        ]
        last = "opposite"
    else:
        brought = {k: to_chip(passed if k > 1 else mine, k) if k else mine for k in range(chips)}
        last = chips - 1
        early = [[(k, True) for k in range(last)] + [(k, False) for k in range(last)]]
    late = [[(last, True)], [(last, False)]]
    swapped = {kind: swap_core(value) for kind, value in brought.items() if kind != last}
    grads = ()
    for n, items in enumerate(early + late):
        if n == len(early):
            held = call(relay_kernel, bf16(*brought[last].shape), [VMEM] * 2)(done, brought[last])
            swapped[last] = swap_core(held)
        values = [(brought if own_core else swapped)[kind] for kind, own_core in items]
        staged = sum(value.shape[0] for value in values) // CHANNELS
        want_done = n == len(early) - 1
        *grads, done = (
            *call(
                functools.partial(final_kernel, items, blocks, want_done),
                (f32(TAPS, 128, 128), f32(TAPS, 128, 128)) + (token,) * want_done,
                [VMEM] * len(items) + [HBM] * len(grads),
                [pltpu.VMEM((staged, 128, 128), jnp.float32), pltpu.SemaphoreType.DMA((staged,))],
                50 * 10**9,
                (HBM, HBM) + (VMEM,) * want_done,
                {len(items): 0, len(items) + 1: 1} if grads else {},
            )(*values, *grads),
            *(() if want_done else (None,)),
        )
    grad_first, grad_second = grads
    return output[None, None], grad_features[None, None], grad_first, grad_second


def solution(mesh):
    placed = (
        P("drift", "wire", None, None),
        P(),
        P(),
        P("drift", "wire", None, None),
        P("drift", "wire"),
        P("drift", "wire", None, None),
        P("drift", "wire", None),
    )
    return jax.shard_map(
        on_device,
        mesh=mesh,
        in_specs=placed,
        out_specs=(P("drift", "wire", None, None), P("drift", "wire", None, None), P(), P()),
        check_vma=False,
    )
```

```python
import functools
import math

import jax
import jax.numpy as jnp
from jax import lax
from jax.experimental import pallas as pl
from jax.experimental.pallas import tpu as pltpu
from jax.sharding import PartitionSpec as P

BX = 3
BW = 3
NX = 4 * BX
NY = 4 * BW
J = 16
PLANE = NX * J
WIDE = (NX + 2) * J
ROWS = 4 * PLANE
FACE = 4 * NX
SLAB = 4 * J
CHANNELS = 128
TAPS = 27
VMEM = pl.BlockSpec(memory_space=pltpu.VMEM)
HBM = pl.BlockSpec(memory_space=pltpu.HBM)
SMEM = pl.BlockSpec(memory_space=pltpu.SMEM)
LISTED = {0: 0, 1: 1, 2: 2, 3: 7, 5: 10, 6: 3, 7: 4, 8: 5}


def call(kernel, out_shape, in_specs, scratch=(), flops=0, out_spec=VMEM, aliases={}, vmem=40):
    return pl.pallas_call(
        kernel,
        out_shape=out_shape,
        in_specs=in_specs,
        out_specs=out_spec if isinstance(out_spec, tuple) else jax.tree.map(lambda _: out_spec, out_shape),
        scratch_shapes=list(scratch),
        input_output_aliases=aliases,
        compiler_params=pltpu.CompilerParams(vmem_limit_bytes=vmem * 1024 * 1024),
        cost_estimate=pl.CostEstimate(
            flops=flops, bytes_accessed=0, transcendentals=0
        ),
    )


def bf16(*shape):
    return jax.ShapeDtypeStruct(shape, jnp.bfloat16)


def f32(*shape):
    return jax.ShapeDtypeStruct(shape, jnp.float32)


def iota(shape, dim):
    return lax.broadcasted_iota(jnp.int32, shape, dim)


def position_slots(listed, count):
    slots = {p: listed(i) for p, i in LISTED.items()}
    present = {p: (s < 9).astype(jnp.int32) for p, s in slots.items()}
    before = present[0] + present[1] + present[2] + present[3]
    others = before + present[5] + present[6] + present[7] + present[8]
    slots[4] = jnp.where(count > others, before, 9)
    return slots


def slot_rows(slots, z, x, y, valid):
    position = (x >> 2) * BW + (y >> 2)
    slot = jnp.full(position.shape, 9, jnp.int32)
    for p, s in slots.items():
        slot = jnp.where(position == p, s, slot)
    row = slot * 64 + (x & 3) * 16 + (y & 3) * 4 + z
    return jnp.where(valid & (slot < 9), row, -1)


def one_hot(rows, width):
    lane = iota(rows.shape, 1)
    parts = [jnp.where(rows == lane + 128 * c, 1.0, 0.0).astype(jnp.bfloat16) for c in range(width // 128)]
    return jnp.concatenate(parts, axis=1)


def dot(a, b):
    return jnp.dot(a, b, preferred_element_type=jnp.float32)


def grid_indices():
    shape = (4, NX, J, 128)
    z, x, j = (iota(shape, d).reshape(ROWS, 128) for d in range(3))
    return z, x, j


def face_indices():
    r = iota((FACE, 128), 0)
    z = (r >= NX).astype(jnp.int32) + (r >= 2 * NX) + (r >= 3 * NX)
    return z, r - NX * z


def write_by_parity(axis, low, high, first, second):
    even = lax.axis_index(axis) % 2 == 0
    first[...] = jnp.where(even, high, low)
    second[...] = jnp.where(even, low, high)


def read_by_parity(axis, first, second):
    me, count = lax.axis_index(axis), lax.axis_size(axis)
    even = me % 2 == 0
    a, b = first[...], second[...]
    nothing = jnp.zeros_like(a)
    low = jnp.where(me > 0, jnp.where(even, b, a), nothing)
    high = jnp.where(me < count - 1, jnp.where(even, a, b), nothing)
    return low, high


def entry_of(lists):
    entries = lists[0]

    def entry(i):
        return jnp.sum(jnp.where(iota(entries.shape, 1) == i, entries, 0), axis=1, keepdims=True)

    return entry


def faces_kernel(lists, f, g, first, second, held, both, sems):
    count = f.shape[0]
    copies = [
        pltpu.make_async_copy(lists, held, sems.at[0]),
        pltpu.make_async_copy(f, both.at[pl.ds(0, count), pl.ds(0, 128)], sems.at[1]),
        pltpu.make_async_copy(g, both.at[pl.ds(0, count), pl.ds(128, 128)], sems.at[2]),
    ]
    for copy in copies:
        copy.start()
    both[count:, :] = jnp.zeros((both.shape[0] - count, 256), jnp.bfloat16)
    z, x = face_indices()
    copies[0].wait()
    slots = position_slots(entry_of(held), 0)
    picks = [
        one_hot(slot_rows(slots, z, x, jnp.full_like(x, y), x >= 0), both.shape[0]) for y in (0, NY - 1)
    ]
    for copy in copies[1:]:
        copy.wait()
    low, high = (dot(pick, both[...]).astype(jnp.bfloat16) for pick in picks)
    write_by_parity("wire", low, high, first, second)


def place_kernel(counts, lists, pair, out, live, both):
    count = pair.shape[0]
    both[0:count, :] = pair[...]
    both[count:, :] = jnp.zeros((both.shape[0] - count, 256), jnp.bfloat16)
    slots = position_slots(entry_of(lists), counts[...])
    z, x, j = grid_indices()
    rows = slot_rows(slots, z, x, j - 1, (j >= 1) & (j <= NY))
    live[...] = (rows >= 0).astype(jnp.bfloat16)
    out[...] = dot(one_hot(rows, both.shape[0]), both[...]).astype(jnp.bfloat16)


def insert_faces(placed, got_second, got_first, out, slab_first, slab_second, faces):
    low, high = read_by_parity("wire", got_first, got_second)
    faces[0:FACE, :] = low
    faces[FACE : 2 * FACE, :] = high
    faces[2 * FACE :, :] = jnp.zeros((faces.shape[0] - 2 * FACE, 256), jnp.bfloat16)
    z, x, j = grid_indices()
    rows = z * NX + x
    rows = jnp.where(j == 0, rows, jnp.where(j == NY + 1, rows + FACE, -1))
    full = (placed[...].astype(jnp.float32) + dot(one_hot(rows, 128), faces[...])).astype(jnp.bfloat16)
    out[...] = full
    low = jnp.concatenate([full[z * PLANE : z * PLANE + J, :] for z in range(4)], axis=0)
    high = jnp.concatenate([full[(z + 1) * PLANE - J : (z + 1) * PLANE, :] for z in range(4)], axis=0)
    write_by_parity("drift", low, high, slab_first, slab_second)


def insert_hidden_faces(placed, got_first, got_second, *refs):
    insert_faces(placed, got_second, got_first, *refs)


def build_window(window, base, plane_of):
    for zi in range(4):
        plane = plane_of(zi)
        wide = plane.astype(jnp.float32)
        before = pltpu.roll(wide, 1, 0).astype(jnp.bfloat16)
        after = pltpu.roll(wide, plane.shape[0] - 1, 0).astype(jnp.bfloat16)
        for oy, shifted in enumerate((before, plane, after)):
            for z in range(max(0, zi - 1), min(3, zi + 1) + 1):
                lane = 128 * (3 * oy + zi - z + 1)
                window[base + z, :, lane : lane + 128] = shifted
    empty = jnp.zeros((plane.shape[0], 128), jnp.bfloat16)
    for oy in range(3):
        window[base, :, 384 * oy : 384 * oy + 128] = empty
        window[base + 3, :, 384 * oy + 256 : 384 * oy + 384] = empty


def wide_plane(full, low, high, z, lanes):
    return jnp.concatenate(
        [
            low[z * J : (z + 1) * J, lanes],
            full[z * PLANE : (z + 1) * PLANE, lanes],
            high[z * J : (z + 1) * J, lanes],
        ],
        axis=0,
    )


def conv(window, weights, base):
    total = None
    for ox in range(3):
        rows = window[:, ox * J : ox * J + PLANE, :].reshape(ROWS, 1152)
        term = dot(rows, weights[base + 9 * ox : base + 9 * (ox + 1)].reshape(1152, 128))
        total = term if total is None else total + term
    return total


def flip_blocks(weights, base, flipped):
    for k in range(TAPS):
        flipped[:, 128 * k : 128 * (k + 1)] = weights[base + TAPS - 1 - k]


def conv_flipped(window, flipped):
    total = None
    for ox in range(3):
        rows = window[:, ox * J : ox * J + PLANE, :].reshape(ROWS, 1152)
        term = lax.dot_general(
            rows,
            flipped[:, 1152 * ox : 1152 * (ox + 1)],
            (((1,), (1,)), ((), ())),
            preferred_element_type=jnp.float32,
        )
        total = term if total is None else total + term
    return total


def inner_kernel(full, weights, pre, back, flipped, window):
    edge = jnp.zeros((SLAB, 256), jnp.bfloat16)
    flip_blocks(weights, TAPS, flipped)
    build_window(window, 0, lambda z: wide_plane(full, edge, edge, z, slice(0, 128)))
    pre[...] = conv(window, weights, 0)
    build_window(window, 0, lambda z: wide_plane(full, edge, edge, z, slice(128, 256)))
    back[...] = conv_flipped(window, flipped)


def add_edges(pre, low, high, edge_window, taps_dot):
    for ox, x, slab in ((0, 0, low), (2, NX - 1, high)):
        build_window(edge_window, 0, lambda z: slab[z * J : (z + 1) * J, :])
        term = taps_dot(edge_window[...].reshape(SLAB, 1152), ox)
        for z in range(4):
            start = z * PLANE + x * J
            pre[start : start + J, :] += term[z * J : (z + 1) * J, :]


def taps_of(weights):
    return lambda rows, ox: dot(rows, weights[9 * ox : 9 * (ox + 1)].reshape(1152, 128))


def flipped_taps_of(flipped):
    return lambda rows, ox: lax.dot_general(
        rows,
        flipped[:, 1152 * ox : 1152 * (ox + 1)],
        (((1,), (1,)), ((), ())),
        preferred_element_type=jnp.float32,
    )


def first_kernel(full, got_second, got_first, live, weights, inner, inner_back, flipped, hb, keep, send, edge_window, pre):
    f_lanes, g_lanes = slice(0, 128), slice(128, 256)
    low, high = read_by_parity("drift", got_first, got_second)
    alive = live[...].astype(jnp.float32)
    pre[...] = inner[...]
    add_edges(pre, low[:, f_lanes], high[:, f_lanes], edge_window, taps_of(weights))
    first_pre = pre[...]
    gate = jax.nn.sigmoid(first_pre)
    hidden = (alive * (first_pre * gate)).astype(jnp.bfloat16)
    slope = alive * (gate * (1.0 + first_pre * (1.0 - gate)))
    pre[...] = inner_back[...]
    add_edges(pre, low[:, g_lanes], high[:, g_lanes], edge_window, flipped_taps_of(flipped))
    back = (pre[...] * slope).astype(jnp.bfloat16)
    hb[...] = jnp.concatenate([hidden, back], axis=1)
    core = lax.axis_index("drift") % 2

    def write(to, values, lanes):
        to[0:ROWS, :] = values
        for z in range(4):
            start = ROWS + z * WIDE
            to[start : start + WIDE, :] = wide_plane(full, low, high, z, lanes)

    @pl.when(core == 0)
    def _():
        write(keep, hidden, g_lanes)
        write(send, back, f_lanes)

    @pl.when(core != 0)
    def _():
        write(keep, back, f_lanes)
        write(send, hidden, g_lanes)


def chip_mask(kind, core):
    if isinstance(kind, int):
        return kind
    first = 1 + core
    return {"own": 0, "first": first, "second": 3 - first, "opposite": 3}[kind]


def left_rows(part):
    return part[0:ROWS, :].astype(jnp.float32).T.astype(jnp.bfloat16)


def term_planes(part):
    return lambda z: part[ROWS + z * WIDE : ROWS + (z + 1) * WIDE, :]


def add_terms(left, window, add_block):
    for ox in range(3):
        shifted = window[:, ox * J : ox * J + PLANE, :].reshape(ROWS, 1152)
        product = dot(left, shifted)
        for k in range(9):
            add_block(128 * (9 * ox + k), product[:, 128 * k : 128 * (k + 1)])


def own_terms_kernel(mine, total, window):
    rows = TAPS * CHANNELS
    if total.shape[0] > rows:
        total[rows:, :] = jnp.zeros((total.shape[0] - rows, 128), jnp.float32)
    build_window(window, 0, term_planes(mine))

    def put(start, block):
        total[start : start + 128, :] = block

    add_terms(left_rows(mine), window, put)


def lead_terms_kernel(blocks, kind, mine, theirs, out, left, window):
    build_window(window, 0, term_planes(theirs))
    left[...] = left_rows(theirs)
    me, core = lax.axis_index("drift") // 2, lax.axis_index("drift") % 2
    lead = (me ^ chip_mask(kind, core)) * blocks
    columns = []
    for i in range(blocks):
        tap = jnp.minimum(lead + i, TAPS - 1)
        row = pl.multiple_of(tap // 9 * J, J)
        lane = pl.multiple_of(tap % 9 * 128, 128)
        columns.append(window[:, pl.ds(row, PLANE), pl.ds(lane, 128)].reshape(ROWS, 128))
    product = dot(left[...], jnp.concatenate(columns, axis=1))
    for i in range(blocks):
        held = mine[pl.ds(pl.multiple_of((lead + i) * 128, 128), 128), :]
        term = product[:, 128 * i : 128 * (i + 1)]
        out[128 * i : 128 * (i + 1), :] = (held + jnp.where(lead + i < TAPS, term, 0.0)).astype(out.dtype)


def terms_kernel(chunk, kinds, mine, left, window, hb, *refs):
    *outs, first, second, total = refs
    rows = TAPS * CHANNELS
    if total.shape[0] > rows:
        total[rows:, :] = mine[rows:, :]

    def put(start, block):
        total[start : start + 128, :] = mine[start : start + 128, :] + block

    add_terms(left[...], window, put)
    me, core = lax.axis_index("drift") // 2, lax.axis_index("drift") % 2
    for kind, out in zip(kinds, outs):
        start = pl.multiple_of((me ^ chip_mask(kind, core)) * chunk, 128)
        out[...] = total[pl.ds(start, chunk), :].astype(out.dtype)
    z, x = face_indices()
    start = z * PLANE + x * J
    low, high = (dot(one_hot(start + j, ROWS), hb[...]).astype(jnp.bfloat16) for j in (1, NY))
    write_by_parity("wire", low, high, first, second)


def passed_on_kernel(partial, received, out):
    out[...] = (partial[...] + received[...].astype(jnp.float32)).astype(jnp.bfloat16)


def relay_kernel(after, value, out):
    out[...] = value[...]


def split_kernel(unit, count, after, own, *refs):
    received, (*sends, rest, total) = refs[:count], refs[count:]
    summed = own[...]
    for part in received:
        summed = summed + part[...].astype(jnp.float32)
    total[...] = summed
    me = lax.axis_index("wire")
    rest[...] = total[pl.ds(pl.multiple_of(me * unit, 16), unit), :]
    for step, out in enumerate(sends):
        start = pl.multiple_of((me ^ (step + 1)) * unit, 16)
        out[...] = total[pl.ds(start, unit), :].astype(jnp.bfloat16)


def sum_kernel(scale, after, own, *refs):
    *received, out = refs
    summed = own[...]
    for part in received:
        summed = summed + part[...].astype(jnp.float32)
    out[...] = (summed * scale).astype(jnp.bfloat16)


def joined_kernel(unit, after, *refs):
    *parts, out = refs
    me = lax.axis_index("wire")
    for step, part in enumerate(parts):
        start = pl.multiple_of((me ^ step) * unit, 16)
        out[pl.ds(start, unit), :] = part[...]


def final_kernel(items, blocks, want_done, *refs):
    parts = refs[: len(items)]
    first, second, *done, staged, sems = refs[len(refs) - 4 - want_done :]
    me = lax.axis_index("drift") // 2
    for ref in done:
        ref[...] = jnp.zeros_like(ref)

    def write(core):
        copies = []
        for part, (kind, mine) in zip(parts, items):
            source = core if mine else 1 - core
            count, here = part.shape[0] // 128, len(copies)
            chunk = me ^ chip_mask(kind, source)
            for i in range(count):
                block = part[128 * i : 128 * (i + 1), :].astype(jnp.float32)
                staged[here + i] = block.T if source else block
                tap = chunk * blocks + i
                safe = jnp.minimum(tap, TAPS - 1)
                to = first.at[safe] if source else second.at[TAPS - 1 - safe]
                copies.append((tap < TAPS, pltpu.make_async_copy(staged.at[here + i], to, sems.at[here + i])))
                pl.when(copies[-1][0])(copies[-1][1].start)
        for used, copy in copies:
            pl.when(used)(copy.wait)

    even = lax.axis_index("drift") % 2 == 0
    pl.when(even)(lambda: write(0))
    pl.when(jnp.logical_not(even))(lambda: write(1))


def second_inner_kernel(field, hb, weights, inner, done, window, *flipped):
    edge = jnp.zeros((SLAB, 256), jnp.bfloat16)
    build_window(window, 0, lambda z: wide_plane(hb, edge, edge, z, slice(128 * field, 128 * (field + 1))))
    if field:
        flip_blocks(weights, 0, *flipped)
        inner[...] = conv_flipped(window, *flipped)
    else:
        inner[...] = conv(window, weights, TAPS)
    done[...] = jnp.zeros_like(done)


def second_kernel(
    lists, counts, inner_hidden, inner_back, got_first, got_second, base, live, weights, held, output, grad, passed, edge_window, pre, taps
):
    low, high = read_by_parity("drift", got_first, got_second)
    results = []
    for field in (0, 1):
        lanes = slice(128 * field, 128 * (field + 1))
        pre[...] = inner_back[...] if field else inner_hidden[...]
        if field:
            for k in (*range(9), *range(18, 27)):
                taps[k] = weights[TAPS - 1 - k].astype(jnp.float32).T.astype(jnp.bfloat16)
            add_edges(pre, low[:, lanes], high[:, lanes], edge_window, taps_of(taps))
        else:
            add_edges(pre, low[:, lanes], high[:, lanes], edge_window, taps_of(weights.at[TAPS:]))
        value = base[:, lanes].astype(jnp.float32) + pre[...]
        results.append((live[...].astype(jnp.float32) * value).astype(jnp.bfloat16))
    both = jnp.concatenate(results, axis=1)
    slots = position_slots(lambda i: lists[0, 0, i], counts[0, 0])
    count = output.shape[0]
    pieces = []
    row = iota((count, 128), 0)
    for c in range(ROWS // 128):
        col = iota((8, 128), 1) + 128 * c
        z = (col >= PLANE).astype(jnp.int32) + (col >= 2 * PLANE) + (col >= 3 * PLANE)
        rest = col - PLANE * z
        x, j = rest >> 4, rest & 15
        source = slot_rows(slots, z, x, j - 1, (j >= 1) & (j <= NY))
        source = jnp.broadcast_to(source[0:1, :], (count, 128))
        pieces.append(jnp.where(row == source, 1.0, 0.0).astype(jnp.bfloat16))
    by_slot = dot(jnp.concatenate(pieces, axis=1), both).astype(jnp.bfloat16)
    output[...] = by_slot[:, 0:128]
    grad[...] = by_slot[:, 128:256]
    passed[...] = held[...]


def pairs(value_first, value_second, axis):
    drift, wire = lax.axis_size("drift"), lax.axis_size("wire")
    count = lax.axis_size(axis)
    first = [(i, i ^ 1) for i in range(count) if i ^ 1 < count]
    second = {i: i + 1 if i % 2 else i - 1 for i in range(1, count - 1)}
    if axis == "drift":
        second.update({0: count - 1, count - 1: 0})
        got_second = lax.ppermute(value_second, axis, sorted(second.items()))
    else:
        moves = [
            (d * wire + w, d * wire + second[w] if w in second else (d ^ 1) * wire + w)
            for d in range(drift)
            for w in range(wire)
        ]
        got_second = lax.ppermute(value_second, ("drift", "wire"), moves)
    got_first = lax.ppermute(value_first, axis, first)
    return got_first, got_second


def on_device(features, first_weight, second_weight, cotangent, counts, kernel_map, send_lists):
    drift, wire = lax.axis_size("drift"), lax.axis_size("wire")
    chips = drift // 2
    blocks = -(-TAPS // chips)
    chunk = blocks * CHANNELS
    unit = chunk // wire
    rows = TAPS * CHANNELS
    f, g = features[0, 0], cotangent[0, 0]
    slots = f.shape[0]
    padded = -(-slots // 128) * 128
    conv_scratch = [pltpu.VMEM((4, WIDE, 1152), jnp.bfloat16), pltpu.VMEM((128, rows), jnp.bfloat16)]
    edge_window = pltpu.VMEM((4, J, 1152), jnp.bfloat16)
    faces_scratch = pltpu.VMEM((128, 256), jnp.bfloat16)
    face, slab, grid = bf16(FACE, 256), bf16(SLAB, 256), bf16(ROWS, 256)

    def swap_core(value):
        return lax.ppermute(value, "drift", [(i, i ^ 1) for i in range(drift)])

    def to_chip(value, kind):
        return lax.ppermute(value, "drift", [(i, i ^ (2 * chip_mask(kind, i % 2))) for i in range(drift)])

    def to_wire(value, step):
        return lax.ppermute(value, "wire", [(i, i ^ step) for i in range(wire)])

    pair = jnp.concatenate([f, g], axis=1)
    weights = jnp.concatenate([first_weight, second_weight], axis=0)
    pair_scratch = [pltpu.VMEM((padded, 256), jnp.bfloat16)]
    faces = call(
        faces_kernel,
        (face, face),
        [HBM] * 3,
        [pltpu.VMEM(send_lists.shape, jnp.int32)] + pair_scratch + [pltpu.SemaphoreType.DMA((3,))],
        vmem=60,
    )(send_lists, f, g)
    placed, live = call(place_kernel, (grid, bf16(ROWS, 128)), [VMEM] * 3, pair_scratch)(counts, send_lists, pair)
    faces = pairs(*faces, "wire")
    full, *slabs = call(insert_faces, (grid, slab, slab), [VMEM] * 3, [faces_scratch])(placed, *faces[::-1])
    slabs = pairs(*slabs, "drift")
    message = bf16(ROWS + 4 * WIDE, 128)
    inner = call(
        inner_kernel, (f32(ROWS, 128), f32(ROWS, 128), bf16(128, rows)), [VMEM] * 2, conv_scratch[:1]
    )(full, weights)
    hb, keep, send = call(
        first_kernel,
        (grid, message, message),
        [VMEM] * 8,
        [edge_window, pltpu.VMEM((ROWS, 128), jnp.float32)],
    )(full, *slabs[::-1], live, weights, *inner)
    got = swap_core(send)
    term_window = pltpu.VMEM((4, WIDE, 1152), jnp.bfloat16)
    terms = f32(chunk * chips, 128)
    own_terms = call(own_terms_kernel, terms, [VMEM], [term_window])(keep)
    four = chips == 4
    kinds = ("opposite", "first", "second", "own") if four else (*range(1, chips), 0)
    shapes = [f32(chunk, 128) if k in ("second", "own", 0) else bf16(chunk, 128) for k in kinds]
    lead, left, held_window = call(
        functools.partial(lead_terms_kernel, blocks, kinds[0]),
        (shapes[0], bf16(128, ROWS), bf16(4, WIDE, 1152)),
        [VMEM] * 2,
    )(own_terms, got)
    *sends, own, face_first, face_second = call(
        functools.partial(terms_kernel, chunk, kinds[1:]),
        (*shapes[1:], face, face),
        [VMEM] * 4,
        [pltpu.VMEM(terms.shape, jnp.float32)],
    )(own_terms, left, held_window, hb)
    sends = [lead] + sends
    if four:
        opposite, first, second_part = sends
        passed = to_chip(opposite, "first")
        parts = [to_chip(first, "first")]
        passed = call(passed_on_kernel, bf16(chunk, 128), [VMEM] * 2)(second_part, passed)
        parts.append(to_chip(passed, "second"))
    else:
        parts = [to_chip(value, k) for k, value in zip(kinds, sends)]
    faces = pairs(face_first, face_second, "wire")
    hb_full, *hb_slabs = call(insert_hidden_faces, (grid, slab, slab), [VMEM] * 3, [faces_scratch])(hb, *faces)
    inserted = hb_slabs[0]
    hb_slabs = pairs(*hb_slabs, "drift")
    token = f32(8, 128)
    (inner_hidden, hidden_done), (inner_back, back_done) = (
        call(
            functools.partial(second_inner_kernel, field),
            (f32(ROWS, 128), token),
            [VMEM] * 2,
            conv_scratch[: 1 + field],
        )(hb_full, weights)
        for field in (0, 1)
    )
    *sends, own = call(
        functools.partial(split_kernel, unit, len(parts)),
        tuple([bf16(unit, 128)] * (wire - 1) + [f32(unit, 128)]),
        [VMEM] * (2 + len(parts)),
        [pltpu.VMEM((chunk, 128), jnp.float32)],
    )(inserted, own, *parts)

    received = [to_wire(sends[k - 1], k) for k in reversed(range(1, wire))]
    scale = 1.0 / math.sqrt(float(drift * wire * slots))
    summed = call(functools.partial(sum_kernel, scale), bf16(unit, 128), [VMEM] * (1 + wire))(
        hidden_done, own, *received
    )
    pieces = [summed] + [to_wire(summed, k) for k in range(1, wire)]
    mine = call(functools.partial(joined_kernel, unit), bf16(chunk, 128), [VMEM] * (1 + wire))(back_done, *pieces)
    output, grad_features, passed = call(
        second_kernel,
        (bf16(slots, 128), bf16(slots, 128), bf16(chunk, 128)),
        [SMEM] * 2 + [VMEM] * 8,
        [edge_window, pltpu.VMEM((ROWS, 128), jnp.float32), pltpu.VMEM((TAPS, 128, 128), jnp.bfloat16)],
    )(send_lists, counts, inner_hidden, inner_back, *hb_slabs, full, live, weights, mine)
    if four:
        brought = {"own": mine, "first": to_chip(mine, "first"), "second": to_chip(passed, "second")}
        brought["opposite"] = to_chip(brought["first"], "second")
        early = [
            [("own", True), ("own", False), ("first", True)],
            [("second", True), ("first", False), ("second", False)],
        ]
        last = "opposite"
    else:
        brought = {k: to_chip(passed if k > 1 else mine, k) if k else mine for k in range(chips)}
        last = chips - 1
        early = [[(k, True) for k in range(last)] + [(k, False) for k in range(last)]]
    late = [[(last, True)], [(last, False)]]
    swapped = {kind: swap_core(value) for kind, value in brought.items() if kind != last}
    grads = ()
    for n, items in enumerate(early + late):
        if n == len(early):
            held = call(relay_kernel, bf16(*brought[last].shape), [VMEM] * 2)(done, brought[last])
            swapped[last] = swap_core(held)
        values = [(brought if own_core else swapped)[kind] for kind, own_core in items]
        staged = sum(value.shape[0] for value in values) // CHANNELS
        want_done = n == len(early) - 1
        *grads, done = (
            *call(
                functools.partial(final_kernel, items, blocks, want_done),
                (f32(TAPS, 128, 128), f32(TAPS, 128, 128)) + (token,) * want_done,
                [VMEM] * len(items) + [HBM] * len(grads),
                [pltpu.VMEM((staged, 128, 128), jnp.float32), pltpu.SemaphoreType.DMA((staged,))],
                50 * 10**9,
                (HBM, HBM) + (VMEM,) * want_done,
                {len(items): 0, len(items) + 1: 1} if grads else {},
            )(*values, *grads),
            *(() if want_done else (None,)),
        )
    grad_first, grad_second = grads
    return output[None, None], grad_features[None, None], grad_first, grad_second


def solution(mesh):
    placed = (
        P("drift", "wire", None, None),
        P(),
        P(),
        P("drift", "wire", None, None),
        P("drift", "wire"),
        P("drift", "wire", None, None),
        P("drift", "wire", None),
    )
    return jax.shard_map(
        on_device,
        mesh=mesh,
        in_specs=placed,
        out_specs=(P("drift", "wire", None, None), P("drift", "wire", None, None), P(), P()),
        check_vma=False,
    )
```
